32 devices in a mesh: clip: 4 (over y, x), fsdp: 8 (over z, core).
Axes of the slice: x: 2, y: 2, z: 4, core: 2. Of those that a mesh axis runs over, the one named last changes fastest.
Arguments:
- sample: bfloat16 [4096, 5120], P('clip', 'fsdp'), may hold values from -150 to 150
- noise: bfloat16 [4096, 5120], P('clip', 'fsdp'), may hold values from -6 to 6
- gen_branch: bfloat16 [4096, 5120], P('clip', 'fsdp'), may hold values from -6 to 6
- step: int32 [4], P('clip'), may hold values from 20 to 979
- teacher_mod: float32 [4, 2, 5120], P('clip'), may hold values from -3 to 3
- fake_mod: float32 [4, 2, 5120], P('clip'), may hold values from -3 to 3
- teacher_weight: bfloat16 [5120, 5120], P('clip', 'fsdp'), may hold values from -0.078125 to 0.078125
- fake_weight: bfloat16 [5120, 5120], P('clip', 'fsdp'), may hold values from -0.078125 to 0.078125
- gen_gate: float32 [4, 5120], P('clip', 'fsdp'), may hold values from -4 to 4
Outputs:
- branch_cot: bfloat16 [4096, 5120], P('clip', 'fsdp')
- gate_grad: float32 [4, 5120], P('clip', 'fsdp')
- fake_grad: float32 [5120, 5120], P('clip', 'fsdp')
The draws below stay inside these ranges and needn't reach their ends.
All inputs are finite; a program needn't handle non-finite values. Where the reference program divides by a largest or mean magnitude, that divisor is 1e-20 or more.
Results may differ from the reference program's by a relative error of at most 0.017.
Values may be sent and summed in bfloat16 or wider, within the bound.
No kernel may reach another device: no remote copies, remote signals or barrier semaphores. Data moves between devices by JAX's collectives and lax.ppermute only.
A program may use at most 128 MiB of HBM per device.

```python
import math
import jax
import jax.numpy as jnp
from jax import lax

D = 5120
CLIP_TOK = 1024
CLIPS = 4
TOKENS = 4096


def draw_sample(key, part):
    key = jax.random.fold_in(key, 11)
    first, second, third = jax.random.split(key, 3)
    row_scale = jnp.exp(jax.random.uniform(first, (TOKENS, 1), jnp.float32, math.log(0.5), math.log(5.0)))
    ramp = jnp.arange(D, dtype=jnp.float32) / D
    rough = jnp.exp(jax.random.uniform(second, (1, D), jnp.float32, -0.35, 0.35))
    col_scale = 0.5 * jnp.exp(math.log(10.0) * ramp)[None, :] * rough
    base = jnp.clip(jax.random.normal(third, (TOKENS, D), jnp.float32), -4.0, 4.0)
    values = base * row_scale * col_scale
    return values.astype(jnp.bfloat16)


def set_ends(entries, own_key, least, top_value):
    shape = entries.shape
    spot = [jax.random.randint(jax.random.fold_in(own_key, axis), (), 0, shape[axis]) for axis in range(len(shape))]
    entries = entries.at[tuple(spot)].set(least)
    longest = shape.index(max(shape))
    spot[longest] = (spot[longest] + 1) % shape[longest]
    return entries.at[tuple(spot)].set(top_value)


def block_levels(key, extent, pieces, low, largest):
    def one(dim, blocks):
        heights = jax.random.uniform(jax.random.fold_in(jax.random.fold_in(key, 6), dim), (blocks,), jnp.float32, low / len(pieces), largest / len(pieces))
        return jnp.repeat(jnp.exp(heights), extent[dim] // blocks).reshape((-1,) + (1,) * (len(extent) - dim - 1))

    level = one(*pieces[0])
    for cut in pieces[1:]:
        level = level * one(*cut)
    return level


def gaussian(key, extent, scale, most, cuts=(), kind=jnp.bfloat16):
    values = scale * jax.random.normal(key, extent, jnp.float32)
    if cuts:
        values = values * block_levels(key, extent, cuts, -0.22, 0.18)
    return jnp.clip(values, -most, most).astype(kind)


def setup_inputs(seed: int = 0) -> dict:
    streams_of = jax.random.split(jax.random.key(seed), 10)
    return {
        "sample": draw_sample(jax.random.fold_in(streams_of[9], 71), 0),
        "noise": gaussian(streams_of[1], (TOKENS, D), 1.0, 6.0, ((0, 4), (1, 8))),
        "gen_branch": gaussian(streams_of[2], (TOKENS, D), 1.0, 6.0, ((0, 4), (1, 8))),
        "step": set_ends(jax.random.randint(streams_of[3], (CLIPS,), 20, 980), jax.random.fold_in(streams_of[3], 1), 20, 979).astype(jnp.int32),
        "teacher_mod": gaussian(streams_of[4], (CLIPS, 2, D), 0.5, 3.0, ((0, 4),), jnp.float32),
        "fake_mod": gaussian(streams_of[5], (CLIPS, 2, D), 0.5, 3.0, ((0, 4),), jnp.float32),
        "teacher_weight": gaussian(streams_of[6], (D, D), D ** -0.5, 0.078125, ((0, 4), (1, 8))),
        "fake_weight": gaussian(streams_of[7], (D, D), D ** -0.5, 0.078125, ((0, 4), (1, 8))),
        "gen_gate": gaussian(streams_of[8], (CLIPS, D), 1.0, 4.0, ((0, 4), (1, 8)), jnp.float32),
    }


EPS = 1e-06

def reference(sample, noise, gen_branch, step, teacher_mod, fake_mod, teacher_weight, fake_weight, gen_gate):
    shaped = (CLIPS, CLIP_TOK, D)
    items = (sample.reshape(shaped), noise.reshape(shaped), gen_branch.reshape(shaped), step, teacher_mod, fake_mod, gen_gate)

    def one_clip(total, item):
        smp, nse, brn, stp, tmod, fmod, gate = item
        frac = stp.astype(jnp.float32) / 1000.0
        sigma = 5.0 * frac / (1.0 + 4.0 * frac)
        smp32 = smp.astype(jnp.float32)
        nse32 = nse.astype(jnp.float32)
        noised = ((1.0 - sigma) * smp32 + sigma * nse32).astype(jnp.bfloat16)
        noised32 = noised.astype(jnp.float32)
        center = lax.optimization_barrier(jnp.mean(noised32, axis=1, keepdims=True))
        spread = noised32 - center
        power = lax.optimization_barrier(jnp.mean(spread * spread, axis=1, keepdims=True))
        normed = (spread * lax.rsqrt(power + EPS)).astype(jnp.bfloat16)
        normed32 = normed.astype(jnp.float32)
        teacher_in = (normed32 * (1.0 + tmod[1]) + tmod[0]).astype(jnp.bfloat16)
        fake_in = (normed32 * (1.0 + fmod[1]) + fmod[0]).astype(jnp.bfloat16)
        teacher_velocity = jnp.dot(teacher_in, teacher_weight, preferred_element_type=jnp.float32)
        fake_velocity = jnp.dot(fake_in, fake_weight, preferred_element_type=jnp.float32)
        target = nse32 - smp32
        teacher_estimate = noised32 - sigma * teacher_velocity
        fake_estimate = noised32 - sigma * fake_velocity
        gap = jnp.mean(jnp.abs(smp32 - teacher_estimate))
        push = (fake_estimate - teacher_estimate) / (gap + EPS)
        branch_cot = (gate * push).astype(jnp.bfloat16)
        gate_grad = lax.optimization_barrier(jnp.sum(push * brn.astype(jnp.float32), axis=0)) / math.sqrt(CLIP_TOK)
        velocity_error = ((fake_velocity - target) / math.sqrt(TOKENS)).astype(jnp.bfloat16)
        term = jnp.dot(fake_in.T, velocity_error, preferred_element_type=jnp.float32)
        return (total + term, (branch_cot, gate_grad))
    fake_grad, outputs = lax.scan(one_clip, jnp.zeros((D, D), jnp.float32), items)
    branch_cot, gate_grad = outputs
    return (branch_cot.reshape(TOKENS, D), gate_grad, fake_grad)
```

```python
import math

import jax
import jax.numpy as jnp
from jax import lax
from jax.sharding import PartitionSpec as P

EPS = 1e-06
BF16 = jnp.bfloat16
F32 = jnp.float32


def swap_clip(value, bit, count):
    return lax.ppermute(value, "clip", [(i, i ^ bit) for i in range(count)])


def swap_core(value, count):
    return lax.ppermute(value, "fsdp", [(i, i ^ 1) for i in range(count)])


def ring_next(count):
    order = list(range(0, count, 2)) + list(range(count - 1, 0, -2))
    if count % 2:
        order = list(range(0, count, 2)) + list(range(count - 2, 0, -2))
    return {order[i]: order[(i + 1) % count] for i in range(count)}


def gather_halves(weight, count):
    bits = [1 << i for i in range(count.bit_length() - 1)]
    rows = weight.shape[0] // 2
    pieces = {}
    for half, order in ((0, bits), (1, bits[::-1])):
        held = {0: weight[half * rows : (half + 1) * rows]}
        for bit in order:
            held.update({mask ^ bit: swap_clip(block, bit, count) for mask, block in held.items()})
        for mask, block in held.items():
            pieces[mask, half] = block
    return pieces


def assemble(pieces, clip, rows):
    full = jnp.zeros((rows * len(pieces), next(iter(pieces.values())).shape[1]), BF16)
    for (mask, half), block in pieces.items():
        full = lax.dynamic_update_slice(full, block, (((clip ^ mask) * 2 + half) * rows, 0))
    return full


def per_device(
    sample, noise, gen_branch, step, teacher_mod, fake_mod, teacher_weight, fake_weight, gen_gate
):
    clips = lax.axis_size("clip")
    shards = lax.axis_size("fsdp")
    clip = lax.axis_index("clip")
    shard = lax.axis_index("fsdp")
    clip_rows, cols = sample.shape
    width = cols * shards
    total_tokens = clip_rows * clips
    half_rows = fake_weight.shape[0] // 2

    frac = step.astype(F32)[0] / 1000.0
    sigma = 5.0 * frac / (1.0 + 4.0 * frac)
    sample32 = sample.astype(F32)
    noise32 = noise.astype(F32)
    noised = ((1.0 - sigma) * sample32 + sigma * noise32).astype(BF16)
    noised32 = noised.astype(F32)

    fake_pieces = gather_halves(fake_weight, clips)
    teacher_pieces = gather_halves(teacher_weight, clips)

    after = ring_next(shards // 2)
    ring = [(2 * a + core, 2 * b + core) for a, b in after.items() for core in range(2)]
    before = jnp.array([a for a, _ in sorted(after.items(), key=lambda pair: pair[1])], jnp.int32)
    place = shard // 2
    parts = 2
    part_rows = clip_rows // parts
    blocks = []
    travel = [noised[i * part_rows : (i + 1) * part_rows] for i in range(parts)]
    for hop in range(shards // 2):
        if hop:
            travel = [lax.ppermute(piece, "fsdp", ring) for piece in travel]
            place = before[place]
        for i, piece in enumerate(travel):
            blocks.append((i, 2 * place + shard % 2, piece))
            blocks.append((i, 2 * place + 1 - shard % 2, swap_core(piece, shards)))

    partial = jnp.stack([jnp.sum(noised32, axis=1), jnp.sum(noised32 * noised32, axis=1)])
    row_sum, row_total = lax.psum(partial, "fsdp")
    center = row_sum / width
    variance = jnp.maximum(row_total / width - center * center, 0.0)
    row_factor = lax.rsqrt(variance + EPS)

    fake_in = jnp.zeros((clip_rows, width), BF16)
    teacher_in = jnp.zeros((clip_rows, width), BF16)
    for i, source, piece in blocks:
        part = slice(i * part_rows, (i + 1) * part_rows)
        spread = piece.astype(F32) - center[part, None]
        normed32 = (spread * row_factor[part, None]).astype(BF16).astype(F32)
        spot = (i * part_rows, source * cols)
        fake_cut = lax.dynamic_slice(fake_mod[0], (0, source * cols), (2, cols))
        teacher_cut = lax.dynamic_slice(teacher_mod[0], (0, source * cols), (2, cols))
        fake_in = lax.dynamic_update_slice(
            fake_in, (normed32 * (1.0 + fake_cut[1]) + fake_cut[0]).astype(BF16), spot
        )
        teacher_in = lax.dynamic_update_slice(
            teacher_in, (normed32 * (1.0 + teacher_cut[1]) + teacher_cut[0]).astype(BF16), spot
        )

    target = noise32 - sample32
    fake_velocity = jnp.dot(
        fake_in, assemble(fake_pieces, clip, half_rows), preferred_element_type=F32
    )
    velocity_error = ((fake_velocity - target) / math.sqrt(total_tokens)).astype(BF16)

    bits = [1 << i for i in range(clips.bit_length() - 1)]

    def term(mask, half):
        left = lax.dynamic_slice(
            fake_in, (0, ((clip ^ mask) * 2 + half) * half_rows), (clip_rows, half_rows)
        )
        return lax.dot_general(
            left, velocity_error, (((0,), (0,)), ((), ())), preferred_element_type=F32
        )

    sums = []
    for half, order in ((0, bits), (1, bits[::-1])):
        held = {mask: term(mask, half) for mask in range(clips)}
        for bit in order:
            sent = {mask: held.pop(mask) for mask in list(held) if mask & bit}
            for mask, block in sent.items():
                held[mask ^ bit] = held[mask ^ bit] + swap_clip(
                    block.astype(BF16), bit, clips
                ).astype(F32)
        sums.append(held[0])
    fake_grad = jnp.concatenate(sums, axis=0)

    teacher_velocity = jnp.dot(
        teacher_in, assemble(teacher_pieces, clip, half_rows), preferred_element_type=F32
    )
    teacher_estimate = noised32 - sigma * teacher_velocity
    fake_estimate = noised32 - sigma * fake_velocity
    local_gap = jnp.sum(jnp.abs(sample32 - teacher_estimate))
    gap_value = lax.psum(local_gap, "fsdp") / (clip_rows * width)
    push = (fake_estimate - teacher_estimate) / (gap_value + EPS)
    branch_cot = (gen_gate * push).astype(BF16)
    gate_grad = jnp.sum(push * gen_branch.astype(F32), axis=0, keepdims=True) / math.sqrt(clip_rows)
    return (branch_cot, gate_grad, fake_grad)


def solution(mesh):
    placed = (
        P("clip", "fsdp"),
        P("clip", "fsdp"),
        P("clip", "fsdp"),
        P("clip"),
        P("clip", None, None),
        P("clip", None, None),
        P("clip", "fsdp"),
        P("clip", "fsdp"),
        P("clip", "fsdp"),
    )
    return jax.shard_map(
        per_device,
        mesh=mesh,
        in_specs=placed,
        out_specs=(P("clip", "fsdp"), P("clip", "fsdp"), P("clip", "fsdp")),
        check_vma=False,
    )
```

```python
import functools
import math

import jax
import jax.numpy as jnp
from jax import lax
from jax.experimental import pallas as pl
from jax.experimental.pallas import tpu as pltpu
from jax.sharding import PartitionSpec as P

EPS = 1e-06
BF16 = jnp.bfloat16
F32 = jnp.float32
VMEM_BYTES = 48 * 1024 * 1024
CHUNKS = 2
TILE = 256
ANY = pl.BlockSpec(memory_space=pl.ANY)
SMEM = pl.BlockSpec(memory_space=pltpu.SMEM)


def after(value, *earlier):
    return lax.optimization_barrier((value, *earlier))[0]


def swap_clip(value, bit, count):
    return lax.ppermute(value, "clip", [(i, i ^ bit) for i in range(count)])


def clip_orders(count):
    bits = [1 << i for i in range(count.bit_length() - 1)]
    return ((0, bits), (1, bits[::-1]))


def gather_halves(weight, count, early=(), late=()):
    rows = weight.shape[0] // 2
    pieces = {}
    for half, order in clip_orders(count):
        own = weight[half * rows : (half + 1) * rows]
        held = {0: own}
        for bit in order:
            for mask in list(held):
                block = held[mask]
                if mask == 0:
                    block = after(own, *(early if bit == order[0] else late))
                held[mask ^ bit] = swap_clip(block, bit, count)
        for mask, block in held.items():
            pieces[mask, half] = block
    return pieces


def project_kernel(
    fake, start, masks, where, scalars, mod, sample, other, gathered, weight, *refs
):
    blocks, refs = refs[: (masks - 1) * 2], refs[(masks - 1) * 2 :]
    if fake:
        refs = refs[3 if start else 0 :]
        velocity, inputs, error = refs[:3]
        refs = refs[3:]
    else:
        refs = refs[1 if start else 0 :]
        velocity, gap = refs[:2]
        refs = refs[2:]
    held, full, total, wrong, sems, wsems, osems, *tiles = refs
    places, rows, depth = held.shape
    cols = total.shape[1]
    shards = gathered.shape[0]
    group = depth // cols
    count = len(tiles)
    tile = rows // count
    half_rows = weight.shape[0] // 2
    width = places * depth
    loads = []
    for mask in range(masks):
        for half in range(2):
            if mask:
                source = blocks[(mask - 1) * 2 + half]
            else:
                source = weight.at[pl.ds(half * half_rows, half_rows)]
            spot = pl.multiple_of((where[mask] * 2 + half) * half_rows, half_rows)
            target = full.at[pl.ds(spot, half_rows)]
            loads.append(pltpu.make_async_copy(source, target, wsems.at[mask * 2 + half]))
    arrivals = []
    for i in range(count):
        at = pl.ds(i * tile, tile)
        arrivals.append([
            pltpu.make_async_copy(
                gathered.at[f, at],
                held.at[f // group, at, pl.ds(f % group * cols, cols)],
                sems.at[i * shards + f],
            )
            for f in range(shards)
        ])
    for copy in arrivals[0] + loads:
        copy.start()
    for copies in arrivals[1:]:
        for copy in copies:
            copy.start()
    slab = tile // places

    def normalise(i, step):
        low = pl.multiple_of(step * slab, slab)
        at = pl.ds(i * tile + low, slab)
        sums = jnp.zeros((slab, 1), F32)
        for p in range(places):
            sums += jnp.sum(held[p, at, :].astype(F32), axis=1, keepdims=True)
        center = sums * (1.0 / width)
        power = jnp.zeros((slab, 1), F32)
        for p in range(places):
            spread = held[p, at, :].astype(F32) - center
            power += jnp.sum(spread * spread, axis=1, keepdims=True)
        factor = lax.rsqrt(power * (1.0 / width) + EPS)
        for p in range(places):
            spread = held[p, at, :].astype(F32) - center
            normed = (spread * factor).astype(BF16).astype(F32)
            put = (normed * (1.0 + mod[p, 1:2, :]) + mod[p, 0:1, :]).astype(BF16)
            tiles[i][p, pl.ds(low, slab), :] = put

    for copy in arrivals[0]:
        copy.wait()

    @pl.loop(0, places)
    def _(step):
        normalise(0, step)

    for copy in loads:
        copy.wait()
    drains = []

    def drain(source, target, index):
        drains.append(pltpu.make_async_copy(source, target, osems.at[index]))
        drains[-1].start()

    if not fake:
        gap[...] = jnp.zeros_like(gap)
    for i in range(count):
        at = pl.ds(i * tile, tile)
        out_at = pl.ds(start + i * tile, tile)
        if fake:
            drain(tiles[i], inputs.at[:, out_at, :], 3 * i)
        if i + 1 < count:
            for copy in arrivals[i + 1]:
                copy.wait()
        total[at, :] = jnp.zeros((tile, cols), F32)

        @pl.loop(0, places)
        def _(step):
            total[at, :] += jnp.dot(
                tiles[i][step],
                full[pl.ds(pl.multiple_of(step * depth, depth), depth), :],
                preferred_element_type=F32,
            )
            if i + 1 < count:
                normalise(i + 1, step)

        drain(total.at[at], velocity.at[out_at], 3 * i + 1)
        piece = 64

        @pl.loop(0, tile // piece)
        def _(step):
            low = pl.ds(pl.multiple_of(i * tile + step * piece, piece), piece)
            if fake:
                target = other[low, :].astype(F32) - sample[low, :].astype(F32)
                wrong[low, :] = ((total[low, :] - target) * scalars[1]).astype(BF16)
            else:
                estimate = other[low, :].astype(F32) - scalars[0] * total[low, :]
                away = jnp.abs(sample[low, :].astype(F32) - estimate)
                gap[...] += jnp.sum(away.reshape(piece // 8, 8, cols), axis=0)

        if fake:
            drain(wrong.at[at], error.at[out_at], 3 * i + 2)
    for copy in drains:
        copy.wait()


def project(fake, chunk, where, scalars, mod, sample, other, gathered, weight, blocks, earlier):
    clip_rows, cols = sample.shape
    shards, rows, _ = gathered.shape
    masks = len(blocks) // 2 + 1
    places, _, depth = mod.shape
    width = places * depth
    tile = min(TILE, rows)
    count = rows // tile
    window = pl.BlockSpec((rows, cols), lambda i: (chunk, 0))
    scratch = [
        pltpu.VMEM((places, rows, depth), BF16),
        pltpu.VMEM((width, cols), BF16),
        pltpu.VMEM((rows, cols), F32),
        pltpu.VMEM((rows, cols), BF16),
        pltpu.SemaphoreType.DMA((count * shards,)),
        pltpu.SemaphoreType.DMA((masks * 2,)),
        pltpu.SemaphoreType.DMA((3 * count,)),
    ] + [pltpu.VMEM((places, tile, depth), BF16)] * count
    out_shape = [jax.ShapeDtypeStruct((clip_rows, cols), F32)]
    out_specs = [ANY]
    if fake:
        out_shape.append(jax.ShapeDtypeStruct((places, clip_rows, depth), BF16))
        out_shape.append(jax.ShapeDtypeStruct((clip_rows, cols), BF16))
        out_specs += [ANY, ANY]
    else:
        out_shape.append(jax.ShapeDtypeStruct((8, cols), F32))
        out_specs.append(pl.BlockSpec((8, cols), lambda i: (0, 0)))
    first = 7 + len(blocks)
    return pl.pallas_call(
        functools.partial(project_kernel, fake, chunk * rows, masks),
        grid=(1,),
        out_shape=out_shape,
        in_specs=[SMEM, SMEM, pl.BlockSpec((places, 2, depth), lambda i: (0, 0, 0)), window, window]
        + [ANY] * (2 + len(blocks) + len(earlier)),
        out_specs=out_specs,
        scratch_shapes=scratch,
        input_output_aliases={first + i: i for i in range(len(earlier))},
        compiler_params=pltpu.CompilerParams(vmem_limit_bytes=VMEM_BYTES),
        cost_estimate=pl.CostEstimate(
            flops=2 * rows * width * cols,
            bytes_accessed=2 * (2 * rows * width + width * cols + 4 * rows * cols),
            transcendentals=0,
        ),
        name="project_fake" if fake else "project_teacher",
    )(where, scalars, mod, sample, other, gathered, weight, *blocks, *earlier)


def per_device(
    sample, noise, gen_branch, step, teacher_mod, fake_mod, teacher_weight, fake_weight, gen_gate
):
    clips = lax.axis_size("clip")
    shards = lax.axis_size("fsdp")
    clip = lax.axis_index("clip")
    clip_rows, cols = sample.shape
    width = cols * shards
    total_tokens = clip_rows * clips
    half_rows = fake_weight.shape[0] // 2
    group = 1 if cols % 128 else 2
    rows = clip_rows // CHUNKS

    frac = step.astype(F32)[0] / 1000.0
    sigma = 5.0 * frac / (1.0 + 4.0 * frac)
    noised = ((1.0 - sigma) * sample.astype(F32) + sigma * noise.astype(F32)).astype(BF16)
    gathered = [
        lax.all_gather(noised[i * rows : (i + 1) * rows], "fsdp") for i in range(CHUNKS)
    ]

    orders = clip_orders(clips)
    keys = [(mask, half) for mask in range(1, clips) for half in range(2)]
    fake_pieces = gather_halves(fake_weight, clips)
    crossed = [fake_pieces[order[-1], half] for half, order in orders]
    relayed = [fake_pieces[clips - 1, half] for half, order in orders]
    teacher_pieces = gather_halves(teacher_weight, clips, crossed, relayed)
    direct = [teacher_pieces[order[0], half] for half, order in orders]

    where = jnp.stack([clip ^ mask for mask in range(clips)]).astype(jnp.int32)
    scalars = jnp.stack([sigma, jnp.float32(1.0 / math.sqrt(total_tokens))])

    def by_place(mod):
        return jnp.swapaxes(mod[0].reshape(2, shards // group, group * cols), 0, 1)

    fake_by_place = by_place(fake_mod)
    teacher_by_place = by_place(teacher_mod)
    done = ()
    for i in range(CHUNKS):
        tokens = after(gathered[i], *direct) if i == 0 else gathered[i]
        done = project(
            True, i, where, scalars, fake_by_place, sample, noise, tokens,
            fake_weight, [fake_pieces[key] for key in keys], done,
        )
    fake_velocity, fake_in, error = done

    def term(mask, half):
        place = clip ^ mask
        if group == 2:
            left = lax.dynamic_slice(
                fake_in, (place, 0, half * cols), (1, clip_rows, cols)
            )[0]
        else:
            left = lax.dynamic_index_in_dim(fake_in, place * 2 + half, 0, keepdims=False)
        return lax.dot_general(left, error, (((0,), (0,)), ((), ())), preferred_element_type=F32)

    sent = {}
    for mask in range(clips - 1, 0, -1):
        for half, order in orders:
            if mask & order[0]:
                sent[half, mask] = term(mask, half).astype(BF16)
    ready = list(sent.values())
    sums = []
    for half, order in orders:
        mine = {mask: term(mask, half) for mask in range(clips) if not mask & order[0]}
        for bit in order:
            if bit == order[0]:
                going = {mask: block for (h, mask), block in sent.items() if h == half}
            else:
                going = {mask: mine.pop(mask).astype(BF16) for mask in list(mine) if mask & bit}
            for mask, block in going.items():
                mine[mask ^ bit] = mine[mask ^ bit] + swap_clip(block, bit, clips).astype(F32)
        sums.append(mine[0])
    fake_grad = jnp.concatenate(sums, axis=0)

    done = ()
    away = 0.0
    for i in range(CHUNKS):
        tokens = after(gathered[i], *ready) if i == 0 else gathered[i]
        velocity, gap = project(
            False, i, where, scalars, teacher_by_place, sample, noised, tokens,
            teacher_weight, [teacher_pieces[key] for key in keys], done,
        )
        done = (velocity,)
        away = away + gap
    gap_value = lax.psum(jnp.sum(away), "fsdp") / (clip_rows * width)
    push = sigma * (velocity - fake_velocity) / (gap_value + EPS)
    branch_cot = (gen_gate * push).astype(BF16)
    gate_grad = jnp.sum(push * gen_branch.astype(F32), axis=0, keepdims=True) / math.sqrt(clip_rows)
    return (branch_cot, gate_grad, fake_grad)


def solution(mesh):
    placed = (
        P("clip", "fsdp"),
        P("clip", "fsdp"),
        P("clip", "fsdp"),
        P("clip"),
        P("clip", None, None),
        P("clip", None, None),
        P("clip", "fsdp"),
        P("clip", "fsdp"),
        P("clip", "fsdp"),
    )
    return jax.shard_map(
        per_device,
        mesh=mesh,
        in_specs=placed,
        out_specs=(P("clip", "fsdp"), P("clip", "fsdp"), P("clip", "fsdp")),
        check_vma=False,
    )
```

```python
import functools
import math

import jax
import jax.numpy as jnp
from jax import lax
from jax.experimental import pallas as pl
from jax.experimental.pallas import tpu as pltpu
from jax.sharding import PartitionSpec as P

EPS = 1e-06
BF16 = jnp.bfloat16
F32 = jnp.float32
VMEM_BYTES = 48 * 1024 * 1024
CHUNKS = 2
GATES = {'relay': ('cA1', 'own', 'B1'), 'teacher': ('parts', 'parts1'), 'B2': ('A2',), 'A3': ('far0', 'far1'), 'B3': ('A3', 't00', 't01', 'sums'), 'cB1': ('far0', 'far1'), 'cA2': ('far0', 'far1'), 'cB2': ('far0', 'far1'), 'cA3': ('early',), 'cB3': ('early',), 'teacher relay': ('early',)}
ANY = pl.BlockSpec(memory_space=pl.ANY)
SMEM = pl.BlockSpec(memory_space=pltpu.SMEM)
VMEM = pl.BlockSpec(memory_space=pltpu.VMEM)


def after(value, *earlier):
    return lax.optimization_barrier((value, *earlier))[0]


def swap_clip(value, bit, count):
    return lax.ppermute(value, "clip", [(i, i ^ bit) for i in range(count)])


def clip_orders(count):
    bits = [1 << i for i in range(count.bit_length() - 1)]
    return ((0, bits), (1, bits[::-1]))


def neighbour_blocks(weight, count):
    return {bit: swap_clip(weight, bit, count) for bit in clip_orders(count)[0][1]}


def relay_parts(direct, rows):
    parts = {}
    for half in range(2):
        for bit, block in direct.items():
            parts[bit, half] = block[half * rows : (half + 1) * rows]
    return parts


def relay_blocks(parts, count):
    pieces = {}
    for half, order in clip_orders(count):
        held = {}
        for bit in order:
            for mask in list(held):
                held[mask ^ bit] = swap_clip(held[mask], bit, count)
            held[bit] = parts[bit, half]
        for mask, block in held.items():
            pieces[mask, half] = block
    return pieces


def scale_kernel(keys, where, mod, weight, *refs):
    blocks, refs = refs[: len(keys)], refs[len(keys) :]
    out, sums, full, sems, osems = refs
    half_rows = weight.shape[0] // 2
    cols = weight.shape[1]
    loads, drains = [], []
    for index, (mask, half) in enumerate([(0, 0), (0, 1)] + keys):
        ref = weight if mask == 0 else blocks[index - 2]
        source = ref.at[pl.ds(half * half_rows, half_rows)] if ref.shape[0] > half_rows else ref
        spot = pl.multiple_of((where[mask] * 2 + half) * half_rows, half_rows)
        at = pl.ds(spot, half_rows)
        loads.append((pltpu.make_async_copy(source, full.at[at], sems.at[index]), spot))
        drains.append(pltpu.make_async_copy(full.at[at], out.at[at], osems.at[index]))
        loads[-1][0].start()
    tile = 160
    sums[...] = jnp.zeros_like(sums)
    for (load, spot), drain in zip(loads, drains):
        load.wait()

        @pl.loop(0, half_rows // tile)
        def _(step):
            at = pl.ds(pl.multiple_of(spot + step * tile, tile), tile)
            value = full[at, :].astype(F32)
            shifted = value * mod[at, 0:1]
            scaled = (value * (1.0 + mod[at, 1:2])).astype(BF16)
            full[at, :] = scaled
            sums[0] += jnp.sum(scaled.astype(F32).reshape(tile // 8, 8, cols), axis=0)
            sums[1] += jnp.sum(shifted.reshape(tile // 8, 8, cols), axis=0)

        drain.start()
    for i in range(2):
        sums[i] = jnp.broadcast_to(jnp.sum(sums[i], axis=0, keepdims=True), (8, cols))
    for drain in drains:
        drain.wait()


def scale(where, mod, weight, blocks):
    cols = weight.shape[1]
    half_rows = weight.shape[0] // 2
    count = len(blocks) + 2
    width = half_rows * count
    return pl.pallas_call(
        functools.partial(scale_kernel, list(blocks)),
        out_shape=(
            jax.ShapeDtypeStruct((width, cols), BF16),
            jax.ShapeDtypeStruct((2, 8, cols), F32),
        ),
        in_specs=[SMEM, VMEM] + [ANY] * (1 + len(blocks)),
        out_specs=(ANY, VMEM),
        scratch_shapes=[
            pltpu.VMEM((width, cols), BF16),
            pltpu.SemaphoreType.DMA((count,)),
            pltpu.SemaphoreType.DMA((count,)),
        ],
        compiler_params=pltpu.CompilerParams(vmem_limit_bytes=VMEM_BYTES),
        cost_estimate=pl.CostEstimate(
            flops=1, bytes_accessed=1, transcendentals=0
        ),
        name="scale",
    )(where, mod, weight, *blocks.values())


def project_kernel(
    first, last, hops, core_at, where, scalars, sums, sample, other, scaled, *refs
):
    count = len(hops)
    pieces, refs = refs[: sum(len(hop) for hop in hops)], refs[sum(len(hop) for hop in hops) :]
    if not first:
        carry, means, powers, _, *refs = refs
    if last:
        velocity, inputs, flipped, centers, factors, edge, *refs = refs
    else:
        velocity, inputs, centers, factors, *refs = refs
    held, full, tail, sems, wsems, osems = refs
    rows, depth = held.shape[1:]
    cols = velocity.shape[1]
    group = depth // cols
    core = where[core_at]
    loads, arrivals, drains = [], [], []
    index = 0
    for n, hop in enumerate(hops):
        copies = []
        for low, side, place in hop:
            owner = core if side == 0 else 1 - core
            ref = pieces[index]
            at = pl.ds(low, ref.shape[0])
            if group == 2:
                lanes = pl.ds(pl.multiple_of(owner * cols, cols), cols)
                spot = held.at[n, at, lanes]
            else:
                spot = held.at[2 * n + owner, at]
            copies.append(pltpu.make_async_copy(ref, spot, sems.at[index]))
            index += 1
        arrivals.append(copies)
        place = where[hop[0][2]]
        span = 2 * cols
        loads.append(
            pltpu.make_async_copy(
                scaled.at[pl.ds(pl.multiple_of(place * span, span), span)], full.at[n], wsems.at[n]
            )
        )
        parts = 2 // group
        drains.append(
            pltpu.make_async_copy(
                held.at[pl.ds(n * parts, parts)],
                inputs.at[pl.ds(place * parts, parts)],
                osems.at[n],
            )
        )
    for copies, load in zip(arrivals, loads):
        for copy in copies:
            copy.start()
        load.start()
    slots = held.shape[0]
    for n in range(count):
        for copy in arrivals[n]:
            copy.wait()
        loads[n].wait()
        drains[n].start()
        for part in range(2 // group):
            slot = n * (2 // group) + part
            term = jnp.dot(
                held[slot], full[n, pl.ds(part * depth, depth), :], preferred_element_type=F32
            )
            if n or part:
                velocity[...] += term
            elif first:
                velocity[...] = term
            else:
                velocity[...] = carry[...] + term
    piece = 128
    many = slots * depth
    total = many if first else many * (scaled.shape[0] // many)
    if last:
        tail[...] = jnp.zeros_like(tail)

    @pl.loop(0, rows // piece)
    def _(step):
        low = pl.multiple_of(step * piece, piece)
        at = pl.ds(low, piece)
        sum_ = jnp.zeros((piece, 1), F32)
        for slot in range(slots):
            sum_ += jnp.sum(held[slot, at, :].astype(F32), axis=1, keepdims=True)
        mean = sum_ * (1.0 / many)
        power = jnp.zeros((piece, 1), F32)
        for slot in range(slots):
            spread = held[slot, at, :].astype(F32) - mean
            power += jnp.sum(spread * spread, axis=1, keepdims=True)
        if not first:
            others = scaled.shape[0] - many
            apart = means[at, 0:1] - mean
            power += powers[at, 0:1] + apart * apart * (many * others / scaled.shape[0])
            mean += apart * (others / scaled.shape[0])
        if last:
            by = lax.rsqrt(power * (1.0 / scaled.shape[0]) + EPS)
            power = by
            value = by * (velocity[at, :] - mean * sums[0, 0:1, :]) + sums[1, 0:1, :]
            velocity[at, :] = value
            target = other[at, :].astype(F32) - sample[at, :].astype(F32)
            wrong = (value - target) * scalars[1]
            sent = (by * wrong).astype(BF16).astype(F32)
            flipped[:, at] = jnp.transpose(sent).astype(BF16)
            tail[0] += jnp.sum((mean * sent).reshape(piece // 8, 8, cols), axis=0)
            tail[1] += jnp.sum(wrong.reshape(piece // 8, 8, cols), axis=0)
        centers[at, :] = jnp.broadcast_to(mean, (piece, 128))
        factors[at, :] = jnp.broadcast_to(power, (piece, 128))

    if last:
        ends = [jnp.sum(jnp.transpose(tail[i]), axis=1, keepdims=True) for i in range(2)]
        edge[...] = jnp.concatenate(ends, axis=1)
    for copy in drains:
        copy.wait()


def project(where, scalars, sums, sample, other, scaled, hops, earlier, last):
    clip_rows, cols = sample.shape
    width = scaled.shape[0]
    group = 1 if cols % 128 else 2
    depth = group * cols
    places = width // depth
    slots = len(hops) * 2 // group
    first = not earlier
    pieces = [piece for hop, _ in hops for piece, _, _ in hop]
    plan = [[(low, side, place) for _, low, side in hop] for hop, place in hops]
    wide = jax.ShapeDtypeStruct((clip_rows, 128), F32)
    out_shape = [
        jax.ShapeDtypeStruct((clip_rows, cols), F32),
        jax.ShapeDtypeStruct((places, clip_rows, depth), BF16),
    ]
    if last:
        out_shape.append(jax.ShapeDtypeStruct((cols, clip_rows), BF16))
    out_shape += [wide, wide]
    if last:
        out_shape.append(jax.ShapeDtypeStruct((cols, 2), F32))
    if not first:
        velocity, inputs, means, powers = earlier
        earlier = [velocity, means, powers, inputs]
    return pl.pallas_call(
        functools.partial(project_kernel, first, last, plan, where.shape[0] - 1),
        out_shape=out_shape,
        in_specs=[SMEM, SMEM] + [VMEM] * 3 + [ANY] * (1 + len(pieces)) + ([] if first else [VMEM] * 3 + [ANY]),
        out_specs=[VMEM, ANY] + [VMEM] * (len(out_shape) - 2),
        scratch_shapes=[
            pltpu.VMEM((slots, clip_rows, depth), BF16),
            pltpu.VMEM((len(hops), 2 * cols, cols), BF16),
            pltpu.VMEM((2, 8, cols), F32),
            pltpu.SemaphoreType.DMA((len(pieces),)),
            pltpu.SemaphoreType.DMA((len(hops),)),
            pltpu.SemaphoreType.DMA((len(hops),)),
        ],
        input_output_aliases={} if first else {6 + len(pieces) + 3: 1},
        compiler_params=pltpu.CompilerParams(vmem_limit_bytes=VMEM_BYTES),
        cost_estimate=pl.CostEstimate(
            flops=1, bytes_accessed=1,
            transcendentals=0,
        ),
        name="project",
    )(where, scalars, sums, sample, other, scaled, *pieces, *earlier)


def outer_kernel(picks, mod, edge, flipped, inputs, *outs):
    del picks
    term = jnp.dot(flipped[...], inputs[0], preferred_element_type=F32)
    term = (term - edge[:, 0:1]) * (1.0 + mod[0, 1:2, :]) + edge[:, 1:2] * mod[0, 0:1, :]
    for i, out in enumerate(outs):

        @pl.when(pl.program_id(0) == i)
        def _():
            out[...] = term.astype(out.dtype)


def outer(picks, mod, edge, flipped, inputs, dtype):
    cols, rows = flipped.shape
    count = len(picks)
    group = inputs.shape[2] // cols

    def spot(i, picks):
        return (picks[i] // group, 0, lax.rem(picks[i], group))

    return pl.pallas_call(
        outer_kernel,
        out_shape=[jax.ShapeDtypeStruct((cols, cols), dtype)] * count,
        grid_spec=pltpu.PrefetchScalarGridSpec(
            num_scalar_prefetch=1,
            grid=(count,),
            in_specs=[
                pl.BlockSpec((1, 2, cols), spot),
                pl.BlockSpec((cols, 2), lambda i, picks: (0, 0)),
                pl.BlockSpec((cols, rows), lambda i, picks: (0, 0)),
                pl.BlockSpec((1, rows, cols), spot),
            ],
            out_specs=[pl.BlockSpec((cols, cols), lambda i, picks: (0, 0))] * count,
        ),
        compiler_params=pltpu.CompilerParams(vmem_limit_bytes=VMEM_BYTES),
        cost_estimate=pl.CostEstimate(
            flops=1, bytes_accessed=1,
            transcendentals=0,
        ),
        name="outer",
    )(jnp.stack(picks).astype(jnp.int32), mod, edge, flipped, inputs)


def finish_kernel(terms, *refs):
    *parts, out = refs
    for half in range(2):
        total = parts[half * terms][...]
        for ref in parts[half * terms + 1 : (half + 1) * terms]:
            total += ref[...].astype(F32)
        out[half] = jnp.transpose(total)


def finish(halves):
    cols = halves[0][0].shape[0]
    lanes = 128 if cols % 128 == 0 else cols
    parts = [part for half in halves for part in half]
    return pl.pallas_call(
        functools.partial(finish_kernel, len(halves[0])),
        grid=(cols // lanes,),
        out_shape=jax.ShapeDtypeStruct((2, cols, cols), F32),
        in_specs=[pl.BlockSpec((cols, lanes), lambda i: (0, i))] * len(parts),
        out_specs=pl.BlockSpec((2, lanes, cols), lambda i: (0, i, 0)),
        compiler_params=pltpu.CompilerParams(vmem_limit_bytes=VMEM_BYTES),
        name="finish",
    )(*parts).reshape(2 * cols, cols)


def per_device(
    sample, noise, gen_branch, step, teacher_mod, fake_mod, teacher_weight, fake_weight, gen_gate
):
    clips = lax.axis_size("clip")
    shards = lax.axis_size("fsdp")
    clip = lax.axis_index("clip")
    shard = lax.axis_index("fsdp")
    clip_rows, cols = sample.shape
    width = cols * shards
    total_tokens = clip_rows * clips
    hops = shards // 2
    group = 1 if cols % 128 else 2
    rows = clip_rows // CHUNKS
    orders = clip_orders(clips)

    frac = step.astype(F32)[0] / 1000.0
    sigma = 5.0 * frac / (1.0 + 4.0 * frac)
    noised = ((1.0 - sigma) * sample.astype(F32) + sigma * noise.astype(F32)).astype(BF16)

    order = list(range(0, hops, 2)) + list(range(hops - 1 - hops % 2, 0, -2))
    ring = [
        (2 * order[i] + core, 2 * order[(i + 1) % hops] + core)
        for i in range(hops)
        for core in range(2)
    ]
    line = shard // 2
    rank = jnp.where(line % 2 == 0, line // 2, hops - 1 - line // 2)
    places = []
    for hop in range(hops):
        at = (rank + hops - hop) % hops
        places.append(jnp.where(2 * at < hops, 2 * at, 2 * (hops - 1 - at) + 1))
    swap = [(i, i ^ 1) for i in range(shards)]
    half_rows = fake_weight.shape[0] // 2
    far = [key for key in ((m, h) for m in range(clips) for h in range(2)) if key[0] & (key[0] - 1)]
    seen = {}

    def gated(name, value):
        names = [other for other in GATES.get(name, ()) if other in seen]
        return after(value, *(seen[other] for other in names))

    def hop_to(hop, i):
        name = "AB"[i] + str(hop)
        source = seen["AB"[i] + str(hop - 1)] if hop > 1 else noised[i * rows : (i + 1) * rows]
        seen[name] = lax.ppermute(gated(name, source), "fsdp", ring)

    def cross(hop, i):
        name = "AB"[i] + str(hop)
        seen["c" + name] = lax.ppermute(gated("c" + name, seen[name]), "fsdp", swap)

    fake_direct = neighbour_blocks(fake_weight, clips)
    for i, block in enumerate(fake_direct.values()):
        seen["f" + str(i)] = block
    for i in range(CHUNKS):
        hop_to(1, i)
    seen["own"] = lax.ppermute(noised, "fsdp", swap)
    for i in range(CHUNKS):
        cross(1, i)
    for i in range(CHUNKS):
        hop_to(2, i)
    parts = relay_parts({bit: gated("relay", block) for bit, block in fake_direct.items()}, half_rows)
    seen["parts"] = list(parts.values())[0]
    seen["parts1"] = list(parts.values())[-1]
    fake_blocks = relay_blocks(parts, clips)
    for mask, block in fake_direct.items():
        fake_blocks[mask, 0] = fake_blocks[mask, 1] = block
    seen["far0"], seen["far1"] = fake_blocks[far[0]], fake_blocks[far[1]]
    scalars = jnp.stack([sigma, jnp.float32(1.0 / math.sqrt(total_tokens))])
    owners = jnp.stack([clip ^ mask for mask in range(clips)]).astype(jnp.int32)
    where = jnp.stack(places + [shard % 2]).astype(jnp.int32)
    scaled, sums = scale(owners, jnp.transpose(fake_mod[0]), fake_weight, fake_blocks)
    seen["sums"] = sums
    teacher_parts = {}
    own = gated("teacher", teacher_weight)
    own = [own[:half_rows], own[half_rows:]]
    for phase in range(len(orders[0][1])):
        for half, order in orders:
            block = swap_clip(gated("teacher" + str(min(phase, 1)), own[half]), order[phase], clips)
            teacher_parts[order[phase], half] = block
            seen["t" + str(phase) + str(half)] = block
    tokens = [([(noised, 0, 0), (seen["own"], 0, 1)], 0)]

    def add_hop(hop):
        pieces = []
        for i in range(CHUNKS):
            name = "AB"[i] + str(hop)
            pieces += [(seen[name], i * rows, 0), (seen["c" + name], i * rows, 1)]
        tokens.append((pieces, hop))

    add_hop(1)
    for hop in range(2, hops):
        for i in range(CHUNKS):
            if hop > 2:
                hop_to(hop, i)
            if hop < hops - 1:
                cross(hop, i)
        if hop < hops - 1:
            add_hop(hop)
    done = project(where, scalars, sums, sample, noise, scaled, tokens, (), False)
    seen["early"] = done[2]
    for key, block in teacher_parts.items():
        teacher_parts[key] = gated("teacher relay", block)
    teacher_blocks = relay_blocks(teacher_parts, clips)
    for i in range(CHUNKS):
        cross(hops - 1, i)
    add_hop(hops - 1)
    fake_velocity, inputs, flipped, centers, factors, edge = project(
        where, scalars, sums, sample, noise, scaled, tokens[-1:], done, True
    )
    by_place = jnp.swapaxes(fake_mod[0].reshape(2, shards // group, group * cols), 0, 1)
    flipped = after(flipped, *(teacher_blocks[key] for key in far))

    def terms(keys, left, dtype):
        picks = [(clip ^ mask) * 2 + half for mask, half in keys]
        return dict(zip(keys, outer(picks, by_place, edge, left, inputs, dtype)))

    held = {}
    going = [(mask, half) for half, order in orders for mask in range(clips) if mask & order[0]]
    held.update(terms([key for key in going if key[0] & (key[0] - 1)], flipped, BF16))
    held.update(terms([key for key in going if key not in held], flipped, BF16))
    ready = list(held.values())
    keys = [key for m in range(clips) for key in [(m, 0), (m, 1)] if key not in held]
    held.update(terms(keys, after(flipped, *ready), F32))
    halves = []
    firsts, seconds = [], []
    for half, order in orders:
        mine = {mask: [block] for (mask, h), block in held.items() if h == half}
        for bit in order:
            for mask in [mask for mask in mine if mask & bit]:
                block = sum(part.astype(F32) for part in mine.pop(mask)).astype(BF16)
                got = swap_clip(block, bit, clips)
                if bit == order[0]:
                    (firsts if mask & (mask - 1) else seconds).append(got)
                mine[mask ^ bit].append(got)
        halves.append(mine[0])
    fake_grad = finish(halves)

    scaled, sums = scale(
        owners, jnp.transpose(teacher_mod[0]), after(teacher_weight, *ready), teacher_blocks
    )
    depth = group * cols
    velocity = 0.0
    for p in range(width // depth):
        left = inputs[p]
        if p == width // depth // 2:
            left = after(left, *firsts)
        right = scaled[p * depth : (p + 1) * depth]
        velocity = velocity + jnp.dot(left, right, preferred_element_type=F32)
    velocity = factors[:, :1] * (velocity - centers[:, :1] * sums[0, :1]) + sums[1, :1]
    away = sample.astype(F32) - (noised.astype(F32) - sigma * velocity)
    away = after(jnp.sum(jnp.abs(away)).reshape(1, 1), *seconds)
    bit = 1
    while bit < shards:
        away = away + lax.ppermute(away, "fsdp", [(i, i ^ bit) for i in range(shards)])
        bit *= 2
    gap_value = away / (clip_rows * width)
    push = sigma * (velocity - fake_velocity) / (gap_value + EPS)
    branch_cot = (gen_gate * push).astype(BF16)
    gate_grad = jnp.sum(push * gen_branch.astype(F32), axis=0, keepdims=True) / math.sqrt(clip_rows)
    return (branch_cot, gate_grad, fake_grad)


def solution(mesh):
    placed = (
        P("clip", "fsdp"),
        P("clip", "fsdp"),
        P("clip", "fsdp"),
        P("clip"),
        P("clip", None, None),
        P("clip", None, None),
        P("clip", "fsdp"),
        P("clip", "fsdp"),
        P("clip", "fsdp"),
    )
    return jax.shard_map(
        per_device,
        mesh=mesh,
        in_specs=placed,
        out_specs=(P("clip", "fsdp"), P("clip", "fsdp"), P("clip", "fsdp")),
        check_vma=False,
    )
```

```python
import functools
import math

import jax
import jax.numpy as jnp
from jax import lax
from jax.experimental import pallas as pl
from jax.experimental.pallas import tpu as pltpu
from jax.sharding import PartitionSpec as P

EPS = 1e-06
BF16 = jnp.bfloat16
F32 = jnp.float32
MIB = 1024 * 1024
CHUNKS = 2
GATES = {'relay': ('cA1',), 'teacher': ('parts', 'parts1'), 'teacher1': ('far0', 'far1'), 'A2': ('B1',), 'B2': ('A2',), 'A3': ('far0', 'far1'), 'B3': ('A3', 'sums'), 'cB1': ('f0', 'f1'), 'cA2': ('soon',), 'cB2': ('sums',), 'cB3': ('early',), 'teacher relay': ('sums',)}
ANY = pl.BlockSpec(memory_space=pl.ANY)
SMEM = pl.BlockSpec(memory_space=pltpu.SMEM)
VMEM = pl.BlockSpec(memory_space=pltpu.VMEM)


def after(value, *earlier):
    return lax.optimization_barrier((value, *earlier))[0]


def swap_clip(value, bit, count):
    return lax.ppermute(value, "clip", [(i, i ^ bit) for i in range(count)])


def clip_orders(count):
    bits = [1 << i for i in range(count.bit_length() - 1)]
    return ((0, bits), (1, bits[::-1]))


def neighbour_blocks(weight, count):
    return {bit: swap_clip(weight, bit, count) for bit in clip_orders(count)[0][1]}


def relay_parts(direct, rows):
    parts = {}
    for half in range(2):
        for bit, block in direct.items():
            parts[bit, half] = block[half * rows : (half + 1) * rows]
    return parts


def relay_blocks(parts, count):
    pieces = {}
    for half, order in clip_orders(count):
        held = {}
        for bit in order:
            for mask in list(held):
                held[mask ^ bit] = swap_clip(held[mask], bit, count)
            held[bit] = parts[bit, half]
        for mask, block in held.items():
            pieces[mask, half] = block
    return pieces


def scale_kernel(keys, where, mod, weight, *refs):
    blocks, refs = refs[: len(keys)], refs[len(keys) :]
    out, sums, full, sems, osems = refs
    half_rows = weight.shape[0] // 2
    cols = weight.shape[1]
    loads, drains = [], []
    for index, (mask, half) in enumerate([(0, 0), (0, 1)] + keys):
        ref = weight if mask == 0 else blocks[index - 2]
        source = ref.at[pl.ds(half * half_rows, half_rows)] if ref.shape[0] > half_rows else ref
        spot = pl.multiple_of((where[mask] * 2 + half) * half_rows, half_rows)
        at = pl.ds(spot, half_rows)
        loads.append((pltpu.make_async_copy(source, full.at[at], sems.at[index]), spot))
        drains.append(pltpu.make_async_copy(full.at[at], out.at[at], osems.at[index]))
        loads[-1][0].start()
    tile = 160
    sums[...] = jnp.zeros_like(sums)
    for (load, spot), drain in zip(loads, drains):
        load.wait()

        @pl.loop(0, half_rows // tile)
        def _(step):
            at = pl.ds(pl.multiple_of(spot + step * tile, tile), tile)
            value = full[at, :].astype(F32)
            shifted = value * mod[at, 0:1]
            scaled = (value * (1.0 + mod[at, 1:2])).astype(BF16)
            full[at, :] = scaled
            sums[0] += jnp.sum(scaled.astype(F32).reshape(tile // 8, 8, cols), axis=0)
            sums[1] += jnp.sum(shifted.reshape(tile // 8, 8, cols), axis=0)

        drain.start()
    for i in range(2):
        sums[i] = jnp.broadcast_to(jnp.sum(sums[i], axis=0, keepdims=True), (8, cols))
    for drain in drains:
        drain.wait()


def scale(where, mod, weight, blocks):
    cols = weight.shape[1]
    half_rows = weight.shape[0] // 2
    count = len(blocks) + 2
    width = half_rows * count
    return pl.pallas_call(
        functools.partial(scale_kernel, list(blocks)),
        out_shape=(
            jax.ShapeDtypeStruct((width, cols), BF16),
            jax.ShapeDtypeStruct((2, 8, cols), F32),
        ),
        in_specs=[SMEM, VMEM] + [ANY] * (1 + len(blocks)),
        out_specs=(ANY, VMEM),
        scratch_shapes=[
            pltpu.VMEM((width, cols), BF16),
            pltpu.SemaphoreType.DMA((count,)),
            pltpu.SemaphoreType.DMA((count,)),
        ],
        compiler_params=pltpu.CompilerParams(
            vmem_limit_bytes=2 * width * (cols + 256) + 8 * MIB
        ),
        cost_estimate=pl.CostEstimate(
            flops=1, bytes_accessed=1, transcendentals=0
        ),
        name="scale",
    )(where, mod, weight, *blocks.values())


def project_kernel(
    prior, last, hops, where, scalars, sums, sample, other, scaled, *refs
):
    count = sum(len(hop) for hop in hops)
    pieces, refs = refs[:count], refs[count:]
    if prior:
        carry, carried, _, *refs = refs
    if last:
        velocity, inputs, stats, flipped, edge, *refs = refs
    else:
        velocity, inputs, stats, *refs = refs
    held, full, moments, tail, sems, wsems, osems = refs
    slots, rows, depth = held.shape
    cols = velocity.shape[1]
    width = scaled.shape[0]
    parts = 2 * cols // depth
    core = where[where.shape[0] - 1]
    loads, arrivals, drains = [], [], []
    index = 0
    for n, hop in enumerate(hops):
        copies = []
        for low, side, place in hop:
            owner = core if side == 0 else 1 - core
            ref = pieces[index]
            at = pl.ds(low, ref.shape[0])
            if parts == 1:
                lanes = pl.ds(pl.multiple_of(owner * cols, cols), cols)
                spot = held.at[n, at, lanes]
            else:
                spot = held.at[2 * n + owner, at]
            copies.append(pltpu.make_async_copy(ref, spot, sems.at[index]))
            index += 1
        arrivals.append(copies)
        place = where[hop[0][2]]
        span = 2 * cols
        loads.append(
            pltpu.make_async_copy(
                scaled.at[pl.ds(pl.multiple_of(place * span, span), span)], full.at[n], wsems.at[n]
            )
        )
        drains.append(
            pltpu.make_async_copy(
                held.at[pl.ds(n * parts, parts)],
                inputs.at[pl.ds(place * parts, parts)],
                osems.at[n],
            )
        )
    for copies, load in zip(arrivals, loads):
        for copy in copies:
            copy.start()
        load.start()
    piece = 256
    lane = lax.broadcasted_iota(jnp.int32, (piece, 128), 1)
    for n in range(len(hops)):
        for copy in arrivals[n]:
            copy.wait()
        loads[n].wait()
        drains[n].start()
        for part in range(parts):
            slot = n * parts + part
            term = jnp.dot(
                held[slot], full[n, pl.ds(part * depth, depth), :], preferred_element_type=F32
            )
            if slot:
                velocity[...] += term
            elif prior:
                velocity[...] = carry[...] + term
            else:
                velocity[...] = term
            for low in range(0, rows, piece):
                at = pl.ds(low, piece)
                if slot == 0 and prior:
                    moments[at, :] = carried[at, :]
                elif slot == 0:
                    near = held[0, at, :128].astype(F32)
                    near = jnp.sum(near, axis=1, keepdims=True) * (1.0 / 128)
                    moments[at, :] = jnp.where(lane == 0, near, 0.0)
                spread = held[slot, at, :].astype(F32) - moments[at, 0:1]
                sum_ = jnp.sum(spread, axis=1, keepdims=True)
                power = jnp.sum(spread * spread, axis=1, keepdims=True)
                more = jnp.where(lane == 1, sum_, jnp.where(lane == 2, power, 0.0))
                moments[at, :] += more
    if not last:
        stats[...] = moments[...]
    else:
        tail[...] = jnp.zeros_like(tail)

        @pl.loop(0, rows // piece)
        def _(step):
            low = pl.multiple_of(step * piece, piece)
            at = pl.ds(low, piece)
            away = moments[at, 1:2] * (1.0 / width)
            power = jnp.maximum(moments[at, 2:3] * (1.0 / width) - away * away, 0.0)
            mean = moments[at, 0:1] + away
            by = lax.rsqrt(power + EPS)
            stats[at, :] = jnp.where(lane == 0, mean, by)
            value = by * (velocity[at, :] - mean * sums[0, 0:1, :]) + sums[1, 0:1, :]
            velocity[at, :] = value
            target = other[at, :].astype(F32) - sample[at, :].astype(F32)
            wrong = (value - target) * scalars[1]
            sent = (by * wrong).astype(BF16).astype(F32)
            flipped[:, at] = jnp.transpose(sent).astype(BF16)
            tail[0] += jnp.sum((mean * sent).reshape(piece // 8, 8, cols), axis=0)
            tail[1] += jnp.sum(wrong.reshape(piece // 8, 8, cols), axis=0)

        ends = [jnp.sum(jnp.transpose(tail[i]), axis=1, keepdims=True) for i in range(2)]
        edge[...] = jnp.concatenate(ends, axis=1)
    for copy in drains:
        copy.wait()


def project(where, scalars, sums, sample, other, scaled, hops, prior, earlier, last):
    clip_rows, cols = sample.shape
    width = scaled.shape[0]
    group = 1 if cols % 128 else 2
    depth = group * cols
    places = width // depth
    slots = len(hops) * 2 // group
    pieces = [piece for hop, _ in hops for piece, _, _ in hop]
    plan = [[(low, side, place) for _, low, side in hop] for hop, place in hops]
    out_shape = [
        jax.ShapeDtypeStruct((clip_rows, cols), F32),
        jax.ShapeDtypeStruct((places, clip_rows, depth), BF16),
        jax.ShapeDtypeStruct((clip_rows, 128), F32),
    ]
    if last:
        out_shape.append(jax.ShapeDtypeStruct((cols, clip_rows), BF16))
        out_shape.append(jax.ShapeDtypeStruct((cols, 2), F32))
    if prior:
        velocity, inputs, stats = earlier
        earlier = [velocity, stats, inputs]
    need = 2 * slots * depth * (clip_rows + cols) + clip_rows * cols * 20 + clip_rows * 128 * 16
    return pl.pallas_call(
        functools.partial(project_kernel, prior, last, plan),
        out_shape=out_shape,
        in_specs=[SMEM, SMEM] + [VMEM] * 3 + [ANY] * (1 + len(pieces))
        + ([VMEM, VMEM, ANY] if prior else []),
        out_specs=[VMEM, ANY] + [VMEM] * (len(out_shape) - 2),
        scratch_shapes=[
            pltpu.VMEM((slots, clip_rows, depth), BF16),
            pltpu.VMEM((len(hops), 2 * cols, cols), BF16),
            pltpu.VMEM((clip_rows, 128), F32),
            pltpu.VMEM((2, 8, cols), F32),
            pltpu.SemaphoreType.DMA((len(pieces),)),
            pltpu.SemaphoreType.DMA((len(hops),)),
            pltpu.SemaphoreType.DMA((len(hops),)),
        ],
        input_output_aliases={6 + len(pieces) + 2: 1} if prior else {},
        compiler_params=pltpu.CompilerParams(vmem_limit_bytes=need + 8 * MIB),
        cost_estimate=pl.CostEstimate(flops=1, bytes_accessed=1, transcendentals=0),
        name="project",
    )(where, scalars, sums, sample, other, scaled, *pieces, *earlier)


def outer_kernel(picks, mod, edge, flipped, inputs, *outs):
    del picks
    cols = flipped.shape[0]
    if inputs.shape[0] == 1:
        term = jnp.dot(flipped[...], inputs[0], preferred_element_type=F32)
        terms = [term[:, half * cols : (half + 1) * cols] for half in range(2)]
        mods = [mod[0, :, half * cols : (half + 1) * cols] for half in range(2)]
    else:
        terms = [jnp.dot(flipped[...], inputs[h], preferred_element_type=F32) for h in range(2)]
        mods = [mod[0], mod[1]]
    for half in range(2):
        shift, gain = mods[half][0:1, :], 1.0 + mods[half][1:2, :]
        term = (terms[half] - edge[:, 0:1]) * gain + edge[:, 1:2] * shift
        for i, out in enumerate(outs[half::2]):

            @pl.when(pl.program_id(0) == i)
            def _():
                out[...] = term.astype(out.dtype)


def outer(picks, mod, edge, flipped, inputs, dtypes):
    cols, rows = flipped.shape
    count = len(picks)
    group = inputs.shape[2] // cols

    def spot(i, picks):
        return (picks[i], 0, 0)

    return pl.pallas_call(
        outer_kernel,
        out_shape=[jax.ShapeDtypeStruct((cols, cols), dtype) for dtype in dtypes],
        grid_spec=pltpu.PrefetchScalarGridSpec(
            num_scalar_prefetch=1,
            grid=(count,),
            in_specs=[
                pl.BlockSpec((2 // group, 2, group * cols), spot),
                pl.BlockSpec((cols, 2), lambda i, picks: (0, 0)),
                pl.BlockSpec((cols, rows), lambda i, picks: (0, 0)),
                pl.BlockSpec((2 // group, rows, group * cols), spot),
            ],
            out_specs=[pl.BlockSpec((cols, cols), lambda i, picks: (0, 0))] * (2 * count),
        ),
        compiler_params=pltpu.CompilerParams(
            vmem_limit_bytes=cols * (rows * 16 + cols * (16 * count + 16)) + 6 * MIB
        ),
        cost_estimate=pl.CostEstimate(
            flops=4 * rows * cols * cols * count,
            bytes_accessed=4 * rows * cols * (count + 1) + 4 * cols * cols * count,
            transcendentals=0,
        ),
        name="outer",
    )(jnp.stack(picks).astype(jnp.int32), mod, edge, flipped, inputs)


def finish_kernel(terms, *refs):
    *parts, out = refs
    for half in range(2):
        total = parts[half * terms][...]
        for ref in parts[half * terms + 1 : (half + 1) * terms]:
            total += ref[...].astype(F32)
        out[half] = jnp.transpose(total)


def finish(halves):
    cols = halves[0][0].shape[0]
    lanes = 128 if cols % 128 == 0 else cols
    parts = [part for half in halves for part in half]
    return pl.pallas_call(
        functools.partial(finish_kernel, len(halves[0])),
        grid=(cols // lanes,),
        out_shape=jax.ShapeDtypeStruct((2, cols, cols), F32),
        in_specs=[pl.BlockSpec((cols, lanes), lambda i: (0, i))] * len(parts),
        out_specs=pl.BlockSpec((2, lanes, cols), lambda i: (0, i, 0)),
        compiler_params=pltpu.CompilerParams(vmem_limit_bytes=cols * cols * 16 + 8 * MIB),
        name="finish",
    )(*parts).reshape(2 * cols, cols)


def per_device(
    sample, noise, gen_branch, step, teacher_mod, fake_mod, teacher_weight, fake_weight, gen_gate
):
    clips = lax.axis_size("clip")
    shards = lax.axis_size("fsdp")
    clip = lax.axis_index("clip")
    shard = lax.axis_index("fsdp")
    clip_rows, cols = sample.shape
    width = cols * shards
    total_tokens = clip_rows * clips
    hops = shards // 2
    group = 1 if cols % 128 else 2
    rows = clip_rows // CHUNKS
    orders = clip_orders(clips)

    frac = step.astype(F32)[0] / 1000.0
    sigma = 5.0 * frac / (1.0 + 4.0 * frac)
    noised = ((1.0 - sigma) * sample.astype(F32) + sigma * noise.astype(F32)).astype(BF16)

    order = list(range(0, hops, 2)) + list(range(hops - 1 - hops % 2, 0, -2))
    ring = [
        (2 * order[i] + core, 2 * order[(i + 1) % hops] + core)
        for i in range(hops)
        for core in range(2)
    ]
    line = shard // 2
    rank = jnp.where(line % 2 == 0, line // 2, hops - 1 - line // 2)
    places = []
    for hop in range(hops):
        at = (rank + hops - hop) % hops
        places.append(jnp.where(2 * at < hops, 2 * at, 2 * (hops - 1 - at) + 1))
    swap = [(i, i ^ 1) for i in range(shards)]
    half_rows = fake_weight.shape[0] // 2
    far = [key for key in ((m, h) for m in range(clips) for h in range(2)) if key[0] & (key[0] - 1)]
    seen = {}

    def gated(name, value):
        names = [other for other in GATES.get(name, ()) if other in seen]
        return after(value, *(seen[other] for other in names))

    def hop_to(hop, i):
        name = "AB"[i] + str(hop)
        source = seen["AB"[i] + str(hop - 1)] if hop > 1 else noised[i * rows : (i + 1) * rows]
        seen[name] = lax.ppermute(gated(name, source), "fsdp", ring)

    def cross(hop, i):
        name = "AB"[i] + str(hop)
        seen["c" + name] = lax.ppermute(gated("c" + name, seen[name]), "fsdp", swap)

    fake_direct = neighbour_blocks(fake_weight, clips)
    for i, block in enumerate(fake_direct.values()):
        seen["f" + str(i)] = block
    for i in range(CHUNKS):
        hop_to(1, i)
    seen["own"] = lax.ppermute(noised, "fsdp", swap)
    for i in range(CHUNKS):
        cross(1, i)
    for i in range(CHUNKS):
        hop_to(2, i)
    parts = relay_parts({bit: gated("relay", block) for bit, block in fake_direct.items()}, half_rows)
    seen["parts"] = list(parts.values())[0]
    seen["parts1"] = list(parts.values())[-1]
    fake_blocks = relay_blocks(parts, clips)
    for mask, block in fake_direct.items():
        fake_blocks[mask, 0] = fake_blocks[mask, 1] = block
    seen["far0"], seen["far1"] = fake_blocks[far[0]], fake_blocks[far[1]]
    scalars = jnp.stack([sigma, jnp.float32(1.0 / math.sqrt(total_tokens))])
    owners = jnp.stack([clip ^ mask for mask in range(clips)]).astype(jnp.int32)
    where = jnp.stack(places + [shard % 2]).astype(jnp.int32)
    scaled, sums = scale(owners, jnp.transpose(fake_mod[0]), fake_weight, fake_blocks)
    seen["sums"] = sums
    teacher_parts = {}
    own = gated("teacher", teacher_weight)
    own = [own[:half_rows], own[half_rows:]]
    for phase in range(len(orders[0][1])):
        for half, order in orders:
            block = swap_clip(gated("teacher" + str(min(phase, 1)), own[half]), order[phase], clips)
            teacher_parts[order[phase], half] = block
            seen["t" + str(phase) + str(half)] = block
    tokens = [([(noised, 0, 0), (seen["own"], 0, 1)], 0)]

    def add_hop(hop):
        pieces = []
        for i in range(CHUNKS):
            name = "AB"[i] + str(hop)
            pieces += [(seen[name], i * rows, 0), (seen["c" + name], i * rows, 1)]
        tokens.append((pieces, hop))

    add_hop(1)
    for hop in range(2, hops):
        for i in range(CHUNKS):
            if hop > 2:
                hop_to(hop, i)
            if hop < hops - 1:
                cross(hop, i)
        if hop < hops - 1:
            add_hop(hop)
    cut = max(1, hops - 2)
    done = project(
        where, scalars, sums, sample, noise, scaled, tokens[:cut], 0, (), False
    )
    seen["soon"] = done[2]
    if cut < hops - 1:
        done = project(
            where, scalars, sums, sample, noise, scaled, tokens[cut:], 2 * cols * cut, done, False
        )
    seen["early"] = done[2]
    for key, block in teacher_parts.items():
        teacher_parts[key] = gated("teacher relay", block)
    teacher_blocks = relay_blocks(teacher_parts, clips)
    for i in range(CHUNKS):
        cross(hops - 1, i)
    add_hop(hops - 1)
    fake_velocity, inputs, stats, flipped, edge = project(
        where, scalars, sums, sample, noise, scaled, tokens[-1:], 2 * cols * (hops - 1), done, True
    )
    by_place = jnp.swapaxes(fake_mod[0].reshape(2, shards // group, group * cols), 0, 1)
    flipped = after(flipped, *(teacher_blocks[key] for key in far))

    def going(mask):
        return [bool(mask & order[0]) for _, order in orders]

    held = {}

    def terms(masks, left):
        dtypes = [BF16 if out else F32 for mask in masks for out in going(mask)]
        got = outer([clip ^ mask for mask in masks], by_place, edge, left, inputs, dtypes)
        held.update(zip([(mask, half) for mask in masks for half in range(2)], got))

    ranks = [[m for m in range(clips) if sum(going(m)) == n] for n in (2, 1, 0)]
    terms(ranks[0], flipped)
    if ranks[1]:
        terms(ranks[1], flipped)
    ready = list(held.values())
    halves = []
    sent = {key: swap_clip(held[key], orders[key[1]][1][0], clips) for key in held if going(key[0])[key[1]]}
    firsts = [sent[key] for key in sent if key[0] in ranks[0]]
    seconds = [sent[key] for key in sent if key[0] not in ranks[0]]
    terms(ranks[2], after(flipped, *firsts))
    for half, order in orders:
        mine = {mask: [block] for (mask, h), block in held.items() if h == half}
        for bit in order:
            for mask in [mask for mask in mine if mask & bit]:
                block = mine.pop(mask)
                if bit == order[0]:
                    got = sent[mask, half]
                else:
                    got = swap_clip(sum(part.astype(F32) for part in block).astype(BF16), bit, clips)
                mine[mask ^ bit].append(got)
        halves.append(mine[0])
    fake_grad = finish(halves)

    scaled, sums = scale(
        owners, jnp.transpose(teacher_mod[0]), after(teacher_weight, *ready), teacher_blocks
    )
    depth = group * cols
    velocity = 0.0
    for p in range(width // depth):
        left = inputs[p]
        left = after(left, *firsts) if p == 0 else after(left, velocity)
        right = scaled[p * depth : (p + 1) * depth]
        velocity = velocity + jnp.dot(left, right, preferred_element_type=F32)
    velocity = stats[:, 1:2] * (velocity - stats[:, 0:1] * sums[0, :1]) + sums[1, :1]
    away = sample.astype(F32) - (noised.astype(F32) - sigma * velocity)
    away = after(jnp.sum(jnp.abs(away)).reshape(1, 1), *seconds)
    bit = 1
    while bit < shards:
        away = away + lax.ppermute(away, "fsdp", [(i, i ^ bit) for i in range(shards)])
        bit *= 2
    gap_value = away / (clip_rows * width)
    push = sigma * (velocity - fake_velocity) / (gap_value + EPS)
    branch_cot = (gen_gate * push).astype(BF16)
    gate_grad = jnp.sum(push * gen_branch.astype(F32), axis=0, keepdims=True) / math.sqrt(clip_rows)
    return (branch_cot, gate_grad, fake_grad)


def solution(mesh):
    placed = (
        P("clip", "fsdp"),
        P("clip", "fsdp"),
        P("clip", "fsdp"),
        P("clip"),
        P("clip", None, None),
        P("clip", None, None),
        P("clip", "fsdp"),
        P("clip", "fsdp"),
        P("clip", "fsdp"),
    )
    return jax.shard_map(
        per_device,
        mesh=mesh,
        in_specs=placed,
        out_specs=(P("clip", "fsdp"), P("clip", "fsdp"), P("clip", "fsdp")),
        check_vma=False,
    )
```

```python
import functools
import math

import jax
import jax.numpy as jnp
from jax import lax
from jax.experimental import pallas as pl
from jax.experimental.pallas import tpu as pltpu
from jax.sharding import PartitionSpec as P

EPS = 1e-06
BF16 = jnp.bfloat16
F32 = jnp.float32
MIB = 1024 * 1024
CHUNKS = 2
GATES = {'relay': ('own',), 'teacher': ('parts', 'parts1'), 'B2': ('f0', 'f1'), 'B3': ('sums', 't00', 't01'), 'cB2': ('far0', 'far1'), 'cA3': ('soon',), 'cB3': ('early', 't10', 't11'), 'teacher relay': ('sums',), 'cA2': ('sums',), 'cB1': ('far0', 'far1')}
ANY = pl.BlockSpec(memory_space=pl.ANY)
SMEM = pl.BlockSpec(memory_space=pltpu.SMEM)
VMEM = pl.BlockSpec(memory_space=pltpu.VMEM)


def after(value, *earlier):
    return lax.optimization_barrier((value, *earlier))[0]


def swap_clip(value, bit, count):
    return lax.ppermute(value, "clip", [(i, i ^ bit) for i in range(count)])


def clip_orders(count):
    bits = [1 << i for i in range(count.bit_length() - 1)]
    return ((0, bits), (1, bits[::-1]))


def neighbour_blocks(weight, count):
    return {bit: swap_clip(weight, bit, count) for bit in clip_orders(count)[0][1]}


def relay_parts(direct, rows):
    parts = {}
    for half in range(2):
        for bit, block in direct.items():
            parts[bit, half] = block[half * rows : (half + 1) * rows]
    return parts


def relay_blocks(parts, count):
    pieces = {}
    for half, order in clip_orders(count):
        held = {}
        for bit in order:
            for mask in list(held):
                held[mask ^ bit] = swap_clip(held[mask], bit, count)
            held[bit] = parts[bit, half]
        for mask, block in held.items():
            pieces[mask, half] = block
    return pieces


def scale_kernel(keys, where, mod, weight, *refs):
    blocks, refs = refs[: len(keys)], refs[len(keys) :]
    out, sums, full, column, sems, osems = refs
    half_rows = weight.shape[0] // 2
    cols = weight.shape[1]
    loads, drains = [], []
    for index, (mask, half) in enumerate([(0, 0), (0, 1)] + keys):
        ref = weight if mask == 0 else blocks[index - 2]
        source = ref.at[pl.ds(half * half_rows, half_rows)] if ref.shape[0] > half_rows else ref
        spot = pl.multiple_of((where[mask] * 2 + half) * half_rows, half_rows)
        at = pl.ds(spot, half_rows)
        loads.append((pltpu.make_async_copy(source, full.at[at], sems.at[index]), spot))
        drains.append(pltpu.make_async_copy(full.at[at], out.at[at], osems.at[index]))
        loads[-1][0].start()
    tile = 160
    sums[...] = jnp.zeros_like(sums)
    for index, ((load, spot), drain) in enumerate(zip(loads, drains)):
        mask, half = ([(0, 0), (0, 1)] + keys)[index]
        column[...] = jnp.transpose(mod[where[mask] * 2 + half])
        load.wait()

        @pl.loop(0, half_rows // tile)
        def _(step):
            low = pl.multiple_of(step * tile, tile)
            at = pl.ds(pl.multiple_of(spot + low, tile), tile)
            value = full[at, :].astype(F32)
            shifted = value * column[pl.ds(low, tile), 0:1]
            scaled = (value * (1.0 + column[pl.ds(low, tile), 1:2])).astype(BF16)
            full[at, :] = scaled
            sums[0] += jnp.sum(scaled.astype(F32).reshape(tile // 8, 8, cols), axis=0)
            sums[1] += jnp.sum(shifted.reshape(tile // 8, 8, cols), axis=0)

        drain.start()
    for i in range(2):
        sums[i] = jnp.broadcast_to(jnp.sum(sums[i], axis=0, keepdims=True), (8, cols))
    for drain in drains:
        drain.wait()


def scale(where, mod, weight, blocks):
    cols = weight.shape[1]
    half_rows = weight.shape[0] // 2
    mod = jnp.swapaxes(mod.reshape(2, -1, half_rows), 0, 1)
    count = len(blocks) + 2
    width = half_rows * count
    return pl.pallas_call(
        functools.partial(scale_kernel, list(blocks)),
        out_shape=(
            jax.ShapeDtypeStruct((width, cols), BF16),
            jax.ShapeDtypeStruct((2, 8, cols), F32),
        ),
        in_specs=[SMEM, VMEM] + [ANY] * (1 + len(blocks)),
        out_specs=(ANY, VMEM),
        scratch_shapes=[
            pltpu.VMEM((width, cols), BF16),
            pltpu.VMEM((half_rows, 2), F32),
            pltpu.SemaphoreType.DMA((count,)),
            pltpu.SemaphoreType.DMA((count,)),
        ],
        compiler_params=pltpu.CompilerParams(vmem_limit_bytes=60 * MIB),
        cost_estimate=pl.CostEstimate(
            flops=1, bytes_accessed=1, transcendentals=0
        ),
        name="scale",
    )(where, mod, weight, *blocks.values())


def gradient_halves(flipped, tokens, mod, edge):
    cols = flipped.shape[0]
    if len(tokens.shape) == 2:
        term = jnp.dot(flipped[...], tokens[...], preferred_element_type=F32)
        terms = [term[:, half * cols : (half + 1) * cols] for half in range(2)]
        mods = [mod[0][:, half * cols : (half + 1) * cols] for half in range(2)]
    else:
        terms = [jnp.dot(flipped[...], tokens[h], preferred_element_type=F32) for h in range(2)]
        mods = mod
    return [
        (term - edge[:, 0:1]) * (1.0 + part[1:2, :]) + edge[:, 1:2] * part[0:1, :]
        for term, part in zip(terms, mods)
    ]


def project_kernel(
    prior, last, hops, core_at, where, scalars, sums, mod, sample, other, scaled, *refs
):
    count = sum(len(hop) for hop in hops)
    pieces, refs = refs[:count], refs[count:]
    if prior:
        carried, carry, _, *refs = refs
    velocity, inputs, stats, *refs = refs
    if last:
        fars = where.shape[0] - core_at - 1
        flipped, edge, *refs = refs
        blocks, refs = refs[: 2 * fars], refs[2 * fars :]
    held, full, moments, total, sems, wsems, osems, esems, *refs = refs
    if prior:
        before, *refs = refs
    if last:
        tail, mine, noisy, turned, far = refs
    slots, rows, depth = held.shape
    cols = total.shape[1]
    width = scaled.shape[0]
    parts = 2 * cols // depth
    core = where[core_at]
    span = 2 * cols

    def at_place(place):
        if parts == 1:
            return inputs.at[:, pl.ds(pl.multiple_of(place * span, span), span)]
        return inputs.at[pl.ds(place * 2, 2)]

    loads, arrivals, drains = [], [], []
    index = 0
    for n, hop in enumerate(hops):
        copies = []
        for low, side, place in hop:
            owner = core if side == 0 else 1 - core
            ref = pieces[index]
            at = pl.ds(low, ref.shape[0])
            if parts == 1:
                lanes = pl.ds(pl.multiple_of(owner * cols, cols), cols)
                spot = held.at[n, at, lanes]
            else:
                spot = held.at[2 * n + owner, at]
            copies.append(pltpu.make_async_copy(ref, spot, sems.at[index]))
            index += 1
        arrivals.append(copies)
        place = where[hop[0][2]]
        low = pl.multiple_of(place * span, span)
        loads.append(pltpu.make_async_copy(scaled.at[pl.ds(low, span)], full.at[n], wsems.at[n]))
        here = held.at[n] if parts == 1 else held.at[pl.ds(2 * n, 2)]
        drains.append(pltpu.make_async_copy(here, at_place(place), osems.at[n]))
    for copies, load in zip(arrivals, loads):
        for copy in copies:
            copy.start()
        load.start()
    extras = []

    def extra(source, target):
        extras.append(pltpu.make_async_copy(source, target, esems.at[len(extras)]))
        extras[-1].start()
        return extras[-1]

    waits = []
    if prior:
        waits.append(extra(carry, before))
    if last:
        waits += [extra(sample, mine), extra(other, noisy)]
    piece = 256
    lane = lax.broadcasted_iota(jnp.int32, (piece, 128), 1)
    for n in range(len(hops)):
        for copy in arrivals[n]:
            copy.wait()
        drains[n].start()
        loads[n].wait()
        for part in range(parts):
            slot = n * parts + part
            term = jnp.dot(
                held[slot], full[n, pl.ds(part * depth, depth), :], preferred_element_type=F32
            )
            if slot:
                total[...] += term
            else:
                total[...] = term
            for low in range(0, rows, piece):
                at = pl.ds(low, piece)
                if slot == 0 and prior:
                    moments[at, :] = carried[at, :]
                elif slot == 0:
                    near = held[0, at, :128].astype(F32)
                    near = jnp.sum(near, axis=1, keepdims=True) * (1.0 / 128)
                    moments[at, :] = jnp.where(lane == 0, near, 0.0)
                spread = held[slot, at, :].astype(F32) - moments[at, 0:1]
                sum_ = jnp.sum(spread, axis=1, keepdims=True)
                power = jnp.sum(spread * spread, axis=1, keepdims=True)
                more = jnp.where(lane == 1, sum_, jnp.where(lane == 2, power, 0.0))
                moments[at, :] += more
    for copy in waits:
        copy.wait()
    if not last:
        stats[...] = moments[...]
        if prior:
            total[...] += before[...]
        outs = [extra(total, velocity)]
    else:
        for copy in drains:
            copy.wait()
        nears = [extra(at_place(where[core_at + 1 + j]), far.at[j]) for j in range(fars)]
        tail[...] = jnp.zeros_like(tail)

        @pl.loop(0, rows // piece)
        def _(step):
            low = pl.multiple_of(step * piece, piece)
            at = pl.ds(low, piece)
            away = moments[at, 1:2] * (1.0 / width)
            power = jnp.maximum(moments[at, 2:3] * (1.0 / width) - away * away, 0.0)
            mean = moments[at, 0:1] + away
            by = lax.rsqrt(power + EPS)
            stats[at, :] = jnp.where(lane == 0, mean, by)
            value = total[at, :] + before[at, :]
            value = by * (value - mean * sums[0, 0:1, :]) + sums[1, 0:1, :]
            total[at, :] = value
            target = noisy[at, :].astype(F32) - mine[at, :].astype(F32)
            wrong = (value - target) * scalars[1]
            sent = (by * wrong).astype(BF16).astype(F32)
            turned[:, at] = jnp.transpose(sent).astype(BF16)
            tail[0] += jnp.sum((mean * sent).reshape(piece // 8, 8, cols), axis=0)
            tail[1] += jnp.sum(wrong.reshape(piece // 8, 8, cols), axis=0)

        outs = [extra(turned, flipped), extra(total, velocity)]
        ends = [jnp.sum(jnp.transpose(tail[i]), axis=1, keepdims=True) for i in range(2)]
        edge[...] = jnp.concatenate(ends, axis=1)
        for j in range(fars):
            nears[j].wait()
            place = where[core_at + 1 + j]
            mods = [mod[place]] if parts == 1 else [mod[2 * place], mod[2 * place + 1]]
            for half, term in enumerate(gradient_halves(turned, far.at[j], mods, edge)):
                blocks[2 * j + half][...] = term.astype(BF16)
    for copy in outs + ([] if last else drains):
        copy.wait()


def project(where, scalars, sums, mod, sample, other, scaled, hops, prior, earlier, core_at, last):
    clip_rows, cols = sample.shape
    width = scaled.shape[0]
    group = 1 if cols % 128 else 2
    depth = group * cols
    slots = len(hops) * 2 // group
    pieces = [piece for hop, _ in hops for piece, _, _ in hop]
    plan = [[(low, side, place) for _, low, side in hop] for hop, place in hops]
    laid = (clip_rows, width) if group == 2 else (width // cols, clip_rows, cols)
    near = (clip_rows, depth) if group == 2 else (2, clip_rows, cols)
    fars = where.shape[0] - core_at - 1
    out_shape = [
        jax.ShapeDtypeStruct((clip_rows, cols), F32),
        jax.ShapeDtypeStruct(laid, BF16),
        jax.ShapeDtypeStruct((clip_rows, 128), F32),
    ]
    out_specs = [ANY, ANY, VMEM]
    scratch = [
        pltpu.VMEM((slots, clip_rows, depth), BF16),
        pltpu.VMEM((len(hops), 2 * cols, cols), BF16),
        pltpu.VMEM((clip_rows, 128), F32),
        pltpu.VMEM((clip_rows, cols), F32),
        pltpu.SemaphoreType.DMA((len(pieces),)),
        pltpu.SemaphoreType.DMA((len(hops),)),
        pltpu.SemaphoreType.DMA((len(hops),)),
        pltpu.SemaphoreType.DMA((5 + fars,)),
    ]
    if prior:
        velocity, inputs, stats = earlier
        earlier = [stats, velocity, inputs]
        scratch.append(pltpu.VMEM((clip_rows, cols), F32))
    if last:
        out_shape.append(jax.ShapeDtypeStruct((cols, clip_rows), BF16))
        out_shape.append(jax.ShapeDtypeStruct((cols, 2), F32))
        out_shape += [jax.ShapeDtypeStruct((cols, cols), BF16)] * (2 * fars)
        out_specs += [ANY, VMEM] + [VMEM] * (2 * fars)
        scratch += [
            pltpu.VMEM((2, 8, cols), F32),
            pltpu.VMEM((clip_rows, cols), BF16),
            pltpu.VMEM((clip_rows, cols), BF16),
            pltpu.VMEM((cols, clip_rows), BF16),
            pltpu.VMEM((fars, *near), BF16),
        ]
    return pl.pallas_call(
        functools.partial(project_kernel, prior, last, plan, core_at),
        out_shape=out_shape,
        in_specs=[SMEM, SMEM, VMEM, VMEM] + [ANY] * (3 + len(pieces)) + ([VMEM, ANY, ANY] if prior else []),
        out_specs=out_specs,
        scratch_shapes=scratch,
        input_output_aliases={7 + len(pieces) + 2: 1} if prior else {},
        compiler_params=pltpu.CompilerParams(vmem_limit_bytes=60 * MIB),
        cost_estimate=pl.CostEstimate(flops=1, bytes_accessed=1, transcendentals=0),
        name="project",
    )(where, scalars, sums, mod, sample, other, scaled, *pieces, *earlier)


def outer_kernel(picks, mod, edge, flipped, inputs, *outs):
    del picks
    mods = [mod[i] for i in range(mod.shape[0])]
    for half, term in enumerate(gradient_halves(flipped, inputs, mods, edge)):
        for i, out in enumerate(outs[half::2]):

            @pl.when(pl.program_id(0) == i)
            def _():
                out[...] = term.astype(out.dtype)


def outer(picks, mod, edge, flipped, inputs, dtypes):
    cols, rows = flipped.shape
    count = len(picks)
    group = 2 if len(inputs.shape) == 2 else 1

    def spot(i, picks):
        return (picks[i], 0, 0)

    if group == 2:
        tokens = pl.BlockSpec((rows, 2 * cols), lambda i, picks: (0, picks[i]))
    else:
        tokens = pl.BlockSpec((2, rows, cols), spot)
    return pl.pallas_call(
        outer_kernel,
        out_shape=[jax.ShapeDtypeStruct((cols, cols), dtype) for dtype in dtypes],
        grid_spec=pltpu.PrefetchScalarGridSpec(
            num_scalar_prefetch=1,
            grid=(count,),
            in_specs=[
                pl.BlockSpec((2 // group, 2, group * cols), spot),
                pl.BlockSpec((cols, 2), lambda i, picks: (0, 0)),
                pl.BlockSpec((cols, rows), lambda i, picks: (0, 0)),
                tokens,
            ],
            out_specs=[pl.BlockSpec((cols, cols), lambda i, picks: (0, 0))] * (2 * count),
        ),
        compiler_params=pltpu.CompilerParams(vmem_limit_bytes=60 * MIB),
        cost_estimate=pl.CostEstimate(
            flops=4 * rows * cols * cols * count,
            bytes_accessed=4 * rows * cols * (count + 1) + 4 * cols * cols * count,
            transcendentals=0,
        ),
        name="outer",
    )(jnp.stack(picks).astype(jnp.int32), mod, edge, flipped, inputs)


def finish_kernel(terms, *refs):
    *parts, out = refs
    for half in range(2):
        total = parts[half * terms][...]
        for ref in parts[half * terms + 1 : (half + 1) * terms]:
            total += ref[...].astype(F32)
        out[half] = jnp.transpose(total)


def finish(halves):
    cols = halves[0][0].shape[0]
    lanes = 128 if cols % 128 == 0 else cols
    parts = [part for half in halves for part in half]
    return pl.pallas_call(
        functools.partial(finish_kernel, len(halves[0])),
        grid=(cols // lanes,),
        out_shape=jax.ShapeDtypeStruct((2, cols, cols), F32),
        in_specs=[pl.BlockSpec((cols, lanes), lambda i: (0, i))] * len(parts),
        out_specs=pl.BlockSpec((2, lanes, cols), lambda i: (0, i, 0)),
        compiler_params=pltpu.CompilerParams(vmem_limit_bytes=cols * cols * 16 + 8 * MIB),
        name="finish",
    )(*parts).reshape(2 * cols, cols)


def per_device(
    sample, noise, gen_branch, step, teacher_mod, fake_mod, teacher_weight, fake_weight, gen_gate
):
    clips = lax.axis_size("clip")
    shards = lax.axis_size("fsdp")
    clip = lax.axis_index("clip")
    shard = lax.axis_index("fsdp")
    clip_rows, cols = sample.shape
    width = cols * shards
    total_tokens = clip_rows * clips
    hops = shards // 2
    group = 1 if cols % 128 else 2
    rows = clip_rows // CHUNKS
    orders = clip_orders(clips)

    frac = step.astype(F32)[0] / 1000.0
    sigma = 5.0 * frac / (1.0 + 4.0 * frac)
    noised = ((1.0 - sigma) * sample.astype(F32) + sigma * noise.astype(F32)).astype(BF16)

    order = list(range(0, hops, 2)) + list(range(hops - 1 - hops % 2, 0, -2))
    ring = [
        (2 * order[i] + core, 2 * order[(i + 1) % hops] + core)
        for i in range(hops)
        for core in range(2)
    ]
    line = shard // 2
    rank = jnp.where(line % 2 == 0, line // 2, hops - 1 - line // 2)
    places = []
    for hop in range(hops):
        at = (rank + hops - hop) % hops
        places.append(jnp.where(2 * at < hops, 2 * at, 2 * (hops - 1 - at) + 1))
    swap = [(i, i ^ 1) for i in range(shards)]
    half_rows = fake_weight.shape[0] // 2
    far = [key for key in ((m, h) for m in range(clips) for h in range(2)) if key[0] & (key[0] - 1)]
    seen = {}

    def gated(name, value):
        names = [other for other in GATES.get(name, ()) if other in seen]
        return after(value, *(seen[other] for other in names))

    def hop_to(hop, i):
        name = "AB"[i] + str(hop)
        source = seen["AB"[i] + str(hop - 1)] if hop > 1 else noised[i * rows : (i + 1) * rows]
        seen[name] = lax.ppermute(gated(name, source), "fsdp", ring)

    def cross(hop, i):
        name = "AB"[i] + str(hop)
        seen["c" + name] = lax.ppermute(gated("c" + name, seen[name]), "fsdp", swap)

    fake_direct = neighbour_blocks(fake_weight, clips)
    for i, block in enumerate(fake_direct.values()):
        seen["f" + str(i)] = block
    for i in range(CHUNKS):
        hop_to(1, i)
    seen["own"] = lax.ppermute(noised, "fsdp", swap)
    for i in range(CHUNKS):
        cross(1, i)
    for i in range(CHUNKS):
        hop_to(2, i)
    parts = relay_parts({bit: gated("relay", block) for bit, block in fake_direct.items()}, half_rows)
    seen["parts"] = list(parts.values())[0]
    seen["parts1"] = list(parts.values())[-1]
    fake_blocks = relay_blocks(parts, clips)
    for mask, block in fake_direct.items():
        fake_blocks[mask, 0] = fake_blocks[mask, 1] = block
    seen["far0"], seen["far1"] = fake_blocks[far[0]], fake_blocks[far[1]]
    scalars = jnp.stack([sigma, jnp.float32(1.0 / math.sqrt(total_tokens))])
    owners = jnp.stack([clip ^ mask for mask in range(clips)]).astype(jnp.int32)
    where = jnp.stack(places + [shard % 2]).astype(jnp.int32)
    by_place = jnp.swapaxes(fake_mod[0].reshape(2, shards // group, group * cols), 0, 1)
    scaled, sums = scale(owners, fake_mod[0], fake_weight, fake_blocks)
    seen["sums"] = sums
    teacher_parts = {}
    own = gated("teacher", teacher_weight)
    own = [own[:half_rows], own[half_rows:]]
    for phase in range(len(orders[0][1])):
        for half, order in orders:
            block = swap_clip(gated("teacher" + str(min(phase, 1)), own[half]), order[phase], clips)
            teacher_parts[order[phase], half] = block
            seen["t" + str(phase) + str(half)] = block
    tokens = [([(noised, 0, 0), (seen["own"], 0, 1)], 0)]

    def add_hop(hop):
        pieces = []
        for i in range(CHUNKS):
            name = "AB"[i] + str(hop)
            pieces += [(seen[name], i * rows, 0), (seen["c" + name], i * rows, 1)]
        tokens.append((pieces, hop))

    add_hop(1)
    for hop in range(2, hops):
        for i in range(CHUNKS):
            if hop > 2:
                hop_to(hop, i)
            if hop < hops - 1:
                cross(hop, i)
        if hop < hops - 1:
            add_hop(hop)
    cut = max(1, hops - 2)
    done = project(
        where, scalars, sums, by_place, sample, noise, scaled, tokens[:cut], 0, (), hops, False
    )
    seen["soon"] = done[2]
    if cut < hops - 1:
        done = project(
            where, scalars, sums, by_place, sample, noise, scaled, tokens[cut:], 2 * cols * cut,
            done, hops, False,
        )
    seen["early"] = done[2]
    for key, block in teacher_parts.items():
        teacher_parts[key] = gated("teacher relay", block)
    teacher_blocks = relay_blocks(teacher_parts, clips)
    for i in range(CHUNKS):
        cross(hops - 1, i)
    add_hop(hops - 1)
    def going(mask):
        return [bool(mask & order[0]) for _, order in orders]

    ranks = [[m for m in range(clips) if sum(going(m)) == n] for n in (2, 1, 0)]
    where = jnp.concatenate([where, jnp.stack([clip ^ mask for mask in ranks[0]]).astype(jnp.int32)])
    fake_velocity, inputs, stats, flipped, edge, *blocks = project(
        where, scalars, sums, by_place, sample, noise, scaled, tokens[-1:], 2 * cols * (hops - 1),
        done, hops, True,
    )

    held = dict(zip([(mask, half) for mask in ranks[0] for half in range(2)], blocks))

    def terms(masks, left):
        dtypes = [BF16 if out else F32 for mask in masks for out in going(mask)]
        got = outer([clip ^ mask for mask in masks], by_place, edge, left, inputs, dtypes)
        held.update(zip([(mask, half) for mask in masks for half in range(2)], got))

    if ranks[1]:
        terms(ranks[1], after(flipped, *blocks))
    ready = list(held.values())
    halves, relayed = [], []
    sent = {key: swap_clip(held[key], orders[key[1]][1][0], clips) for key in held if going(key[0])[key[1]]}
    firsts = [sent[key] for key in sent if key[0] in ranks[0]]
    seconds = [sent[key] for key in sent if key[0] not in ranks[0]]
    terms(ranks[2], after(flipped, *firsts))
    for half, order in orders:
        mine = {mask: [block] for (mask, h), block in held.items() if h == half}
        for bit in order:
            for mask in [mask for mask in mine if mask & bit]:
                block = mine.pop(mask)
                if bit == order[0]:
                    got = sent[mask, half]
                else:
                    block = sum(part.astype(F32) for part in block).astype(BF16)
                    relayed.append(block)
                    got = swap_clip(block, bit, clips)
                mine[mask ^ bit].append(got)
        halves.append(mine[0])
    fake_grad = finish(halves)

    scaled, sums = scale(
        owners, teacher_mod[0], after(teacher_weight, *ready), teacher_blocks
    )
    left = after(inputs, *relayed)

    def add_place(p, total):
        tokens = lax.dynamic_index_in_dim(left, p, 0, keepdims=False)
        right = lax.dynamic_slice(scaled, (p * cols, 0), (cols, cols))
        return total + jnp.dot(tokens, right, preferred_element_type=F32)

    if group == 2:
        velocity = jnp.dot(left, scaled, preferred_element_type=F32)
    else:
        velocity = jnp.zeros((clip_rows, cols), F32)
        velocity = lax.fori_loop(0, width // cols, add_place, velocity)
    velocity = stats[:, 1:2] * (velocity - stats[:, 0:1] * sums[0, :1]) + sums[1, :1]
    away = sample.astype(F32) - (noised.astype(F32) - sigma * velocity)
    away = after(jnp.sum(jnp.abs(away)).reshape(1, 1), *seconds)
    bit = 1
    while bit < shards:
        away = away + lax.ppermute(away, "fsdp", [(i, i ^ bit) for i in range(shards)])
        bit *= 2
    gap_value = away / (clip_rows * width)
    push = sigma * (velocity - fake_velocity) / (gap_value + EPS)
    branch_cot = (gen_gate * push).astype(BF16)
    gate_grad = jnp.sum(push * gen_branch.astype(F32), axis=0, keepdims=True) / math.sqrt(clip_rows)
    return (branch_cot, gate_grad, fake_grad)


def solution(mesh):
    placed = (
        P("clip", "fsdp"),
        P("clip", "fsdp"),
        P("clip", "fsdp"),
        P("clip"),
        P("clip", None, None),
        P("clip", None, None),
        P("clip", "fsdp"),
        P("clip", "fsdp"),
        P("clip", "fsdp"),
    )
    return jax.shard_map(
        per_device,
        mesh=mesh,
        in_specs=placed,
        out_specs=(P("clip", "fsdp"), P("clip", "fsdp"), P("clip", "fsdp")),
        check_vma=False,
    )
```

```python
import functools
import math

import jax
import jax.numpy as jnp
from jax import lax
from jax.experimental import pallas as pl
from jax.experimental.pallas import tpu as pltpu
from jax.sharding import PartitionSpec as P

EPS = 1e-06
BF16 = jnp.bfloat16
F32 = jnp.float32
MIB = 1024 * 1024
CHUNKS = 2
GATES = {
    "relay": ("own",),
    "teacher": ("parts", "parts1"),
    "A3": ("far0", "far1"),
    "B2": ("A2",),
    "B3": ("sums", "t00", "t01"),
    "cB1": ("far0", "far1"),
    "cA2": ("sums",),
    "cB2": ("far0", "far1"),
    "cA3": ("soon",),
    "cB3": ("early", "t10", "t11"),
    "teacher relay": ("sums",),
}
ANY = pl.BlockSpec(memory_space=pl.ANY)
SMEM = pl.BlockSpec(memory_space=pltpu.SMEM)
VMEM = pl.BlockSpec(memory_space=pltpu.VMEM)


def after(value, *earlier):
    return lax.optimization_barrier((value, *earlier))[0]


def swap_clip(value, bit, count):
    return lax.ppermute(value, "clip", [(i, i ^ bit) for i in range(count)])


def clip_orders(count):
    bits = [1 << i for i in range(count.bit_length() - 1)]
    return ((0, bits), (1, bits[::-1]))


def neighbour_blocks(weight, count):
    return {bit: swap_clip(weight, bit, count) for bit in clip_orders(count)[0][1]}


def relay_parts(direct, rows):
    parts = {}
    for half in range(2):
        for bit, block in direct.items():
            parts[bit, half] = block[half * rows : (half + 1) * rows]
    return parts


def relay_blocks(parts, count):
    pieces = {}
    for half, order in clip_orders(count):
        held = {}
        for bit in order:
            for mask in list(held):
                held[mask ^ bit] = swap_clip(held[mask], bit, count)
            held[bit] = parts[bit, half]
        for mask, block in held.items():
            pieces[mask, half] = block
    return pieces


def scale_kernel(keys, where, mod, weight, *refs):
    blocks, refs = refs[: len(keys)], refs[len(keys) :]
    out, sums, full, column, sems, osems = refs
    half_rows = weight.shape[0] // 2
    cols = weight.shape[1]
    loads, drains = [], []
    for index, (mask, half) in enumerate([(0, 0), (0, 1)] + keys):
        ref = weight if mask == 0 else blocks[index - 2]
        source = ref.at[pl.ds(half * half_rows, half_rows)] if ref.shape[0] > half_rows else ref
        spot = pl.multiple_of((where[mask] * 2 + half) * half_rows, half_rows)
        at = pl.ds(spot, half_rows)
        loads.append((pltpu.make_async_copy(source, full.at[at], sems.at[index]), spot))
        drains.append(pltpu.make_async_copy(full.at[at], out.at[at], osems.at[index]))
        loads[-1][0].start()
    tile = 160
    sums[...] = jnp.zeros_like(sums)
    ones = jnp.ones((16, half_rows), BF16)
    row = lax.broadcasted_iota(jnp.int32, (16, half_rows), 0)
    for index, ((load, spot), drain) in enumerate(zip(loads, drains)):
        mask, half = ([(0, 0), (0, 1)] + keys)[index]
        part = mod[where[mask] * 2 + half]
        column[...] = jnp.transpose(part)
        shift = part[0:1, :]
        high = shift.astype(BF16).astype(F32)
        shift = jnp.where(row == 0, high, jnp.where(row == 1, shift - high, 0.0)).astype(BF16)
        load.wait()
        whole = pl.ds(spot, half_rows)
        sums[1] += jnp.dot(shift, full[whole, :], preferred_element_type=F32)

        @pl.loop(0, half_rows // tile)
        def _(step):
            low = pl.multiple_of(step * tile, tile)
            at = pl.ds(pl.multiple_of(spot + low, tile), tile)
            gain = 1.0 + column[pl.ds(low, tile), 1:2]
            full[at, :] = (full[at, :].astype(F32) * gain).astype(BF16)

        drain.start()
        sums[0] += jnp.dot(ones, full[whole, :], preferred_element_type=F32)
    sums[1, 0:1, :] = sums[1, 0:1, :] + sums[1, 1:2, :]
    for drain in drains:
        drain.wait()


def scale(where, mod, weight, blocks):
    cols = weight.shape[1]
    half_rows = weight.shape[0] // 2
    mod = jnp.swapaxes(mod.reshape(2, -1, half_rows), 0, 1)
    count = len(blocks) + 2
    width = half_rows * count
    return pl.pallas_call(
        functools.partial(scale_kernel, list(blocks)),
        out_shape=(
            jax.ShapeDtypeStruct((width, cols), BF16),
            jax.ShapeDtypeStruct((2, 16, cols), F32),
        ),
        in_specs=[SMEM, VMEM] + [ANY] * (1 + len(blocks)),
        out_specs=(ANY, VMEM),
        scratch_shapes=[
            pltpu.VMEM((width, cols), BF16),
            pltpu.VMEM((half_rows, 2), F32),
            pltpu.SemaphoreType.DMA((count,)),
            pltpu.SemaphoreType.DMA((count,)),
        ],
        compiler_params=pltpu.CompilerParams(vmem_limit_bytes=60 * MIB),
        cost_estimate=pl.CostEstimate(
            flops=1, bytes_accessed=1, transcendentals=0
        ),
        name="scale",
    )(where, mod, weight, *blocks.values())


def gradient_halves(flipped, tokens, mod, edge):
    cols = flipped.shape[0]
    if len(tokens.shape) == 2:
        term = jnp.dot(flipped[...], tokens[...], preferred_element_type=F32)
        terms = [term[:, half * cols : (half + 1) * cols] for half in range(2)]
        mods = [mod[0][:, half * cols : (half + 1) * cols] for half in range(2)]
    else:
        terms = [jnp.dot(flipped[...], tokens[h], preferred_element_type=F32) for h in range(2)]
        mods = mod
    return [
        (term - edge[:, 0:1]) * (1.0 + part[1:2, :]) + edge[:, 1:2] * part[0:1, :]
        for term, part in zip(terms, mods)
    ]


def project_kernel(
    prior, last, hops, core_at, where, scalars, sums, mod, sample, other, scaled, *refs
):
    count = sum(len(hop) for hop in hops)
    pieces, refs = refs[:count], refs[count:]
    if prior:
        carried, carry, _, *refs = refs
    velocity, inputs, stats, *refs = refs
    if last:
        fars = where.shape[0] - core_at - 1
        flipped, edge, *refs = refs
        blocks, refs = refs[: 2 * fars], refs[2 * fars :]
    held, full, moments, total, sems, wsems, osems, esems, *refs = refs
    if prior:
        before, *refs = refs
    if last:
        tail, mine, noisy, turned, far = refs
    slots, rows, depth = held.shape
    cols = total.shape[1]
    width = scaled.shape[0]
    parts = 2 * cols // depth
    core = where[core_at]
    span = 2 * cols

    def at_place(place):
        if parts == 1:
            return inputs.at[:, pl.ds(pl.multiple_of(place * span, span), span)]
        return inputs.at[pl.ds(place * 2, 2)]

    loads, arrivals, drains = [], [], []
    index = 0
    for n, hop in enumerate(hops):
        copies = []
        for low, side, place in hop:
            owner = core if side == 0 else 1 - core
            ref = pieces[index]
            at = pl.ds(low, ref.shape[0])
            if parts == 1:
                lanes = pl.ds(pl.multiple_of(owner * cols, cols), cols)
                spot = held.at[n, at, lanes]
            else:
                spot = held.at[2 * n + owner, at]
            copies.append(pltpu.make_async_copy(ref, spot, sems.at[index]))
            index += 1
        arrivals.append(copies)
        place = where[hop[0][2]]
        low = pl.multiple_of(place * span, span)
        loads.append(pltpu.make_async_copy(scaled.at[pl.ds(low, span)], full.at[n], wsems.at[n]))
        here = held.at[n] if parts == 1 else held.at[pl.ds(2 * n, 2)]
        drains.append(pltpu.make_async_copy(here, at_place(place), osems.at[n]))
    for copies, load in zip(arrivals, loads):
        for copy in copies:
            copy.start()
        load.start()
    extras = []

    def extra(source, target):
        extras.append(pltpu.make_async_copy(source, target, esems.at[len(extras)]))
        extras[-1].start()
        return extras[-1]

    waits = []
    if prior:
        waits.append(extra(carry, before))
    if last:
        waits += [extra(sample, mine), extra(other, noisy)]
    piece = 256
    lane = lax.broadcasted_iota(jnp.int32, (piece, 128), 1)
    for n in range(len(hops)):
        for copy in arrivals[n]:
            copy.wait()
        drains[n].start()
        loads[n].wait()
        for part in range(parts):
            slot = n * parts + part
            term = jnp.dot(
                held[slot], full[n, pl.ds(part * depth, depth), :], preferred_element_type=F32
            )
            if slot:
                total[...] += term
            else:
                total[...] = term
            for low in range(0, rows, piece):
                at = pl.ds(low, piece)
                if slot == 0 and prior:
                    moments[at, :] = carried[at, :]
                elif slot == 0:
                    near = held[0, at, :128].astype(F32)
                    near = jnp.sum(near, axis=1, keepdims=True) * (1.0 / 128)
                    moments[at, :] = jnp.where(lane == 0, near, 0.0)
                spread = held[slot, at, :].astype(F32) - moments[at, 0:1]
                sum_ = jnp.sum(spread, axis=1, keepdims=True)
                power = jnp.sum(spread * spread, axis=1, keepdims=True)
                more = jnp.where(lane == 1, sum_, jnp.where(lane == 2, power, 0.0))
                moments[at, :] += more
    for copy in waits:
        copy.wait()
    if not last:
        stats[...] = moments[...]
        if prior:
            total[...] += before[...]
        outs = [extra(total, velocity)]
    else:
        for copy in drains:
            copy.wait()
        nears = [extra(at_place(where[core_at + 1 + j]), far.at[j]) for j in range(fars)]
        tail[...] = jnp.zeros_like(tail)

        @pl.loop(0, rows // piece)
        def _(step):
            low = pl.multiple_of(step * piece, piece)
            at = pl.ds(low, piece)
            away = moments[at, 1:2] * (1.0 / width)
            power = jnp.maximum(moments[at, 2:3] * (1.0 / width) - away * away, 0.0)
            mean = moments[at, 0:1] + away
            by = lax.rsqrt(power + EPS)
            stats[at, :] = jnp.where(lane == 0, mean, by)
            value = total[at, :] + before[at, :]
            value = by * (value - mean * sums[0, 0:1, :]) + sums[1, 0:1, :]
            total[at, :] = value
            target = noisy[at, :].astype(F32) - mine[at, :].astype(F32)
            wrong = (value - target) * scalars[1]
            sent = (by * wrong).astype(BF16).astype(F32)
            turned[:, at] = jnp.transpose(sent).astype(BF16)
            tail[0] += jnp.sum((mean * sent).reshape(piece // 8, 8, cols), axis=0)
            tail[1] += jnp.sum(wrong.reshape(piece // 8, 8, cols), axis=0)

        outs = [extra(turned, flipped), extra(total, velocity)]
        ends = [jnp.sum(jnp.transpose(tail[i]), axis=1, keepdims=True) for i in range(2)]
        edge[...] = jnp.concatenate(ends, axis=1)
        for j in range(fars):
            nears[j].wait()
            place = where[core_at + 1 + j]
            mods = [mod[place]] if parts == 1 else [mod[2 * place], mod[2 * place + 1]]
            for half, term in enumerate(gradient_halves(turned, far.at[j], mods, edge)):
                blocks[2 * j + half][...] = term.astype(BF16)
    for copy in outs + ([] if last else drains):
        copy.wait()


def project(where, scalars, sums, mod, sample, other, scaled, hops, prior, earlier, core_at, last):
    clip_rows, cols = sample.shape
    width = scaled.shape[0]
    group = 1 if cols % 128 else 2
    depth = group * cols
    slots = len(hops) * 2 // group
    pieces = [piece for hop, _ in hops for piece, _, _ in hop]
    plan = [[(low, side, place) for _, low, side in hop] for hop, place in hops]
    laid = (clip_rows, width) if group == 2 else (width // cols, clip_rows, cols)
    near = (clip_rows, depth) if group == 2 else (2, clip_rows, cols)
    fars = where.shape[0] - core_at - 1
    out_shape = [
        jax.ShapeDtypeStruct((clip_rows, cols), F32),
        jax.ShapeDtypeStruct(laid, BF16),
        jax.ShapeDtypeStruct((clip_rows, 128), F32),
    ]
    out_specs = [ANY, ANY, VMEM]
    scratch = [
        pltpu.VMEM((slots, clip_rows, depth), BF16),
        pltpu.VMEM((len(hops), 2 * cols, cols), BF16),
        pltpu.VMEM((clip_rows, 128), F32),
        pltpu.VMEM((clip_rows, cols), F32),
        pltpu.SemaphoreType.DMA((len(pieces),)),
        pltpu.SemaphoreType.DMA((len(hops),)),
        pltpu.SemaphoreType.DMA((len(hops),)),
        pltpu.SemaphoreType.DMA((5 + fars,)),
    ]
    if prior:
        velocity, inputs, stats = earlier
        earlier = [stats, velocity, inputs]
        scratch.append(pltpu.VMEM((clip_rows, cols), F32))
    if last:
        out_shape.append(jax.ShapeDtypeStruct((cols, clip_rows), BF16))
        out_shape.append(jax.ShapeDtypeStruct((cols, 2), F32))
        out_shape += [jax.ShapeDtypeStruct((cols, cols), BF16)] * (2 * fars)
        out_specs += [ANY, VMEM] + [VMEM] * (2 * fars)
        scratch += [
            pltpu.VMEM((2, 8, cols), F32),
            pltpu.VMEM((clip_rows, cols), BF16),
            pltpu.VMEM((clip_rows, cols), BF16),
            pltpu.VMEM((cols, clip_rows), BF16),
            pltpu.VMEM((fars, *near), BF16),
        ]
    return pl.pallas_call(
        functools.partial(project_kernel, prior, last, plan, core_at),
        out_shape=out_shape,
        in_specs=[SMEM, SMEM, VMEM, VMEM] + [ANY] * (3 + len(pieces)) + ([VMEM, ANY, ANY] if prior else []),
        out_specs=out_specs,
        scratch_shapes=scratch,
        input_output_aliases={7 + len(pieces) + 2: 1} if prior else {},
        compiler_params=pltpu.CompilerParams(vmem_limit_bytes=60 * MIB),
        cost_estimate=pl.CostEstimate(flops=4 * slots * clip_rows * depth * cols, bytes_accessed=1, transcendentals=0),
        name="project",
    )(where, scalars, sums, mod, sample, other, scaled, *pieces, *earlier)


def outer_kernel(picks, mod, edge, flipped, inputs, *outs):
    del picks
    mods = [mod[i] for i in range(mod.shape[0])]
    for half, term in enumerate(gradient_halves(flipped, inputs, mods, edge)):
        for i, out in enumerate(outs[half::2]):

            @pl.when(pl.program_id(0) == i)
            def _():
                out[...] = term.astype(out.dtype)


def outer(picks, mod, edge, flipped, inputs, dtypes):
    cols, rows = flipped.shape
    count = len(picks)
    group = 2 if len(inputs.shape) == 2 else 1

    def spot(i, picks):
        return (picks[i], 0, 0)

    if group == 2:
        tokens = pl.BlockSpec((rows, 2 * cols), lambda i, picks: (0, picks[i]))
    else:
        tokens = pl.BlockSpec((2, rows, cols), spot)
    return pl.pallas_call(
        outer_kernel,
        out_shape=[jax.ShapeDtypeStruct((cols, cols), dtype) for dtype in dtypes],
        grid_spec=pltpu.PrefetchScalarGridSpec(
            num_scalar_prefetch=1,
            grid=(count,),
            in_specs=[
                pl.BlockSpec((2 // group, 2, group * cols), spot),
                pl.BlockSpec((cols, 2), lambda i, picks: (0, 0)),
                pl.BlockSpec((cols, rows), lambda i, picks: (0, 0)),
                tokens,
            ],
            out_specs=[pl.BlockSpec((cols, cols), lambda i, picks: (0, 0))] * (2 * count),
        ),
        compiler_params=pltpu.CompilerParams(vmem_limit_bytes=60 * MIB),
        cost_estimate=pl.CostEstimate(
            flops=4 * rows * cols * cols * count,
            bytes_accessed=4 * rows * cols * (count + 1) + 4 * cols * cols * count,
            transcendentals=0,
        ),
        name="outer",
    )(jnp.stack(picks).astype(jnp.int32), mod, edge, flipped, inputs)


def finish_kernel(terms, *refs):
    *parts, out = refs
    for half in range(2):
        total = parts[half * terms][...]
        for ref in parts[half * terms + 1 : (half + 1) * terms]:
            total += ref[...].astype(F32)
        out[half] = jnp.transpose(total)


def finish(halves):
    cols = halves[0][0].shape[0]
    lanes = 128 if cols % 128 == 0 else cols
    parts = [part for half in halves for part in half]
    return pl.pallas_call(
        functools.partial(finish_kernel, len(halves[0])),
        grid=(cols // lanes,),
        out_shape=jax.ShapeDtypeStruct((2, cols, cols), F32),
        in_specs=[pl.BlockSpec((cols, lanes), lambda i: (0, i))] * len(parts),
        out_specs=pl.BlockSpec((2, lanes, cols), lambda i: (0, i, 0)),
        compiler_params=pltpu.CompilerParams(vmem_limit_bytes=cols * cols * 16 + 8 * MIB),
        name="finish",
    )(*parts).reshape(2 * cols, cols)


def per_device(
    sample, noise, gen_branch, step, teacher_mod, fake_mod, teacher_weight, fake_weight, gen_gate
):
    clips = lax.axis_size("clip")
    shards = lax.axis_size("fsdp")
    clip = lax.axis_index("clip")
    shard = lax.axis_index("fsdp")
    clip_rows, cols = sample.shape
    width = cols * shards
    total_tokens = clip_rows * clips
    hops = shards // 2
    group = 1 if cols % 128 else 2
    rows = clip_rows // CHUNKS
    orders = clip_orders(clips)

    frac = step.astype(F32)[0] / 1000.0
    sigma = 5.0 * frac / (1.0 + 4.0 * frac)
    noised = ((1.0 - sigma) * sample.astype(F32) + sigma * noise.astype(F32)).astype(BF16)

    order = list(range(0, hops, 2)) + list(range(hops - 1 - hops % 2, 0, -2))
    ring = [
        (2 * order[i] + core, 2 * order[(i + 1) % hops] + core)
        for i in range(hops)
        for core in range(2)
    ]
    line = shard // 2
    rank = jnp.where(line % 2 == 0, line // 2, hops - 1 - line // 2)
    places = []
    for hop in range(hops):
        at = (rank + hops - hop) % hops
        places.append(jnp.where(2 * at < hops, 2 * at, 2 * (hops - 1 - at) + 1))
    swap = [(i, i ^ 1) for i in range(shards)]
    half_rows = fake_weight.shape[0] // 2
    far = [key for key in ((m, h) for m in range(clips) for h in range(2)) if key[0] & (key[0] - 1)]
    seen = {}

    def gated(name, value):
        names = [other for other in GATES.get(name, ()) if other in seen]
        return after(value, *(seen[other] for other in names))

    def hop_to(hop, i):
        name = "AB"[i] + str(hop)
        source = seen["AB"[i] + str(hop - 1)] if hop > 1 else noised[i * rows : (i + 1) * rows]
        seen[name] = lax.ppermute(gated(name, source), "fsdp", ring)

    def cross(hop, i):
        name = "AB"[i] + str(hop)
        seen["c" + name] = lax.ppermute(gated("c" + name, seen[name]), "fsdp", swap)

    fake_direct = neighbour_blocks(fake_weight, clips)
    for i, block in enumerate(fake_direct.values()):
        seen["f" + str(i)] = block
    for i in range(CHUNKS):
        hop_to(1, i)
    seen["own"] = lax.ppermute(noised, "fsdp", swap)
    for i in range(CHUNKS):
        cross(1, i)
    for i in range(CHUNKS):
        hop_to(2, i)
    parts = relay_parts({bit: gated("relay", block) for bit, block in fake_direct.items()}, half_rows)
    seen["parts"] = list(parts.values())[0]
    seen["parts1"] = list(parts.values())[-1]
    fake_blocks = relay_blocks(parts, clips)
    for mask, block in fake_direct.items():
        fake_blocks[mask, 0] = fake_blocks[mask, 1] = block
    seen["far0"], seen["far1"] = fake_blocks[far[0]], fake_blocks[far[1]]
    scalars = jnp.stack([sigma, jnp.float32(1.0 / math.sqrt(total_tokens))])
    owners = jnp.stack([clip ^ mask for mask in range(clips)]).astype(jnp.int32)
    where = jnp.stack(places + [shard % 2]).astype(jnp.int32)
    by_place = jnp.swapaxes(fake_mod[0].reshape(2, shards // group, group * cols), 0, 1)
    scaled, sums = scale(owners, fake_mod[0], fake_weight, fake_blocks)
    seen["sums"] = sums
    teacher_parts = {}
    own = gated("teacher", teacher_weight)
    own = [own[:half_rows], own[half_rows:]]
    for phase in range(len(orders[0][1])):
        for half, order in orders:
            block = swap_clip(gated("teacher" + str(min(phase, 1)), own[half]), order[phase], clips)
            teacher_parts[order[phase], half] = block
            seen["t" + str(phase) + str(half)] = block
    tokens = [([(noised, 0, 0), (seen["own"], 0, 1)], 0)]

    def add_hop(hop):
        pieces = []
        for i in range(CHUNKS):
            name = "AB"[i] + str(hop)
            pieces += [(seen[name], i * rows, 0), (seen["c" + name], i * rows, 1)]
        tokens.append((pieces, hop))

    add_hop(1)
    for hop in range(2, hops):
        for i in range(CHUNKS):
            if hop > 2:
                hop_to(hop, i)
            if hop < hops - 1:
                cross(hop, i)
        if hop < hops - 1:
            add_hop(hop)
    cut = max(1, hops - 2)
    done = project(
        where, scalars, sums, by_place, sample, noise, scaled, tokens[:cut], 0, (), hops, False
    )
    seen["soon"] = done[2]
    if cut < hops - 1:
        done = project(
            where, scalars, sums, by_place, sample, noise, scaled, tokens[cut:], 2 * cols * cut,
            done, hops, False,
        )
    seen["early"] = done[2]
    for key, block in teacher_parts.items():
        teacher_parts[key] = gated("teacher relay", block)
    teacher_blocks = relay_blocks(teacher_parts, clips)
    for i in range(CHUNKS):
        cross(hops - 1, i)
    add_hop(hops - 1)
    def going(mask):
        return [bool(mask & order[0]) for _, order in orders]

    ranks = [[m for m in range(clips) if sum(going(m)) == n] for n in (2, 1, 0)]
    where = jnp.concatenate([where, jnp.stack([clip ^ mask for mask in ranks[0]]).astype(jnp.int32)])
    fake_velocity, inputs, stats, flipped, edge, *blocks = project(
        where, scalars, sums, by_place, sample, noise, scaled, tokens[-1:], 2 * cols * (hops - 1),
        done, hops, True,
    )

    held = dict(zip([(mask, half) for mask in ranks[0] for half in range(2)], blocks))

    def terms(masks, left):
        dtypes = [BF16 if out else F32 for mask in masks for out in going(mask)]
        got = outer([clip ^ mask for mask in masks], by_place, edge, left, inputs, dtypes)
        held.update(zip([(mask, half) for mask in masks for half in range(2)], got))

    if ranks[1]:
        terms(ranks[1], after(flipped, *blocks))
    ready = list(held.values())
    halves, relayed = [], []
    sent = {key: swap_clip(held[key], orders[key[1]][1][0], clips) for key in held if going(key[0])[key[1]]}
    firsts = [sent[key] for key in sent if key[0] in ranks[0]]
    seconds = [sent[key] for key in sent if key[0] not in ranks[0]]
    terms(ranks[2], after(flipped, *firsts))
    for half, order in orders:
        mine = {mask: [block] for (mask, h), block in held.items() if h == half}
        for bit in order:
            for mask in [mask for mask in mine if mask & bit]:
                block = mine.pop(mask)
                if bit == order[0]:
                    got = sent[mask, half]
                else:
                    block = sum(part.astype(F32) for part in block).astype(BF16)
                    relayed.append(block)
                    got = swap_clip(block, bit, clips)
                mine[mask ^ bit].append(got)
        halves.append(mine[0])
    fake_grad = finish(halves)

    scaled, sums = scale(
        owners, teacher_mod[0], after(teacher_weight, *ready), teacher_blocks
    )
    left = after(inputs, *relayed)

    def add_place(p, total):
        tokens = lax.dynamic_index_in_dim(left, p, 0, keepdims=False)
        right = lax.dynamic_slice(scaled, (p * cols, 0), (cols, cols))
        return total + jnp.dot(tokens, right, preferred_element_type=F32)

    if group == 2:
        velocity = jnp.dot(left, scaled, preferred_element_type=F32)
    else:
        velocity = jnp.zeros((clip_rows, cols), F32)
        velocity = lax.fori_loop(0, width // cols, add_place, velocity)
    velocity = stats[:, 1:2] * (velocity - stats[:, 0:1] * sums[0, :1]) + sums[1, :1]
    apart = velocity - fake_velocity
    pulled = jnp.sum(apart * gen_branch.astype(F32), axis=0, keepdims=True)
    away = sample.astype(F32) - (noised.astype(F32) - sigma * velocity)
    away = after(jnp.sum(jnp.abs(away)).reshape(1, 1), *seconds)
    away = away + lax.ppermute(away, "fsdp", swap)
    away = away + sum(
        lax.ppermute(away, "fsdp", [(i, (i + 2 * k) % shards) for i in range(shards)])
        for k in range(1, hops)
    )
    factor = sigma / (away / (clip_rows * width) + EPS)
    branch_cot = (gen_gate * factor * apart).astype(BF16)
    gate_grad = pulled * factor / math.sqrt(clip_rows)
    return (branch_cot, gate_grad, fake_grad)


def solution(mesh):
    placed = (
        P("clip", "fsdp"),
        P("clip", "fsdp"),
        P("clip", "fsdp"),
        P("clip"),
        P("clip", None, None),
        P("clip", None, None),
        P("clip", "fsdp"),
        P("clip", "fsdp"),
        P("clip", "fsdp"),
    )
    return jax.shard_map(
        per_device,
        mesh=mesh,
        in_specs=placed,
        out_specs=(P("clip", "fsdp"), P("clip", "fsdp"), P("clip", "fsdp")),
        check_vma=False,
    )
```

```python
import functools
import math

import jax
import jax.numpy as jnp
from jax import lax
from jax.experimental import pallas as pl
from jax.experimental.pallas import tpu as pltpu
from jax.sharding import PartitionSpec as P

EPS = 1e-06
BF16 = jnp.bfloat16
F32 = jnp.float32
MIB = 1024 * 1024
CHUNKS = 2
GATES = {
    "relay": ("own",),
    "teacher": ("parts", "parts1"),
    "A3": ("far0", "far1"),
    "B2": ("A2",),
    "B3": ("sums", "t00", "t01"),
    "cB1": ("far0", "far1"),
    "cA2": ("sums",),
    "cB2": ("far0", "far1"),
    "cA3": ("soon",),
    "cB3": ("early", "t10", "t11"),
    "teacher relay": ("sums",),
}
ANY = pl.BlockSpec(memory_space=pl.ANY)
SMEM = pl.BlockSpec(memory_space=pltpu.SMEM)
VMEM = pl.BlockSpec(memory_space=pltpu.VMEM)


def after(value, *earlier):
    return lax.optimization_barrier((value, *earlier))[0]


def swap_clip(value, bit, count):
    return lax.ppermute(value, "clip", [(i, i ^ bit) for i in range(count)])


def clip_orders(count):
    bits = [1 << i for i in range(count.bit_length() - 1)]
    return ((0, bits), (1, bits[::-1]))


def neighbour_blocks(weight, count):
    return {bit: swap_clip(weight, bit, count) for bit in clip_orders(count)[0][1]}


def relay_parts(direct, rows):
    parts = {}
    for half in range(2):
        for bit, block in direct.items():
            parts[bit, half] = block[half * rows : (half + 1) * rows]
    return parts


def relay_blocks(parts, count):
    pieces = {}
    for half, order in clip_orders(count):
        held = {}
        for bit in order:
            for mask in list(held):
                held[mask ^ bit] = swap_clip(held[mask], bit, count)
            held[bit] = parts[bit, half]
        for mask, block in held.items():
            pieces[mask, half] = block
    return pieces


def scale_kernel(keys, where, mod, weight, *refs):
    blocks, refs = refs[: len(keys)], refs[len(keys) :]
    out, sums, full, column, sems, osems = refs
    half_rows = weight.shape[0] // 2
    cols = weight.shape[1]
    loads, drains = [], []
    for index, (mask, half) in enumerate([(0, 0), (0, 1)] + keys):
        ref = weight if mask == 0 else blocks[index - 2]
        source = ref.at[pl.ds(half * half_rows, half_rows)] if ref.shape[0] > half_rows else ref
        spot = pl.multiple_of((where[mask] * 2 + half) * half_rows, half_rows)
        at = pl.ds(spot, half_rows)
        loads.append((pltpu.make_async_copy(source, full.at[at], sems.at[index]), spot))
        drains.append(pltpu.make_async_copy(full.at[at], out.at[at], osems.at[index]))
        loads[-1][0].start()
    sums[...] = jnp.zeros_like(sums)
    tile = half_rows // 2
    for index, ((load, spot), drain) in enumerate(zip(loads, drains)):
        mask, half = ([(0, 0), (0, 1)] + keys)[index]
        column[...] = jnp.transpose(mod[where[mask] * 2 + half])
        load.wait()
        for low in range(0, half_rows, tile):
            at = pl.ds(pl.multiple_of(spot + low, tile), tile)
            value = full[at, :].astype(F32)
            shifted = value * column[low : low + tile, 0:1]
            scaled = (value * (1.0 + column[low : low + tile, 1:2])).astype(BF16)
            full[at, :] = scaled
            sums[0] += jnp.sum(scaled.astype(F32).reshape(tile // 8, 8, cols), axis=0)
            sums[1] += jnp.sum(shifted.reshape(tile // 8, 8, cols), axis=0)
        drain.start()
    for i in range(2):
        sums[i] = jnp.broadcast_to(jnp.sum(sums[i], axis=0, keepdims=True), (8, cols))
    for drain in drains:
        drain.wait()


def scale(where, mod, weight, blocks):
    cols = weight.shape[1]
    half_rows = weight.shape[0] // 2
    mod = jnp.swapaxes(mod.reshape(2, -1, half_rows), 0, 1)
    count = len(blocks) + 2
    width = half_rows * count
    return pl.pallas_call(
        functools.partial(scale_kernel, list(blocks)),
        out_shape=(
            jax.ShapeDtypeStruct((width, cols), BF16),
            jax.ShapeDtypeStruct((2, 8, cols), F32),
        ),
        in_specs=[SMEM, VMEM] + [ANY] * (1 + len(blocks)),
        out_specs=(ANY, VMEM),
        scratch_shapes=[
            pltpu.VMEM((width, cols), BF16),
            pltpu.VMEM((half_rows, 2), F32),
            pltpu.SemaphoreType.DMA((count,)),
            pltpu.SemaphoreType.DMA((count,)),
        ],
        compiler_params=pltpu.CompilerParams(vmem_limit_bytes=60 * MIB),
        cost_estimate=pl.CostEstimate(
            flops=1, bytes_accessed=1, transcendentals=0
        ),
        name="scale",
    )(where, mod, weight, *blocks.values())


def gradient_halves(flipped, tokens, mod, edge):
    cols = flipped.shape[0]
    if len(tokens.shape) == 2:
        term = jnp.dot(flipped[...], tokens[...], preferred_element_type=F32)
        terms = [term[:, half * cols : (half + 1) * cols] for half in range(2)]
        mods = [mod[0][:, half * cols : (half + 1) * cols] for half in range(2)]
    else:
        terms = [jnp.dot(flipped[...], tokens[h], preferred_element_type=F32) for h in range(2)]
        mods = mod
    return [
        (term - edge[:, 0:1]) * (1.0 + part[1:2, :]) + edge[:, 1:2] * part[0:1, :]
        for term, part in zip(terms, mods)
    ]


def project_kernel(
    prior, last, hops, core_at, where, scalars, sums, mod, sample, other, scaled, *refs
):
    count = sum(len(hop) for hop in hops)
    pieces, refs = refs[:count], refs[count:]
    if prior:
        carried, carry, _, *refs = refs
    velocity, inputs, stats, *refs = refs
    if last:
        fars = where.shape[0] - core_at - 1
        flipped, edge, *refs = refs
        blocks, refs = refs[: 2 * fars], refs[2 * fars :]
    held, full, moments, total, sems, wsems, osems, esems, *refs = refs
    if prior:
        before, *refs = refs
    if last:
        tail, mine, noisy, turned, far = refs
    slots, rows, depth = held.shape
    cols = total.shape[1]
    width = scaled.shape[0]
    parts = 2 * cols // depth
    core = where[core_at]
    span = 2 * cols

    def at_place(place):
        if parts == 1:
            return inputs.at[:, pl.ds(pl.multiple_of(place * span, span), span)]
        return inputs.at[pl.ds(place * 2, 2)]

    loads, arrivals, drains = [], [], []
    index = 0
    for n, hop in enumerate(hops):
        copies = []
        for low, side, place in hop:
            owner = core if side == 0 else 1 - core
            ref = pieces[index]
            at = pl.ds(low, ref.shape[0])
            if parts == 1:
                lanes = pl.ds(pl.multiple_of(owner * cols, cols), cols)
                spot = held.at[n, at, lanes]
            else:
                spot = held.at[2 * n + owner, at]
            copies.append(pltpu.make_async_copy(ref, spot, sems.at[index]))
            index += 1
        arrivals.append(copies)
        place = where[hop[0][2]]
        low = pl.multiple_of(place * span, span)
        loads.append(pltpu.make_async_copy(scaled.at[pl.ds(low, span)], full.at[n], wsems.at[n]))
        here = held.at[n] if parts == 1 else held.at[pl.ds(2 * n, 2)]
        drains.append(pltpu.make_async_copy(here, at_place(place), osems.at[n]))
    for copies, load in zip(arrivals, loads):
        for copy in copies:
            copy.start()
        load.start()
    extras = []

    def extra(source, target):
        extras.append(pltpu.make_async_copy(source, target, esems.at[len(extras)]))
        extras[-1].start()
        return extras[-1]

    waits = []
    if prior:
        waits.append(extra(carry, before))
    if last:
        waits += [extra(sample, mine), extra(other, noisy)]
    piece = 256
    lane = lax.broadcasted_iota(jnp.int32, (piece, 128), 1)
    for n in range(len(hops)):
        for copy in arrivals[n]:
            copy.wait()
        drains[n].start()
        loads[n].wait()
        for part in range(parts):
            slot = n * parts + part
            term = jnp.dot(
                held[slot], full[n, pl.ds(part * depth, depth), :], preferred_element_type=F32
            )
            if slot:
                total[...] += term
            else:
                total[...] = term
            for low in range(0, rows, piece):
                at = pl.ds(low, piece)
                if slot == 0 and prior:
                    moments[at, :] = carried[at, :]
                elif slot == 0:
                    near = held[0, at, :128].astype(F32)
                    near = jnp.sum(near, axis=1, keepdims=True) * (1.0 / 128)
                    moments[at, :] = jnp.where(lane == 0, near, 0.0)
                spread = held[slot, at, :].astype(F32) - moments[at, 0:1]
                sum_ = jnp.sum(spread, axis=1, keepdims=True)
                power = jnp.sum(spread * spread, axis=1, keepdims=True)
                more = jnp.where(lane == 1, sum_, jnp.where(lane == 2, power, 0.0))
                moments[at, :] += more
    for copy in waits:
        copy.wait()
    if not last:
        stats[...] = moments[...]
        if prior:
            total[...] += before[...]
        outs = [extra(total, velocity)]
    else:
        for copy in drains:
            copy.wait()
        nears = [extra(at_place(where[core_at + 1 + j]), far.at[j]) for j in range(fars)]
        tail[...] = jnp.zeros_like(tail)

        @pl.loop(0, rows // piece)
        def _(step):
            low = pl.multiple_of(step * piece, piece)
            at = pl.ds(low, piece)
            away = moments[at, 1:2] * (1.0 / width)
            power = jnp.maximum(moments[at, 2:3] * (1.0 / width) - away * away, 0.0)
            mean = moments[at, 0:1] + away
            by = lax.rsqrt(power + EPS)
            stats[at, :] = jnp.where(lane == 0, mean, by)
            value = total[at, :] + before[at, :]
            value = by * (value - mean * sums[0, 0:1, :]) + sums[1, 0:1, :]
            total[at, :] = value
            target = noisy[at, :].astype(F32) - mine[at, :].astype(F32)
            wrong = (value - target) * scalars[1]
            sent = (by * wrong).astype(BF16).astype(F32)
            turned[:, at] = jnp.transpose(sent).astype(BF16)
            tail[0] += jnp.sum((mean * sent).reshape(piece // 8, 8, cols), axis=0)
            tail[1] += jnp.sum(wrong.reshape(piece // 8, 8, cols), axis=0)

        outs = [extra(turned, flipped), extra(total, velocity)]
        ends = [jnp.sum(jnp.transpose(tail[i]), axis=1, keepdims=True) for i in range(2)]
        edge[...] = jnp.concatenate(ends, axis=1)
        for j in range(fars):
            nears[j].wait()
            place = where[core_at + 1 + j]
            mods = [mod[place]] if parts == 1 else [mod[2 * place], mod[2 * place + 1]]
            for half, term in enumerate(gradient_halves(turned, far.at[j], mods, edge)):
                blocks[2 * j + half][...] = term.astype(BF16)
    for copy in outs + ([] if last else drains):
        copy.wait()


def project(where, scalars, sums, mod, sample, other, scaled, hops, prior, earlier, core_at, last):
    clip_rows, cols = sample.shape
    width = scaled.shape[0]
    group = 1 if cols % 128 else 2
    depth = group * cols
    slots = len(hops) * 2 // group
    pieces = [piece for hop, _ in hops for piece, _, _ in hop]
    plan = [[(low, side, place) for _, low, side in hop] for hop, place in hops]
    laid = (clip_rows, width) if group == 2 else (width // cols, clip_rows, cols)
    near = (clip_rows, depth) if group == 2 else (2, clip_rows, cols)
    fars = where.shape[0] - core_at - 1
    out_shape = [
        jax.ShapeDtypeStruct((clip_rows, cols), F32),
        jax.ShapeDtypeStruct(laid, BF16),
        jax.ShapeDtypeStruct((clip_rows, 128), F32),
    ]
    out_specs = [ANY, ANY, VMEM]
    scratch = [
        pltpu.VMEM((slots, clip_rows, depth), BF16),
        pltpu.VMEM((len(hops), 2 * cols, cols), BF16),
        pltpu.VMEM((clip_rows, 128), F32),
        pltpu.VMEM((clip_rows, cols), F32),
        pltpu.SemaphoreType.DMA((len(pieces),)),
        pltpu.SemaphoreType.DMA((len(hops),)),
        pltpu.SemaphoreType.DMA((len(hops),)),
        pltpu.SemaphoreType.DMA((5 + fars,)),
    ]
    if prior:
        velocity, inputs, stats = earlier
        earlier = [stats, velocity, inputs]
        scratch.append(pltpu.VMEM((clip_rows, cols), F32))
    if last:
        out_shape.append(jax.ShapeDtypeStruct((cols, clip_rows), BF16))
        out_shape.append(jax.ShapeDtypeStruct((cols, 2), F32))
        out_shape += [jax.ShapeDtypeStruct((cols, cols), BF16)] * (2 * fars)
        out_specs += [ANY, VMEM] + [VMEM] * (2 * fars)
        scratch += [
            pltpu.VMEM((2, 8, cols), F32),
            pltpu.VMEM((clip_rows, cols), BF16),
            pltpu.VMEM((clip_rows, cols), BF16),
            pltpu.VMEM((cols, clip_rows), BF16),
            pltpu.VMEM((fars, *near), BF16),
        ]
    return pl.pallas_call(
        functools.partial(project_kernel, prior, last, plan, core_at),
        out_shape=out_shape,
        in_specs=[SMEM, SMEM, VMEM, VMEM] + [ANY] * (3 + len(pieces)) + ([VMEM, ANY, ANY] if prior else []),
        out_specs=out_specs,
        scratch_shapes=scratch,
        input_output_aliases={7 + len(pieces) + 2: 1} if prior else {},
        compiler_params=pltpu.CompilerParams(vmem_limit_bytes=60 * MIB),
        cost_estimate=pl.CostEstimate(flops=4 * slots * clip_rows * depth * cols, bytes_accessed=1, transcendentals=0),
        name="project",
    )(where, scalars, sums, mod, sample, other, scaled, *pieces, *earlier)


def outer_kernel(picks, mod, edge, flipped, inputs, *outs):
    del picks
    mods = [mod[i] for i in range(mod.shape[0])]
    for half, term in enumerate(gradient_halves(flipped, inputs, mods, edge)):
        for i, out in enumerate(outs[half::2]):

            @pl.when(pl.program_id(0) == i)
            def _():
                out[...] = term.astype(out.dtype)


def outer(picks, mod, edge, flipped, inputs, dtypes):
    cols, rows = flipped.shape
    count = len(picks)
    group = 2 if len(inputs.shape) == 2 else 1

    def spot(i, picks):
        return (picks[i], 0, 0)

    if group == 2:
        tokens = pl.BlockSpec((rows, 2 * cols), lambda i, picks: (0, picks[i]))
    else:
        tokens = pl.BlockSpec((2, rows, cols), spot)
    return pl.pallas_call(
        outer_kernel,
        out_shape=[jax.ShapeDtypeStruct((cols, cols), dtype) for dtype in dtypes],
        grid_spec=pltpu.PrefetchScalarGridSpec(
            num_scalar_prefetch=1,
            grid=(count,),
            in_specs=[
                pl.BlockSpec((2 // group, 2, group * cols), spot),
                pl.BlockSpec((cols, 2), lambda i, picks: (0, 0)),
                pl.BlockSpec((cols, rows), lambda i, picks: (0, 0)),
                tokens,
            ],
            out_specs=[pl.BlockSpec((cols, cols), lambda i, picks: (0, 0))] * (2 * count),
        ),
        compiler_params=pltpu.CompilerParams(vmem_limit_bytes=60 * MIB),
        cost_estimate=pl.CostEstimate(
            flops=4 * rows * cols * cols * count,
            bytes_accessed=4 * rows * cols * (count + 1) + 4 * cols * cols * count,
            transcendentals=0,
        ),
        name="outer",
    )(jnp.stack(picks).astype(jnp.int32), mod, edge, flipped, inputs)


def finish_kernel(terms, *refs):
    *parts, out = refs
    for half in range(2):
        total = parts[half * terms][...]
        for ref in parts[half * terms + 1 : (half + 1) * terms]:
            total += ref[...].astype(F32)
        out[half] = jnp.transpose(total)


def finish(halves):
    cols = halves[0][0].shape[0]
    lanes = 128 if cols % 128 == 0 else cols
    parts = [part for half in halves for part in half]
    return pl.pallas_call(
        functools.partial(finish_kernel, len(halves[0])),
        grid=(cols // lanes,),
        out_shape=jax.ShapeDtypeStruct((2, cols, cols), F32),
        in_specs=[pl.BlockSpec((cols, lanes), lambda i: (0, i))] * len(parts),
        out_specs=pl.BlockSpec((2, lanes, cols), lambda i: (0, i, 0)),
        compiler_params=pltpu.CompilerParams(vmem_limit_bytes=cols * cols * 16 + 8 * MIB),
        name="finish",
    )(*parts).reshape(2 * cols, cols)


def per_device(
    sample, noise, gen_branch, step, teacher_mod, fake_mod, teacher_weight, fake_weight, gen_gate
):
    clips = lax.axis_size("clip")
    shards = lax.axis_size("fsdp")
    clip = lax.axis_index("clip")
    shard = lax.axis_index("fsdp")
    clip_rows, cols = sample.shape
    width = cols * shards
    total_tokens = clip_rows * clips
    hops = shards // 2
    group = 1 if cols % 128 else 2
    rows = clip_rows // CHUNKS
    orders = clip_orders(clips)

    frac = step.astype(F32)[0] / 1000.0
    sigma = 5.0 * frac / (1.0 + 4.0 * frac)
    noised = ((1.0 - sigma) * sample.astype(F32) + sigma * noise.astype(F32)).astype(BF16)

    order = list(range(0, hops, 2)) + list(range(hops - 1 - hops % 2, 0, -2))
    ring = [
        (2 * order[i] + core, 2 * order[(i + 1) % hops] + core)
        for i in range(hops)
        for core in range(2)
    ]
    line = shard // 2
    rank = jnp.where(line % 2 == 0, line // 2, hops - 1 - line // 2)
    places = []
    for hop in range(hops):
        at = (rank + hops - hop) % hops
        places.append(jnp.where(2 * at < hops, 2 * at, 2 * (hops - 1 - at) + 1))
    swap = [(i, i ^ 1) for i in range(shards)]
    half_rows = fake_weight.shape[0] // 2
    far = [key for key in ((m, h) for m in range(clips) for h in range(2)) if key[0] & (key[0] - 1)]
    seen = {}

    def gated(name, value):
        names = [other for other in GATES.get(name, ()) if other in seen]
        return after(value, *(seen[other] for other in names))

    def hop_to(hop, i):
        name = "AB"[i] + str(hop)
        source = seen["AB"[i] + str(hop - 1)] if hop > 1 else noised[i * rows : (i + 1) * rows]
        seen[name] = lax.ppermute(gated(name, source), "fsdp", ring)

    def cross(hop, i):
        name = "AB"[i] + str(hop)
        seen["c" + name] = lax.ppermute(gated("c" + name, seen[name]), "fsdp", swap)

    fake_direct = neighbour_blocks(fake_weight, clips)
    for i, block in enumerate(fake_direct.values()):
        seen["f" + str(i)] = block
    for i in range(CHUNKS):
        hop_to(1, i)
    seen["own"] = lax.ppermute(noised, "fsdp", swap)
    for i in range(CHUNKS):
        cross(1, i)
    for i in range(CHUNKS):
        hop_to(2, i)
    parts = relay_parts({bit: gated("relay", block) for bit, block in fake_direct.items()}, half_rows)
    seen["parts"] = list(parts.values())[0]
    seen["parts1"] = list(parts.values())[-1]
    fake_blocks = relay_blocks(parts, clips)
    for mask, block in fake_direct.items():
        fake_blocks[mask, 0] = fake_blocks[mask, 1] = block
    seen["far0"], seen["far1"] = fake_blocks[far[0]], fake_blocks[far[1]]
    scalars = jnp.stack([sigma, jnp.float32(1.0 / math.sqrt(total_tokens))])
    owners = jnp.stack([clip ^ mask for mask in range(clips)]).astype(jnp.int32)
    where = jnp.stack(places + [shard % 2]).astype(jnp.int32)
    by_place = jnp.swapaxes(fake_mod[0].reshape(2, shards // group, group * cols), 0, 1)
    scaled, sums = scale(owners, fake_mod[0], fake_weight, fake_blocks)
    seen["sums"] = sums
    teacher_parts = {}
    own = gated("teacher", teacher_weight)
    own = [own[:half_rows], own[half_rows:]]
    for phase in range(len(orders[0][1])):
        for half, order in orders:
            block = swap_clip(gated("teacher" + str(min(phase, 1)), own[half]), order[phase], clips)
            teacher_parts[order[phase], half] = block
            seen["t" + str(phase) + str(half)] = block
    tokens = [([(noised, 0, 0), (seen["own"], 0, 1)], 0)]

    def add_hop(hop):
        pieces = []
        for i in range(CHUNKS):
            name = "AB"[i] + str(hop)
            pieces += [(seen[name], i * rows, 0), (seen["c" + name], i * rows, 1)]
        tokens.append((pieces, hop))

    add_hop(1)
    for hop in range(2, hops):
        for i in range(CHUNKS):
            if hop > 2:
                hop_to(hop, i)
            if hop < hops - 1:
                cross(hop, i)
        if hop < hops - 1:
            add_hop(hop)
    cut = max(1, hops - 2)
    done = project(
        where, scalars, sums, by_place, sample, noise, scaled, tokens[:cut], 0, (), hops, False
    )
    seen["soon"] = done[2]
    if cut < hops - 1:
        done = project(
            where, scalars, sums, by_place, sample, noise, scaled, tokens[cut:], 2 * cols * cut,
            done, hops, False,
        )
    seen["early"] = done[2]
    for key, block in teacher_parts.items():
        teacher_parts[key] = gated("teacher relay", block)
    teacher_blocks = relay_blocks(teacher_parts, clips)
    for i in range(CHUNKS):
        cross(hops - 1, i)
    add_hop(hops - 1)
    def going(mask):
        return [bool(mask & order[0]) for _, order in orders]

    ranks = [[m for m in range(clips) if sum(going(m)) == n] for n in (2, 1, 0)]
    where = jnp.concatenate([where, jnp.stack([clip ^ mask for mask in ranks[0]]).astype(jnp.int32)])
    fake_velocity, inputs, stats, flipped, edge, *blocks = project(
        where, scalars, sums, by_place, sample, noise, scaled, tokens[-1:], 2 * cols * (hops - 1),
        done, hops, True,
    )

    held = dict(zip([(mask, half) for mask in ranks[0] for half in range(2)], blocks))

    def terms(masks, left):
        dtypes = [BF16 if out else F32 for mask in masks for out in going(mask)]
        got = outer([clip ^ mask for mask in masks], by_place, edge, left, inputs, dtypes)
        held.update(zip([(mask, half) for mask in masks for half in range(2)], got))

    if ranks[1]:
        terms(ranks[1], after(flipped, *blocks))
    ready = list(held.values())
    halves, relayed = [], []
    sent = {key: swap_clip(held[key], orders[key[1]][1][0], clips) for key in held if going(key[0])[key[1]]}
    firsts = [sent[key] for key in sent if key[0] in ranks[0]]
    seconds = [sent[key] for key in sent if key[0] not in ranks[0]]
    terms(ranks[2], after(flipped, *firsts))
    for half, order in orders:
        mine = {mask: [block] for (mask, h), block in held.items() if h == half}
        for bit in order:
            for mask in [mask for mask in mine if mask & bit]:
                block = mine.pop(mask)
                if bit == order[0]:
                    got = sent[mask, half]
                else:
                    block = sum(part.astype(F32) for part in block).astype(BF16)
                    relayed.append(block)
                    got = swap_clip(block, bit, clips)
                mine[mask ^ bit].append(got)
        halves.append(mine[0])
    fake_grad = finish(halves)

    scaled, sums = scale(
        owners, teacher_mod[0], after(teacher_weight, *ready), teacher_blocks
    )
    left = after(inputs, *relayed)

    def add_place(p, total):
        tokens = lax.dynamic_index_in_dim(left, p, 0, keepdims=False)
        right = lax.dynamic_slice(scaled, (p * cols, 0), (cols, cols))
        return total + jnp.dot(tokens, right, preferred_element_type=F32)

    if group == 2:
        velocity = jnp.dot(left, scaled, preferred_element_type=F32)
    else:
        velocity = jnp.zeros((clip_rows, cols), F32)
        velocity = lax.fori_loop(0, width // cols, add_place, velocity)
    velocity = stats[:, 1:2] * (velocity - stats[:, 0:1] * sums[0, :1]) + sums[1, :1]
    apart = velocity - fake_velocity
    pulled = jnp.sum(apart * gen_branch.astype(F32), axis=0, keepdims=True)
    away = sample.astype(F32) - (noised.astype(F32) - sigma * velocity)
    away = after(jnp.sum(jnp.abs(away)).reshape(1, 1), *seconds)
    bit = 1
    while bit < shards:
        if bit == 2:
            away = after(away, fake_grad)
        away = away + lax.ppermute(away, "fsdp", [(i, i ^ bit) for i in range(shards)])
        bit *= 2
    factor = sigma / (away / (clip_rows * width) + EPS)
    branch_cot = (gen_gate * factor * apart).astype(BF16)
    gate_grad = pulled * factor / math.sqrt(clip_rows)
    return (branch_cot, gate_grad, fake_grad)


def solution(mesh):
    placed = (
        P("clip", "fsdp"),
        P("clip", "fsdp"),
        P("clip", "fsdp"),
        P("clip"),
        P("clip", None, None),
        P("clip", None, None),
        P("clip", "fsdp"),
        P("clip", "fsdp"),
        P("clip", "fsdp"),
    )
    return jax.shard_map(
        per_device,
        mesh=mesh,
        in_specs=placed,
        out_specs=(P("clip", "fsdp"), P("clip", "fsdp"), P("clip", "fsdp")),
        check_vma=False,
    )
```

```python
import functools
import math

import jax
import jax.numpy as jnp
from jax import lax
from jax.experimental import pallas as pl
from jax.experimental.pallas import tpu as pltpu
from jax.sharding import PartitionSpec as P

EPS = 1e-06
BF16 = jnp.bfloat16
F32 = jnp.float32
MIB = 1024 * 1024
CHUNKS = 2
GATES = {
    "relay": ("own",),
    "teacher": ("parts", "parts1"),
    "B2": ("A2",),
    "cB2": ("far0", "far1"),
    "cA3": ("soon",),
    "teacher relay": ("sums",),
    "cA2": ("sums",),
    "cB1": ("far0", "far1"),
    "B3": ("sums",),
    "cB3": ("early", "t10", "t11"),
    "A3": ("far0", "far1"),
}
ANY = pl.BlockSpec(memory_space=pl.ANY)
SMEM = pl.BlockSpec(memory_space=pltpu.SMEM)
VMEM = pl.BlockSpec(memory_space=pltpu.VMEM)


def after(value, *earlier):
    return lax.optimization_barrier((value, *earlier))[0]


def swap_clip(value, bit, count):
    return lax.ppermute(value, "clip", [(i, i ^ bit) for i in range(count)])


def clip_orders(count):
    bits = [1 << i for i in range(count.bit_length() - 1)]
    return ((0, bits), (1, bits[::-1]))


def neighbour_blocks(weight, count):
    return {bit: swap_clip(weight, bit, count) for bit in clip_orders(count)[0][1]}


def relay_parts(direct, rows):
    parts = {}
    for half in range(2):
        for bit, block in direct.items():
            parts[bit, half] = block[half * rows : (half + 1) * rows]
    return parts


def relay_blocks(parts, count):
    pieces = {}
    for half, order in clip_orders(count):
        held = {}
        for bit in order:
            for mask in list(held):
                held[mask ^ bit] = swap_clip(held[mask], bit, count)
            held[bit] = parts[bit, half]
        for mask, block in held.items():
            pieces[mask, half] = block
    return pieces


def scale_kernel(keys, where, mod, weight, *refs):
    blocks, refs = refs[: len(keys)], refs[len(keys) :]
    out, sums, full, column, sems, osems = refs
    half_rows = weight.shape[0] // 2
    cols = weight.shape[1]
    loads, drains = [], []
    for index, (mask, half) in enumerate([(0, 0), (0, 1)] + keys):
        ref = weight if mask == 0 else blocks[index - 2]
        source = ref.at[pl.ds(half * half_rows, half_rows)] if ref.shape[0] > half_rows else ref
        spot = pl.multiple_of((where[mask] * 2 + half) * half_rows, half_rows)
        at = pl.ds(spot, half_rows)
        loads.append((pltpu.make_async_copy(source, full.at[at], sems.at[index]), spot))
        drains.append(pltpu.make_async_copy(full.at[at], out.at[at], osems.at[index]))
        loads[-1][0].start()
    sums[...] = jnp.zeros_like(sums)
    tile = half_rows // 2
    for index, ((load, spot), drain) in enumerate(zip(loads, drains)):
        mask, half = ([(0, 0), (0, 1)] + keys)[index]
        column[...] = jnp.transpose(mod[where[mask] * 2 + half])
        load.wait()
        for low in range(0, half_rows, tile):
            at = pl.ds(pl.multiple_of(spot + low, tile), tile)
            value = full[at, :].astype(F32)
            shifted = value * column[low : low + tile, 0:1]
            scaled = (value * (1.0 + column[low : low + tile, 1:2])).astype(BF16)
            full[at, :] = scaled
            sums[0] += jnp.sum(scaled.astype(F32).reshape(tile // 8, 8, cols), axis=0)
            sums[1] += jnp.sum(shifted.reshape(tile // 8, 8, cols), axis=0)
        drain.start()
    for i in range(2):
        sums[i] = jnp.broadcast_to(jnp.sum(sums[i], axis=0, keepdims=True), (8, cols))
    for drain in drains:
        drain.wait()


def scale(where, mod, weight, blocks):
    cols = weight.shape[1]
    half_rows = weight.shape[0] // 2
    mod = jnp.swapaxes(mod.reshape(2, -1, half_rows), 0, 1)
    count = len(blocks) + 2
    width = half_rows * count
    return pl.pallas_call(
        functools.partial(scale_kernel, list(blocks)),
        out_shape=(
            jax.ShapeDtypeStruct((width, cols), BF16),
            jax.ShapeDtypeStruct((2, 8, cols), F32),
        ),
        in_specs=[SMEM, VMEM] + [ANY] * (1 + len(blocks)),
        out_specs=(ANY, VMEM),
        scratch_shapes=[
            pltpu.VMEM((width, cols), BF16),
            pltpu.VMEM((half_rows, 2), F32),
            pltpu.SemaphoreType.DMA((count,)),
            pltpu.SemaphoreType.DMA((count,)),
        ],
        compiler_params=pltpu.CompilerParams(vmem_limit_bytes=60 * MIB),
        cost_estimate=pl.CostEstimate(
            flops=2700 * width * cols, bytes_accessed=7 * width * cols, transcendentals=0
        ),
        name="scale",
    )(where, mod, weight, *blocks.values())


def gradient_halves(flipped, tokens, mod, edge):
    cols = flipped.shape[0]
    if len(tokens.shape) == 2:
        term = jnp.dot(flipped[...], tokens[...], preferred_element_type=F32)
        terms = [term[:, half * cols : (half + 1) * cols] for half in range(2)]
        mods = [mod[0][:, half * cols : (half + 1) * cols] for half in range(2)]
    else:
        terms = [jnp.dot(flipped[...], tokens[h], preferred_element_type=F32) for h in range(2)]
        mods = mod
    return [
        (term - edge[:, 0:1]) * (1.0 + part[1:2, :]) + edge[:, 1:2] * part[0:1, :]
        for term, part in zip(terms, mods)
    ]


def project_kernel(
    prior, last, hops, core_at, where, scalars, sums, mod, sample, other, scaled, *refs
):
    count = sum(len(hop) for hop in hops)
    pieces, refs = refs[:count], refs[count:]
    if prior:
        carried, carry, _, *refs = refs
    velocity, inputs, stats, *refs = refs
    if last:
        fars = where.shape[0] - core_at - 1
        flipped, edge, *refs = refs
        blocks, refs = refs[: 2 * fars], refs[2 * fars :]
    held, full, moments, total, sems, wsems, osems, esems, *refs = refs
    if prior:
        before, *refs = refs
    if last:
        tail, mine, noisy, turned, far = refs
    slots, rows, depth = held.shape
    cols = total.shape[1]
    width = scaled.shape[0]
    parts = 2 * cols // depth
    core = where[core_at]
    span = 2 * cols

    def at_place(place):
        if parts == 1:
            return inputs.at[:, pl.ds(pl.multiple_of(place * span, span), span)]
        return inputs.at[pl.ds(place * 2, 2)]

    loads, arrivals, drains = [], [], []
    index = 0
    for n, hop in enumerate(hops):
        copies = []
        for low, side, place in hop:
            owner = core if side == 0 else 1 - core
            ref = pieces[index]
            at = pl.ds(low, ref.shape[0])
            if parts == 1:
                lanes = pl.ds(pl.multiple_of(owner * cols, cols), cols)
                spot = held.at[n, at, lanes]
            else:
                spot = held.at[2 * n + owner, at]
            copies.append(pltpu.make_async_copy(ref, spot, sems.at[index]))
            index += 1
        arrivals.append(copies)
        place = where[hop[0][2]]
        low = pl.multiple_of(place * span, span)
        loads.append(pltpu.make_async_copy(scaled.at[pl.ds(low, span)], full.at[n], wsems.at[n]))
        here = held.at[n] if parts == 1 else held.at[pl.ds(2 * n, 2)]
        drains.append(pltpu.make_async_copy(here, at_place(place), osems.at[n]))
    for copies, load in zip(arrivals, loads):
        for copy in copies:
            copy.start()
        load.start()
    extras = []

    def extra(source, target):
        extras.append(pltpu.make_async_copy(source, target, esems.at[len(extras)]))
        extras[-1].start()
        return extras[-1]

    waits = []
    if prior:
        waits.append(extra(carry, before))
    if last:
        waits += [extra(sample, mine), extra(other, noisy)]
    piece = 256
    lane = lax.broadcasted_iota(jnp.int32, (piece, 128), 1)
    for n in range(len(hops)):
        for copy in arrivals[n]:
            copy.wait()
        drains[n].start()
        loads[n].wait()
        for part in range(parts):
            slot = n * parts + part
            term = jnp.dot(
                held[slot], full[n, pl.ds(part * depth, depth), :], preferred_element_type=F32
            )
            if slot:
                total[...] += term
            else:
                total[...] = term
            for low in range(0, rows, piece):
                at = pl.ds(low, piece)
                if slot == 0 and prior:
                    moments[at, :] = carried[at, :]
                elif slot == 0:
                    near = held[0, at, :128].astype(F32)
                    near = jnp.sum(near, axis=1, keepdims=True) * (1.0 / 128)
                    moments[at, :] = jnp.where(lane == 0, near, 0.0)
                spread = held[slot, at, :].astype(F32) - moments[at, 0:1]
                sum_ = jnp.sum(spread, axis=1, keepdims=True)
                power = jnp.sum(spread * spread, axis=1, keepdims=True)
                more = jnp.where(lane == 1, sum_, jnp.where(lane == 2, power, 0.0))
                moments[at, :] += more
    for copy in waits:
        copy.wait()
    if not last:
        stats[...] = moments[...]
        if prior:
            total[...] += before[...]
        outs = [extra(total, velocity)]
    else:
        for copy in drains:
            copy.wait()
        nears = [extra(at_place(where[core_at + 1 + j]), far.at[j]) for j in range(fars)]
        tail[...] = jnp.zeros_like(tail)

        @pl.loop(0, rows // piece)
        def _(step):
            low = pl.multiple_of(step * piece, piece)
            at = pl.ds(low, piece)
            away = moments[at, 1:2] * (1.0 / width)
            power = jnp.maximum(moments[at, 2:3] * (1.0 / width) - away * away, 0.0)
            mean = moments[at, 0:1] + away
            by = lax.rsqrt(power + EPS)
            stats[at, :] = jnp.where(lane == 0, mean, by)
            value = total[at, :] + before[at, :]
            value = by * (value - mean * sums[0, 0:1, :]) + sums[1, 0:1, :]
            total[at, :] = value
            target = noisy[at, :].astype(F32) - mine[at, :].astype(F32)
            wrong = (value - target) * scalars[1]
            sent = (by * wrong).astype(BF16).astype(F32)
            turned[:, at] = jnp.transpose(sent).astype(BF16)
            tail[0] += jnp.sum((mean * sent).reshape(piece // 8, 8, cols), axis=0)
            tail[1] += jnp.sum(wrong.reshape(piece // 8, 8, cols), axis=0)

        outs = [extra(turned, flipped), extra(total, velocity)]
        ends = [jnp.sum(jnp.transpose(tail[i]), axis=1, keepdims=True) for i in range(2)]
        edge[...] = jnp.concatenate(ends, axis=1)
        for j in range(fars):
            nears[j].wait()
            place = where[core_at + 1 + j]
            mods = [mod[place]] if parts == 1 else [mod[2 * place], mod[2 * place + 1]]
            for half, term in enumerate(gradient_halves(turned, far.at[j], mods, edge)):
                blocks[2 * j + half][...] = term.astype(BF16)
    for copy in outs + ([] if last else drains):
        copy.wait()


def project(where, scalars, sums, mod, sample, other, scaled, hops, prior, earlier, core_at, last):
    clip_rows, cols = sample.shape
    width = scaled.shape[0]
    group = 1 if cols % 128 else 2
    depth = group * cols
    slots = len(hops) * 2 // group
    pieces = [piece for hop, _ in hops for piece, _, _ in hop]
    plan = [[(low, side, place) for _, low, side in hop] for hop, place in hops]
    laid = (clip_rows, width) if group == 2 else (width // cols, clip_rows, cols)
    near = (clip_rows, depth) if group == 2 else (2, clip_rows, cols)
    fars = where.shape[0] - core_at - 1
    out_shape = [
        jax.ShapeDtypeStruct((clip_rows, cols), F32),
        jax.ShapeDtypeStruct(laid, BF16),
        jax.ShapeDtypeStruct((clip_rows, 128), F32),
    ]
    out_specs = [ANY, ANY, VMEM]
    scratch = [
        pltpu.VMEM((slots, clip_rows, depth), BF16),
        pltpu.VMEM((len(hops), 2 * cols, cols), BF16),
        pltpu.VMEM((clip_rows, 128), F32),
        pltpu.VMEM((clip_rows, cols), F32),
        pltpu.SemaphoreType.DMA((len(pieces),)),
        pltpu.SemaphoreType.DMA((len(hops),)),
        pltpu.SemaphoreType.DMA((len(hops),)),
        pltpu.SemaphoreType.DMA((5 + fars,)),
    ]
    if prior:
        velocity, inputs, stats = earlier
        earlier = [stats, velocity, inputs]
        scratch.append(pltpu.VMEM((clip_rows, cols), F32))
    if last:
        out_shape.append(jax.ShapeDtypeStruct((cols, clip_rows), BF16))
        out_shape.append(jax.ShapeDtypeStruct((cols, 2), F32))
        out_shape += [jax.ShapeDtypeStruct((cols, cols), BF16)] * (2 * fars)
        out_specs += [ANY, VMEM] + [VMEM] * (2 * fars)
        scratch += [
            pltpu.VMEM((2, 8, cols), F32),
            pltpu.VMEM((clip_rows, cols), BF16),
            pltpu.VMEM((clip_rows, cols), BF16),
            pltpu.VMEM((cols, clip_rows), BF16),
            pltpu.VMEM((fars, *near), BF16),
        ]
    return pl.pallas_call(
        functools.partial(project_kernel, prior, last, plan, core_at),
        out_shape=out_shape,
        in_specs=[SMEM, SMEM, VMEM, VMEM] + [ANY] * (3 + len(pieces)) + ([VMEM, ANY, ANY] if prior else []),
        out_specs=out_specs,
        scratch_shapes=scratch,
        input_output_aliases={7 + len(pieces) + 2: 1} if prior else {},
        compiler_params=pltpu.CompilerParams(vmem_limit_bytes=60 * MIB),
        cost_estimate=pl.CostEstimate(flops=1, bytes_accessed=1, transcendentals=0),
        name="project",
    )(where, scalars, sums, mod, sample, other, scaled, *pieces, *earlier)


def outer_kernel(picks, mod, edge, flipped, inputs, *outs):
    del picks
    mods = [mod[i] for i in range(mod.shape[0])]
    for half, term in enumerate(gradient_halves(flipped, inputs, mods, edge)):
        for i, out in enumerate(outs[half::2]):

            @pl.when(pl.program_id(0) == i)
            def _():
                out[...] = term.astype(out.dtype)


def outer(picks, mod, edge, flipped, inputs, dtypes):
    cols, rows = flipped.shape
    count = len(picks)
    group = 2 if len(inputs.shape) == 2 else 1

    def spot(i, picks):
        return (picks[i], 0, 0)

    if group == 2:
        tokens = pl.BlockSpec((rows, 2 * cols), lambda i, picks: (0, picks[i]))
    else:
        tokens = pl.BlockSpec((2, rows, cols), spot)
    return pl.pallas_call(
        outer_kernel,
        out_shape=[jax.ShapeDtypeStruct((cols, cols), dtype) for dtype in dtypes],
        grid_spec=pltpu.PrefetchScalarGridSpec(
            num_scalar_prefetch=1,
            grid=(count,),
            in_specs=[
                pl.BlockSpec((2 // group, 2, group * cols), spot),
                pl.BlockSpec((cols, 2), lambda i, picks: (0, 0)),
                pl.BlockSpec((cols, rows), lambda i, picks: (0, 0)),
                tokens,
            ],
            out_specs=[pl.BlockSpec((cols, cols), lambda i, picks: (0, 0))] * (2 * count),
        ),
        compiler_params=pltpu.CompilerParams(vmem_limit_bytes=60 * MIB),
        cost_estimate=pl.CostEstimate(
            flops=4 * rows * cols * cols * count,
            bytes_accessed=4 * rows * cols * (count + 1) + 4 * cols * cols * count,
            transcendentals=0,
        ),
        name="outer",
    )(jnp.stack(picks).astype(jnp.int32), mod, edge, flipped, inputs)


def finish_kernel(terms, *refs):
    *parts, out = refs
    for half in range(2):
        total = parts[half * terms][...]
        for ref in parts[half * terms + 1 : (half + 1) * terms]:
            total += ref[...].astype(F32)
        out[half] = jnp.transpose(total)


def finish(halves):
    cols = halves[0][0].shape[0]
    lanes = 128 if cols % 128 == 0 else cols
    parts = [part for half in halves for part in half]
    return pl.pallas_call(
        functools.partial(finish_kernel, len(halves[0])),
        grid=(cols // lanes,),
        out_shape=jax.ShapeDtypeStruct((2, cols, cols), F32),
        in_specs=[pl.BlockSpec((cols, lanes), lambda i: (0, i))] * len(parts),
        out_specs=pl.BlockSpec((2, lanes, cols), lambda i: (0, i, 0)),
        compiler_params=pltpu.CompilerParams(vmem_limit_bytes=cols * cols * 16 + 8 * MIB),
        name="finish",
    )(*parts).reshape(2 * cols, cols)


def per_device(
    sample, noise, gen_branch, step, teacher_mod, fake_mod, teacher_weight, fake_weight, gen_gate
):
    clips = lax.axis_size("clip")
    shards = lax.axis_size("fsdp")
    clip = lax.axis_index("clip")
    shard = lax.axis_index("fsdp")
    clip_rows, cols = sample.shape
    width = cols * shards
    total_tokens = clip_rows * clips
    hops = shards // 2
    group = 1 if cols % 128 else 2
    rows = clip_rows // CHUNKS
    orders = clip_orders(clips)

    frac = step.astype(F32)[0] / 1000.0
    sigma = 5.0 * frac / (1.0 + 4.0 * frac)
    noised = ((1.0 - sigma) * sample.astype(F32) + sigma * noise.astype(F32)).astype(BF16)

    order = list(range(0, hops, 2)) + list(range(hops - 1 - hops % 2, 0, -2))
    ring = [
        (2 * order[i] + core, 2 * order[(i + 1) % hops] + core)
        for i in range(hops)
        for core in range(2)
    ]
    line = shard // 2
    rank = jnp.where(line % 2 == 0, line // 2, hops - 1 - line // 2)
    places = []
    for hop in range(hops):
        at = (rank + hops - hop) % hops
        places.append(jnp.where(2 * at < hops, 2 * at, 2 * (hops - 1 - at) + 1))
    swap = [(i, i ^ 1) for i in range(shards)]
    half_rows = fake_weight.shape[0] // 2
    far = [key for key in ((m, h) for m in range(clips) for h in range(2)) if key[0] & (key[0] - 1)]
    seen = {}

    def gated(name, value):
        names = [other for other in GATES.get(name, ()) if other in seen]
        return after(value, *(seen[other] for other in names))

    def hop_to(hop, i):
        name = "AB"[i] + str(hop)
        source = seen["AB"[i] + str(hop - 1)] if hop > 1 else noised[i * rows : (i + 1) * rows]
        seen[name] = lax.ppermute(gated(name, source), "fsdp", ring)

    def cross(hop, i):
        name = "AB"[i] + str(hop)
        seen["c" + name] = lax.ppermute(gated("c" + name, seen[name]), "fsdp", swap)

    fake_direct = neighbour_blocks(fake_weight, clips)
    for i, block in enumerate(fake_direct.values()):
        seen["f" + str(i)] = block
    for i in range(CHUNKS):
        hop_to(1, i)
    seen["own"] = lax.ppermute(noised, "fsdp", swap)
    for i in range(CHUNKS):
        cross(1, i)
    for i in range(CHUNKS):
        hop_to(2, i)
    parts = relay_parts({bit: gated("relay", block) for bit, block in fake_direct.items()}, half_rows)
    seen["parts"] = list(parts.values())[0]
    seen["parts1"] = list(parts.values())[-1]
    fake_blocks = relay_blocks(parts, clips)
    for mask, block in fake_direct.items():
        fake_blocks[mask, 0] = fake_blocks[mask, 1] = block
    seen["far0"], seen["far1"] = fake_blocks[far[0]], fake_blocks[far[1]]
    scalars = jnp.stack([sigma, jnp.float32(1.0 / math.sqrt(total_tokens))])
    owners = jnp.stack([clip ^ mask for mask in range(clips)]).astype(jnp.int32)
    where = jnp.stack(places + [shard % 2]).astype(jnp.int32)
    by_place = jnp.swapaxes(fake_mod[0].reshape(2, shards // group, group * cols), 0, 1)
    scaled, sums = scale(owners, fake_mod[0], fake_weight, fake_blocks)
    seen["sums"] = sums
    teacher_parts = {}
    own = gated("teacher", teacher_weight)
    own = [own[:half_rows], own[half_rows:]]
    for phase in range(len(orders[0][1])):
        for half, order in orders:
            block = swap_clip(gated("teacher" + str(min(phase, 1)), own[half]), order[phase], clips)
            teacher_parts[order[phase], half] = block
            seen["t" + str(phase) + str(half)] = block
    tokens = [([(noised, 0, 0), (seen["own"], 0, 1)], 0)]

    def add_hop(hop):
        pieces = []
        for i in range(CHUNKS):
            name = "AB"[i] + str(hop)
            pieces += [(seen[name], i * rows, 0), (seen["c" + name], i * rows, 1)]
        tokens.append((pieces, hop))

    add_hop(1)
    for hop in range(2, hops):
        for i in range(CHUNKS):
            if hop > 2:
                hop_to(hop, i)
            if hop < hops - 1:
                cross(hop, i)
        if hop < hops - 1:
            add_hop(hop)
    cut = max(1, hops - 2)
    done = project(
        where, scalars, sums, by_place, sample, noise, scaled, tokens[:cut], 0, (), hops, False
    )
    seen["soon"] = done[2]
    if cut < hops - 1:
        done = project(
            where, scalars, sums, by_place, sample, noise, scaled, tokens[cut:], 2 * cols * cut,
            done, hops, False,
        )
    seen["early"] = done[2]
    for key, block in teacher_parts.items():
        teacher_parts[key] = gated("teacher relay", block)
    teacher_blocks = relay_blocks(teacher_parts, clips)
    for i in range(CHUNKS):
        cross(hops - 1, i)
    add_hop(hops - 1)
    def going(mask):
        return [bool(mask & order[0]) for _, order in orders]

    ranks = [[m for m in range(clips) if sum(going(m)) == n] for n in (2, 1, 0)]
    where = jnp.concatenate([where, jnp.stack([clip ^ mask for mask in ranks[0]]).astype(jnp.int32)])
    fake_velocity, inputs, stats, flipped, edge, *blocks = project(
        where, scalars, sums, by_place, sample, noise, scaled, tokens[-1:], 2 * cols * (hops - 1),
        done, hops, True,
    )

    held = dict(zip([(mask, half) for mask in ranks[0] for half in range(2)], blocks))

    def terms(masks, left):
        dtypes = [BF16 if out else F32 for mask in masks for out in going(mask)]
        got = outer([clip ^ mask for mask in masks], by_place, edge, left, inputs, dtypes)
        held.update(zip([(mask, half) for mask in masks for half in range(2)], got))

    if ranks[1]:
        terms(ranks[1], after(flipped, *blocks))
    ready = list(held.values())
    halves, relayed = [], []
    sent = {key: swap_clip(held[key], orders[key[1]][1][0], clips) for key in held if going(key[0])[key[1]]}
    firsts = [sent[key] for key in sent if key[0] in ranks[0]]
    seconds = [sent[key] for key in sent if key[0] not in ranks[0]]
    terms(ranks[2], after(flipped, *firsts))
    for half, order in orders:
        mine = {mask: [block] for (mask, h), block in held.items() if h == half}
        for bit in order:
            for mask in [mask for mask in mine if mask & bit]:
                block = mine.pop(mask)
                if bit == order[0]:
                    got = sent[mask, half]
                else:
                    block = sum(part.astype(F32) for part in block).astype(BF16)
                    relayed.append(block)
                    got = swap_clip(block, bit, clips)
                mine[mask ^ bit].append(got)
        halves.append(mine[0])
    fake_grad = finish(halves)

    scaled, sums = scale(
        owners, teacher_mod[0], after(teacher_weight, *ready), teacher_blocks
    )
    left = after(inputs, *relayed)

    def add_place(p, total):
        tokens = lax.dynamic_index_in_dim(left, p, 0, keepdims=False)
        right = lax.dynamic_slice(scaled, (p * cols, 0), (cols, cols))
        return total + jnp.dot(tokens, right, preferred_element_type=F32)

    if group == 2:
        velocity = jnp.dot(left, scaled, preferred_element_type=F32)
    else:
        velocity = jnp.zeros((clip_rows, cols), F32)
        velocity = lax.fori_loop(0, width // cols, add_place, velocity)
    velocity = stats[:, 1:2] * (velocity - stats[:, 0:1] * sums[0, :1]) + sums[1, :1]
    apart = velocity - fake_velocity
    pulled = jnp.sum(apart * gen_branch.astype(F32), axis=0, keepdims=True)
    away = sample.astype(F32) - (noised.astype(F32) - sigma * velocity)
    away = after(jnp.sum(jnp.abs(away)).reshape(1, 1), *seconds)
    bit = 1
    while bit < shards:
        away = away + lax.ppermute(away, "fsdp", [(i, i ^ bit) for i in range(shards)])
        bit *= 2
    factor = sigma / (away / (clip_rows * width) + EPS)
    branch_cot = (gen_gate * factor * apart).astype(BF16)
    gate_grad = pulled * factor / math.sqrt(clip_rows)
    return (branch_cot, gate_grad, fake_grad)


def solution(mesh):
    placed = (
        P("clip", "fsdp"),
        P("clip", "fsdp"),
        P("clip", "fsdp"),
        P("clip"),
        P("clip", None, None),
        P("clip", None, None),
        P("clip", "fsdp"),
        P("clip", "fsdp"),
        P("clip", "fsdp"),
    )
    return jax.shard_map(
        per_device,
        mesh=mesh,
        in_specs=placed,
        out_specs=(P("clip", "fsdp"), P("clip", "fsdp"), P("clip", "fsdp")),
        check_vma=False,
    )
```

```python
import functools
import math

import jax
import jax.numpy as jnp
from jax import lax
from jax.experimental import pallas as pl
from jax.experimental.pallas import tpu as pltpu
from jax.sharding import PartitionSpec as P

EPS = 1e-06
BF16 = jnp.bfloat16
F32 = jnp.float32
MIB = 1024 * 1024
CHUNKS = 2
GATES = {
    "relay": ("own",),
    "teacher": ("parts", "parts1"),
    "B2": ("A2",),
    "cB2": ("far0", "far1"),
    "cA3": ("soon",),
    "teacher relay": ("cA2",),
    "cA2": ("sums",),
    "cB1": ("far0", "far1"),
    "B3": ("sums",),
    "cB3": ("early", "t10", "t11"),
    "A3": ("far0", "far1"),
}
ANY = pl.BlockSpec(memory_space=pl.ANY)
SMEM = pl.BlockSpec(memory_space=pltpu.SMEM)
VMEM = pl.BlockSpec(memory_space=pltpu.VMEM)


def after(value, *earlier):
    return lax.optimization_barrier((value, *earlier))[0]


def swap_clip(value, bit, count):
    return lax.ppermute(value, "clip", [(i, i ^ bit) for i in range(count)])


def clip_orders(count):
    bits = [1 << i for i in range(count.bit_length() - 1)]
    return ((0, bits), (1, bits[::-1]))


def neighbour_blocks(weight, count):
    return {bit: swap_clip(weight, bit, count) for bit in clip_orders(count)[0][1]}


def relay_parts(direct, rows):
    parts = {}
    for half in range(2):
        for bit, block in direct.items():
            parts[bit, half] = block[half * rows : (half + 1) * rows]
    return parts


def relay_blocks(parts, count):
    pieces = {}
    for half, order in clip_orders(count):
        held = {}
        for bit in order:
            for mask in list(held):
                held[mask ^ bit] = swap_clip(held[mask], bit, count)
            held[bit] = parts[bit, half]
        for mask, block in held.items():
            pieces[mask, half] = block
    return pieces


def scale_kernel(keys, where, mod, weight, *refs):
    blocks, refs = refs[: len(keys)], refs[len(keys) :]
    out, sums, full, column, sems, osems = refs
    half_rows = weight.shape[0] // 2
    cols = weight.shape[1]
    loads, drains = [], []
    for index, (mask, half) in enumerate([(0, 0), (0, 1)] + keys):
        ref = weight if mask == 0 else blocks[index - 2]
        source = ref.at[pl.ds(half * half_rows, half_rows)] if ref.shape[0] > half_rows else ref
        spot = pl.multiple_of((where[mask] * 2 + half) * half_rows, half_rows)
        at = pl.ds(spot, half_rows)
        loads.append((pltpu.make_async_copy(source, full.at[at], sems.at[index]), spot))
        drains.append(pltpu.make_async_copy(full.at[at], out.at[at], osems.at[index]))
        loads[-1][0].start()
    sums[...] = jnp.zeros_like(sums)
    tile = half_rows // 2
    for index, ((load, spot), drain) in enumerate(zip(loads, drains)):
        mask, half = ([(0, 0), (0, 1)] + keys)[index]
        column[...] = jnp.transpose(mod[where[mask] * 2 + half])
        load.wait()
        for low in range(0, half_rows, tile):
            at = pl.ds(pl.multiple_of(spot + low, tile), tile)
            value = full[at, :].astype(F32)
            shifted = value * column[low : low + tile, 0:1]
            scaled = (value * (1.0 + column[low : low + tile, 1:2])).astype(BF16)
            full[at, :] = scaled
            sums[0] += jnp.sum(scaled.astype(F32).reshape(tile // 8, 8, cols), axis=0)
            sums[1] += jnp.sum(shifted.reshape(tile // 8, 8, cols), axis=0)
        drain.start()
    for i in range(2):
        sums[i] = jnp.broadcast_to(jnp.sum(sums[i], axis=0, keepdims=True), (8, cols))
    for drain in drains:
        drain.wait()


def scale(where, mod, weight, blocks):
    cols = weight.shape[1]
    half_rows = weight.shape[0] // 2
    mod = jnp.swapaxes(mod.reshape(2, -1, half_rows), 0, 1)
    count = len(blocks) + 2
    width = half_rows * count
    return pl.pallas_call(
        functools.partial(scale_kernel, list(blocks)),
        out_shape=(
            jax.ShapeDtypeStruct((width, cols), BF16),
            jax.ShapeDtypeStruct((2, 8, cols), F32),
        ),
        in_specs=[SMEM, VMEM] + [ANY] * (1 + len(blocks)),
        out_specs=(ANY, VMEM),
        scratch_shapes=[
            pltpu.VMEM((width, cols), BF16),
            pltpu.VMEM((half_rows, 2), F32),
            pltpu.SemaphoreType.DMA((count,)),
            pltpu.SemaphoreType.DMA((count,)),
        ],
        compiler_params=pltpu.CompilerParams(vmem_limit_bytes=60 * MIB),
        cost_estimate=pl.CostEstimate(
            flops=2700 * width * cols, bytes_accessed=7 * width * cols, transcendentals=0
        ),
        name="scale",
    )(where, mod, weight, *blocks.values())


def gradient_halves(flipped, tokens, mod, edge):
    cols = flipped.shape[0]
    if len(tokens.shape) == 2:
        term = jnp.dot(flipped[...], tokens[...], preferred_element_type=F32)
        terms = [term[:, half * cols : (half + 1) * cols] for half in range(2)]
        mods = [mod[0][:, half * cols : (half + 1) * cols] for half in range(2)]
    else:
        terms = [jnp.dot(flipped[...], tokens[h], preferred_element_type=F32) for h in range(2)]
        mods = mod
    return [
        (term - edge[:, 0:1]) * (1.0 + part[1:2, :]) + edge[:, 1:2] * part[0:1, :]
        for term, part in zip(terms, mods)
    ]


def project_kernel(
    prior, last, hops, core_at, where, scalars, sums, mod, sample, other, scaled, *refs
):
    count = sum(len(hop) for hop in hops)
    pieces, refs = refs[:count], refs[count:]
    if prior:
        carried, carry, _, *refs = refs
    velocity, inputs, stats, *refs = refs
    if last:
        fars = where.shape[0] - core_at - 1
        flipped, edge, *refs = refs
        blocks, refs = refs[: 2 * fars], refs[2 * fars :]
    held, full, moments, total, sems, wsems, osems, esems, *refs = refs
    if prior:
        before, *refs = refs
    if last:
        tail, mine, noisy, turned, far = refs
    slots, rows, depth = held.shape
    cols = total.shape[1]
    width = scaled.shape[0]
    parts = 2 * cols // depth
    core = where[core_at]
    span = 2 * cols

    def at_place(place):
        if parts == 1:
            return inputs.at[:, pl.ds(pl.multiple_of(place * span, span), span)]
        return inputs.at[pl.ds(place * 2, 2)]

    loads, arrivals, drains = [], [], []
    index = 0
    for n, hop in enumerate(hops):
        copies = []
        for low, side, place in hop:
            owner = core if side == 0 else 1 - core
            ref = pieces[index]
            at = pl.ds(low, ref.shape[0])
            if parts == 1:
                lanes = pl.ds(pl.multiple_of(owner * cols, cols), cols)
                spot = held.at[n, at, lanes]
            else:
                spot = held.at[2 * n + owner, at]
            copies.append(pltpu.make_async_copy(ref, spot, sems.at[index]))
            index += 1
        arrivals.append(copies)
        place = where[hop[0][2]]
        low = pl.multiple_of(place * span, span)
        loads.append(pltpu.make_async_copy(scaled.at[pl.ds(low, span)], full.at[n], wsems.at[n]))
        here = held.at[n] if parts == 1 else held.at[pl.ds(2 * n, 2)]
        drains.append(pltpu.make_async_copy(here, at_place(place), osems.at[n]))
    for copies, load in zip(arrivals, loads):
        for copy in copies:
            copy.start()
        load.start()
    extras = []

    def extra(source, target):
        extras.append(pltpu.make_async_copy(source, target, esems.at[len(extras)]))
        extras[-1].start()
        return extras[-1]

    waits = []
    if prior:
        waits.append(extra(carry, before))
    if last:
        waits += [extra(sample, mine), extra(other, noisy)]
    piece = 256
    lane = lax.broadcasted_iota(jnp.int32, (piece, 128), 1)
    for n in range(len(hops)):
        for copy in arrivals[n]:
            copy.wait()
        drains[n].start()
        loads[n].wait()
        for part in range(parts):
            slot = n * parts + part
            term = jnp.dot(
                held[slot], full[n, pl.ds(part * depth, depth), :], preferred_element_type=F32
            )
            if slot:
                total[...] += term
            else:
                total[...] = term
            for low in range(0, rows, piece):
                at = pl.ds(low, piece)
                if slot == 0 and prior:
                    moments[at, :] = carried[at, :]
                elif slot == 0:
                    near = held[0, at, :128].astype(F32)
                    near = jnp.sum(near, axis=1, keepdims=True) * (1.0 / 128)
                    moments[at, :] = jnp.where(lane == 0, near, 0.0)
                spread = held[slot, at, :].astype(F32) - moments[at, 0:1]
                sum_ = jnp.sum(spread, axis=1, keepdims=True)
                power = jnp.sum(spread * spread, axis=1, keepdims=True)
                more = jnp.where(lane == 1, sum_, jnp.where(lane == 2, power, 0.0))
                moments[at, :] += more
    for copy in waits:
        copy.wait()
    if not last:
        stats[...] = moments[...]
        if prior:
            total[...] += before[...]
        outs = [extra(total, velocity)]
    else:
        for copy in drains:
            copy.wait()
        nears = [extra(at_place(where[core_at + 1 + j]), far.at[j]) for j in range(fars)]
        tail[...] = jnp.zeros_like(tail)

        @pl.loop(0, rows // piece)
        def _(step):
            low = pl.multiple_of(step * piece, piece)
            at = pl.ds(low, piece)
            away = moments[at, 1:2] * (1.0 / width)
            power = jnp.maximum(moments[at, 2:3] * (1.0 / width) - away * away, 0.0)
            mean = moments[at, 0:1] + away
            by = lax.rsqrt(power + EPS)
            stats[at, :] = jnp.where(lane == 0, mean, by)
            value = total[at, :] + before[at, :]
            value = by * (value - mean * sums[0, 0:1, :]) + sums[1, 0:1, :]
            total[at, :] = value
            target = noisy[at, :].astype(F32) - mine[at, :].astype(F32)
            wrong = (value - target) * scalars[1]
            sent = (by * wrong).astype(BF16).astype(F32)
            turned[:, at] = jnp.transpose(sent).astype(BF16)
            tail[0] += jnp.sum((mean * sent).reshape(piece // 8, 8, cols), axis=0)
            tail[1] += jnp.sum(wrong.reshape(piece // 8, 8, cols), axis=0)

        outs = [extra(turned, flipped), extra(total, velocity)]
        ends = [jnp.sum(jnp.transpose(tail[i]), axis=1, keepdims=True) for i in range(2)]
        edge[...] = jnp.concatenate(ends, axis=1)
        for j in range(fars):
            nears[j].wait()
            place = where[core_at + 1 + j]
            mods = [mod[place]] if parts == 1 else [mod[2 * place], mod[2 * place + 1]]
            for half, term in enumerate(gradient_halves(turned, far.at[j], mods, edge)):
                blocks[2 * j + half][...] = term.astype(BF16)
    for copy in outs + ([] if last else drains):
        copy.wait()


def project(where, scalars, sums, mod, sample, other, scaled, hops, prior, earlier, core_at, last):
    clip_rows, cols = sample.shape
    width = scaled.shape[0]
    group = 1 if cols % 128 else 2
    depth = group * cols
    slots = len(hops) * 2 // group
    pieces = [piece for hop, _ in hops for piece, _, _ in hop]
    plan = [[(low, side, place) for _, low, side in hop] for hop, place in hops]
    laid = (clip_rows, width) if group == 2 else (width // cols, clip_rows, cols)
    near = (clip_rows, depth) if group == 2 else (2, clip_rows, cols)
    fars = where.shape[0] - core_at - 1
    out_shape = [
        jax.ShapeDtypeStruct((clip_rows, cols), F32),
        jax.ShapeDtypeStruct(laid, BF16),
        jax.ShapeDtypeStruct((clip_rows, 128), F32),
    ]
    out_specs = [ANY, ANY, VMEM]
    scratch = [
        pltpu.VMEM((slots, clip_rows, depth), BF16),
        pltpu.VMEM((len(hops), 2 * cols, cols), BF16),
        pltpu.VMEM((clip_rows, 128), F32),
        pltpu.VMEM((clip_rows, cols), F32),
        pltpu.SemaphoreType.DMA((len(pieces),)),
        pltpu.SemaphoreType.DMA((len(hops),)),
        pltpu.SemaphoreType.DMA((len(hops),)),
        pltpu.SemaphoreType.DMA((5 + fars,)),
    ]
    if prior:
        velocity, inputs, stats = earlier
        earlier = [stats, velocity, inputs]
        scratch.append(pltpu.VMEM((clip_rows, cols), F32))
    if last:
        out_shape.append(jax.ShapeDtypeStruct((cols, clip_rows), BF16))
        out_shape.append(jax.ShapeDtypeStruct((cols, 2), F32))
        out_shape += [jax.ShapeDtypeStruct((cols, cols), BF16)] * (2 * fars)
        out_specs += [ANY, VMEM] + [VMEM] * (2 * fars)
        scratch += [
            pltpu.VMEM((2, 8, cols), F32),
            pltpu.VMEM((clip_rows, cols), BF16),
            pltpu.VMEM((clip_rows, cols), BF16),
            pltpu.VMEM((cols, clip_rows), BF16),
            pltpu.VMEM((fars, *near), BF16),
        ]
    return pl.pallas_call(
        functools.partial(project_kernel, prior, last, plan, core_at),
        out_shape=out_shape,
        in_specs=[SMEM, SMEM, VMEM, VMEM] + [ANY] * (3 + len(pieces)) + ([VMEM, ANY, ANY] if prior else []),
        out_specs=out_specs,
        scratch_shapes=scratch,
        input_output_aliases={7 + len(pieces) + 2: 1} if prior else {},
        compiler_params=pltpu.CompilerParams(vmem_limit_bytes=60 * MIB),
        cost_estimate=pl.CostEstimate(flops=1, bytes_accessed=1, transcendentals=0),
        name="project",
    )(where, scalars, sums, mod, sample, other, scaled, *pieces, *earlier)


def outer_kernel(picks, mod, edge, flipped, inputs, *outs):
    del picks
    mods = [mod[i] for i in range(mod.shape[0])]
    for half, term in enumerate(gradient_halves(flipped, inputs, mods, edge)):
        for i, out in enumerate(outs[half::2]):

            @pl.when(pl.program_id(0) == i)
            def _():
                out[...] = term.astype(out.dtype)


def outer(picks, mod, edge, flipped, inputs, dtypes):
    cols, rows = flipped.shape
    count = len(picks)
    group = 2 if len(inputs.shape) == 2 else 1

    def spot(i, picks):
        return (picks[i], 0, 0)

    if group == 2:
        tokens = pl.BlockSpec((rows, 2 * cols), lambda i, picks: (0, picks[i]))
    else:
        tokens = pl.BlockSpec((2, rows, cols), spot)
    return pl.pallas_call(
        outer_kernel,
        out_shape=[jax.ShapeDtypeStruct((cols, cols), dtype) for dtype in dtypes],
        grid_spec=pltpu.PrefetchScalarGridSpec(
            num_scalar_prefetch=1,
            grid=(count,),
            in_specs=[
                pl.BlockSpec((2 // group, 2, group * cols), spot),
                pl.BlockSpec((cols, 2), lambda i, picks: (0, 0)),
                pl.BlockSpec((cols, rows), lambda i, picks: (0, 0)),
                tokens,
            ],
            out_specs=[pl.BlockSpec((cols, cols), lambda i, picks: (0, 0))] * (2 * count),
        ),
        compiler_params=pltpu.CompilerParams(vmem_limit_bytes=60 * MIB),
        cost_estimate=pl.CostEstimate(
            flops=4 * rows * cols * cols * count,
            bytes_accessed=4 * rows * cols * (count + 1) + 4 * cols * cols * count,
            transcendentals=0,
        ),
        name="outer",
    )(jnp.stack(picks).astype(jnp.int32), mod, edge, flipped, inputs)


def finish_kernel(terms, *refs):
    *parts, out = refs
    for half in range(2):
        total = parts[half * terms][...]
        for ref in parts[half * terms + 1 : (half + 1) * terms]:
            total += ref[...].astype(F32)
        out[half] = jnp.transpose(total)


def finish(halves):
    cols = halves[0][0].shape[0]
    lanes = 128 if cols % 128 == 0 else cols
    parts = [part for half in halves for part in half]
    return pl.pallas_call(
        functools.partial(finish_kernel, len(halves[0])),
        grid=(cols // lanes,),
        out_shape=jax.ShapeDtypeStruct((2, cols, cols), F32),
        in_specs=[pl.BlockSpec((cols, lanes), lambda i: (0, i))] * len(parts),
        out_specs=pl.BlockSpec((2, lanes, cols), lambda i: (0, i, 0)),
        compiler_params=pltpu.CompilerParams(vmem_limit_bytes=cols * cols * 16 + 8 * MIB),
        name="finish",
    )(*parts).reshape(2 * cols, cols)


def per_device(
    sample, noise, gen_branch, step, teacher_mod, fake_mod, teacher_weight, fake_weight, gen_gate
):
    clips = lax.axis_size("clip")
    shards = lax.axis_size("fsdp")
    clip = lax.axis_index("clip")
    shard = lax.axis_index("fsdp")
    clip_rows, cols = sample.shape
    width = cols * shards
    total_tokens = clip_rows * clips
    hops = shards // 2
    group = 1 if cols % 128 else 2
    rows = clip_rows // CHUNKS
    orders = clip_orders(clips)

    frac = step.astype(F32)[0] / 1000.0
    sigma = 5.0 * frac / (1.0 + 4.0 * frac)
    noised = ((1.0 - sigma) * sample.astype(F32) + sigma * noise.astype(F32)).astype(BF16)

    order = list(range(0, hops, 2)) + list(range(hops - 1 - hops % 2, 0, -2))
    ring = [
        (2 * order[i] + core, 2 * order[(i + 1) % hops] + core)
        for i in range(hops)
        for core in range(2)
    ]
    line = shard // 2
    rank = jnp.where(line % 2 == 0, line // 2, hops - 1 - line // 2)
    places = []
    for hop in range(hops):
        at = (rank + hops - hop) % hops
        places.append(jnp.where(2 * at < hops, 2 * at, 2 * (hops - 1 - at) + 1))
    swap = [(i, i ^ 1) for i in range(shards)]
    half_rows = fake_weight.shape[0] // 2
    far = [key for key in ((m, h) for m in range(clips) for h in range(2)) if key[0] & (key[0] - 1)]
    seen = {}

    def gated(name, value):
        names = [other for other in GATES.get(name, ()) if other in seen]
        return after(value, *(seen[other] for other in names))

    def hop_to(hop, i):
        name = "AB"[i] + str(hop)
        source = seen["AB"[i] + str(hop - 1)] if hop > 1 else noised[i * rows : (i + 1) * rows]
        seen[name] = lax.ppermute(gated(name, source), "fsdp", ring)

    def cross(hop, i):
        name = "AB"[i] + str(hop)
        seen["c" + name] = lax.ppermute(gated("c" + name, seen[name]), "fsdp", swap)

    fake_direct = neighbour_blocks(fake_weight, clips)
    for i, block in enumerate(fake_direct.values()):
        seen["f" + str(i)] = block
    for i in range(CHUNKS):
        hop_to(1, i)
    seen["own"] = lax.ppermute(noised, "fsdp", swap)
    for i in range(CHUNKS):
        cross(1, i)
    for i in range(CHUNKS):
        hop_to(2, i)
    parts = relay_parts({bit: gated("relay", block) for bit, block in fake_direct.items()}, half_rows)
    seen["parts"] = list(parts.values())[0]
    seen["parts1"] = list(parts.values())[-1]
    fake_blocks = relay_blocks(parts, clips)
    for mask, block in fake_direct.items():
        fake_blocks[mask, 0] = fake_blocks[mask, 1] = block
    seen["far0"], seen["far1"] = fake_blocks[far[0]], fake_blocks[far[1]]
    scalars = jnp.stack([sigma, jnp.float32(1.0 / math.sqrt(total_tokens))])
    owners = jnp.stack([clip ^ mask for mask in range(clips)]).astype(jnp.int32)
    where = jnp.stack(places + [shard % 2]).astype(jnp.int32)
    by_place = jnp.swapaxes(fake_mod[0].reshape(2, shards // group, group * cols), 0, 1)
    scaled, sums = scale(owners, fake_mod[0], fake_weight, fake_blocks)
    seen["sums"] = sums
    teacher_parts = {}
    own = gated("teacher", teacher_weight)
    own = [own[:half_rows], own[half_rows:]]
    for phase in range(len(orders[0][1])):
        for half, order in orders:
            block = swap_clip(gated("teacher" + str(min(phase, 1)), own[half]), order[phase], clips)
            teacher_parts[order[phase], half] = block
            seen["t" + str(phase) + str(half)] = block
    tokens = [([(noised, 0, 0), (seen["own"], 0, 1)], 0)]

    def add_hop(hop):
        pieces = []
        for i in range(CHUNKS):
            name = "AB"[i] + str(hop)
            pieces += [(seen[name], i * rows, 0), (seen["c" + name], i * rows, 1)]
        tokens.append((pieces, hop))

    add_hop(1)
    for hop in range(2, hops):
        for i in range(CHUNKS):
            if hop > 2:
                hop_to(hop, i)
            if hop < hops - 1:
                cross(hop, i)
        if hop < hops - 1:
            add_hop(hop)
    cut = max(1, hops - 2)
    done = project(
        where, scalars, sums, by_place, sample, noise, scaled, tokens[:cut], 0, (), hops, False
    )
    seen["soon"] = done[2]
    if cut < hops - 1:
        done = project(
            where, scalars, sums, by_place, sample, noise, scaled, tokens[cut:], 2 * cols * cut,
            done, hops, False,
        )
    seen["early"] = done[2]
    for key, block in teacher_parts.items():
        teacher_parts[key] = gated("teacher relay", block)
    teacher_blocks = relay_blocks(teacher_parts, clips)
    for i in range(CHUNKS):
        cross(hops - 1, i)
    add_hop(hops - 1)
    def going(mask):
        return [bool(mask & order[0]) for _, order in orders]

    ranks = [[m for m in range(clips) if sum(going(m)) == n] for n in (2, 1, 0)]
    where = jnp.concatenate([where, jnp.stack([clip ^ mask for mask in ranks[0]]).astype(jnp.int32)])
    fake_velocity, inputs, stats, flipped, edge, *blocks = project(
        where, scalars, sums, by_place, sample, noise, scaled, tokens[-1:], 2 * cols * (hops - 1),
        done, hops, True,
    )

    held = dict(zip([(mask, half) for mask in ranks[0] for half in range(2)], blocks))

    def terms(masks, left):
        dtypes = [BF16 if out else F32 for mask in masks for out in going(mask)]
        got = outer([clip ^ mask for mask in masks], by_place, edge, left, inputs, dtypes)
        held.update(zip([(mask, half) for mask in masks for half in range(2)], got))

    if ranks[1]:
        terms(ranks[1], after(flipped, *blocks))
    ready = list(held.values())
    halves, relayed = [], []
    sent = {key: swap_clip(held[key], orders[key[1]][1][0], clips) for key in held if going(key[0])[key[1]]}
    firsts = [sent[key] for key in sent if key[0] in ranks[0]]
    seconds = [sent[key] for key in sent if key[0] not in ranks[0]]
    terms(ranks[2], after(flipped, *firsts))
    for half, order in orders:
        mine = {mask: [block] for (mask, h), block in held.items() if h == half}
        for bit in order:
            for mask in [mask for mask in mine if mask & bit]:
                block = mine.pop(mask)
                if bit == order[0]:
                    got = sent[mask, half]
                else:
                    block = sum(part.astype(F32) for part in block).astype(BF16)
                    relayed.append(block)
                    got = swap_clip(block, bit, clips)
                mine[mask ^ bit].append(got)
        halves.append(mine[0])
    fake_grad = finish(halves)

    scaled, sums = scale(
        owners, teacher_mod[0], after(teacher_weight, *ready), teacher_blocks
    )
    left = after(inputs, *relayed)

    def add_place(p, total):
        tokens = lax.dynamic_index_in_dim(left, p, 0, keepdims=False)
        right = lax.dynamic_slice(scaled, (p * cols, 0), (cols, cols))
        return total + jnp.dot(tokens, right, preferred_element_type=F32)

    if group == 2:
        velocity = jnp.dot(left, scaled, preferred_element_type=F32)
    else:
        velocity = jnp.zeros((clip_rows, cols), F32)
        velocity = lax.fori_loop(0, width // cols, add_place, velocity)
    velocity = stats[:, 1:2] * (velocity - stats[:, 0:1] * sums[0, :1]) + sums[1, :1]
    apart = velocity - fake_velocity
    pulled = jnp.sum(apart * gen_branch.astype(F32), axis=0, keepdims=True)
    away = sample.astype(F32) - (noised.astype(F32) - sigma * velocity)
    away = after(jnp.sum(jnp.abs(away)).reshape(1, 1), *seconds)
    bit = 1
    while bit < shards:
        away = away + lax.ppermute(away, "fsdp", [(i, i ^ bit) for i in range(shards)])
        bit *= 2
    factor = sigma / (away / (clip_rows * width) + EPS)
    branch_cot = (gen_gate * factor * apart).astype(BF16)
    gate_grad = pulled * factor / math.sqrt(clip_rows)
    return (branch_cot, gate_grad, fake_grad)


def solution(mesh):
    placed = (
        P("clip", "fsdp"),
        P("clip", "fsdp"),
        P("clip", "fsdp"),
        P("clip"),
        P("clip", None, None),
        P("clip", None, None),
        P("clip", "fsdp"),
        P("clip", "fsdp"),
        P("clip", "fsdp"),
    )
    return jax.shard_map(
        per_device,
        mesh=mesh,
        in_specs=placed,
        out_specs=(P("clip", "fsdp"), P("clip", "fsdp"), P("clip", "fsdp")),
        check_vma=False,
    )
```
